256 devices in a mesh: ctx: 16 (over y, x_lo, core), tp: 16 (over x_hi, z).
Axes of the slice: x: 4 (x_hi: 2, x_lo: 2; x = x_hi * 2 + x_lo), y: 4, z: 8, core: 2. Of those that a mesh axis runs over, the one named last changes fastest.
Arguments:
- inputs: bfloat16 [2048, 4096], P('ctx', 'tp'), may hold values from -6 to 6
- w_in: bfloat16 [4096, 3, 4096], P(None, None, 'tp'), may hold values from -0.125 to 0.125
- conv_taps: float32 [3, 3, 4096], P(None, None, 'tp'), may hold values from -3 to 3
- pole_rates: float32 [4096, 16], P('tp'), may hold values from 4.8828125e-05 to 0.0333333333
- residues: float32 [4096, 16], P('tp'), may hold values from -2.5 to 2.5
- cotangent: bfloat16 [2048, 4096], P('ctx', 'tp'), may hold values from -6 to 6
Outputs:
- grad_inputs: bfloat16 [2048, 4096], P('ctx', 'tp')
The draws below stay inside these ranges and needn't reach their ends.
All inputs are finite; a program needn't handle non-finite values.
Results may differ from the reference program's by a relative error of at most 0.024.
Values may be sent and summed in bfloat16 or wider, within the bound.
A program may use at most 128 MiB of HBM per device.

```python
import math
import jax
import jax.numpy as jnp
from jax import lax

D = 4096
POLES = 16
TOKENS = 2048
N_TP = 16


def draw_pole_rates(key, part):
    key = jax.random.fold_in(key, 11)
    pick_key, slow_key, fast_key = jax.random.split(key, 3)
    slow_share = 0.5
    slow_log = jax.random.uniform(slow_key, (D, POLES), jnp.float32, math.log(0.1), math.log(2.0)) - math.log(TOKENS)
    fast_log = jax.random.uniform(fast_key, (D, POLES), jnp.float32, math.log(2.0 / TOKENS), math.log(1.0 / 30.0))
    chosen = jax.random.uniform(pick_key, (D, POLES), jnp.float32) < slow_share
    return jnp.exp(jnp.where(chosen, slow_log, fast_log)).astype(jnp.float32)


def strengthened(result, stream_key, source, target, blocks, factor):
    def block_of(position):
        return (jnp.arange(result.shape[position]) // (result.shape[position] // blocks)).reshape((-1,) + (1,) * (result.ndim - 1 - position))

    one_side = jax.random.permutation(stream_key, blocks)[block_of(target)]
    other_side = (block_of(target) + blocks // 2) % blocks
    return jnp.where((block_of(source) == one_side) | (block_of(source) == other_side), factor * result, result)


def levels(key, shape, cuts, low, top_value):
    gain = 1.0
    for dim, parts in cuts:
        draws = jax.random.uniform(jax.random.fold_in(jax.random.fold_in(key, 6), dim), (parts,), jnp.float32, low / len(cuts), top_value / len(cuts))
        gain = gain * jnp.repeat(jnp.exp(draws), shape[dim] // parts).reshape((-1,) + (1,) * (len(shape) - 1 - dim))
    return gain


def gaussian(stream_key, shape, scale, reach, shards=(), kind=jnp.bfloat16):
    values = scale * jax.random.normal(stream_key, shape, jnp.float32)
    if shards:
        values = values * levels(stream_key, shape, shards, -0.22, 0.18)
    return jnp.clip(values, -reach, reach).astype(kind)


def bell_draw_with(own_key, dims, scale, limit, pieces, heavy, dtype=jnp.bfloat16):
    drawn = scale * jax.random.normal(own_key, dims, jnp.float32)
    if pieces:
        drawn = drawn * levels(own_key, dims, pieces, -0.22, 0.18)
    return jnp.clip(strengthened(drawn, jax.random.fold_in(own_key, 3), *heavy), -limit, limit).astype(dtype)


def setup_inputs(seed: int = 0) -> dict:
    key_list = jax.random.split(jax.random.key(seed), 7)
    inputs = gaussian(key_list[0], (TOKENS, D), 1.0, 6.0, ((0, 16), (1, 16)))
    w_in = bell_draw_with(key_list[1], (D, 3, D), D ** -0.5, 0.125, ((2, 16),), (2, 0, 16, 2.0))
    conv_taps = gaussian(key_list[2], (3, 3, D), 0.6, 3.0, ((2, 16),), jnp.float32)
    pole_rates = draw_pole_rates(jax.random.fold_in(key_list[6], 71), 0)
    residues = gaussian(key_list[4], (D, POLES), 0.35, 2.5, ((0, 16),), jnp.float32)
    cotangent = gaussian(key_list[5], (TOKENS, D), 1.0, 6.0, ((0, 16), (1, 16)))
    return {"inputs": inputs, "w_in": w_in, "conv_taps": conv_taps, "pole_rates": pole_rates, "residues": residues, "cotangent": cotangent}


def reference(inputs, w_in, conv_taps, pole_rates, residues, cotangent):
    seq_len = inputs.shape[0]
    width = inputs.shape[1]
    projected = jnp.dot(inputs, w_in.reshape(width, 3 * width), preferred_element_type=jnp.float32)
    projected = projected.astype(jnp.bfloat16).reshape(seq_len, 3, width).astype(jnp.float32)
    padded = jnp.concatenate([jnp.zeros((2, 3, width), jnp.float32), projected], axis=0)
    filtered = conv_taps[0] * padded[2:] + conv_taps[1] * padded[1:seq_len + 1] + conv_taps[2] * padded[0:seq_len]
    gate = filtered[:, 0]
    key_part = filtered[:, 1]
    value_part = filtered[:, 2]
    mixing = key_part * value_part
    decay = jnp.exp(-pole_rates)
    in_gain = jnp.sqrt(-jnp.expm1(-2.0 * pole_rates))

    def step_forward(carried, row):
        carried = decay * carried + in_gain * row[:, None]
        return (carried, lax.optimization_barrier(jnp.sum(residues * carried, axis=1)))
    start_state = jnp.zeros(pole_rates.shape, jnp.float32)
    _, long_out = lax.scan(step_forward, start_state, mixing)
    grads_out = cotangent.astype(jnp.float32)
    grad_long = grads_out * gate
    grad_gate = grads_out * long_out
    out_weight = residues * in_gain

    def step_backward(carried, row):
        carried = decay * carried + row[:, None]
        return (carried, lax.optimization_barrier(jnp.sum(out_weight * carried, axis=1)))
    _, grad_mixing = lax.scan(step_backward, start_state, grad_long, reverse=True)
    grad_filtered = jnp.stack([grad_gate, grad_mixing * value_part, grad_mixing * key_part], axis=1)
    padded_grad = jnp.concatenate([grad_filtered, jnp.zeros((2, 3, width), jnp.float32)], axis=0)
    grad_projected = (conv_taps[0] * padded_grad[0:seq_len] + conv_taps[1] * padded_grad[1:seq_len + 1] + conv_taps[2] * padded_grad[2:seq_len + 2]).astype(jnp.bfloat16)
    groups = N_TP
    channels = width // groups
    grads_grouped = grad_projected.reshape(seq_len, 3, groups, channels).transpose(2, 0, 1, 3).reshape(groups, seq_len, 3 * channels)
    weights_grouped = w_in.reshape(width, 3, groups, channels).transpose(2, 0, 1, 3).reshape(groups, width, 3 * channels)

    def add_group(running, paired):
        term = lax.dot_general(paired[0], paired[1], (((1,), (1,)), ((), ())), preferred_element_type=jnp.float32)
        rounded = lax.optimization_barrier(term.astype(jnp.bfloat16))
        return (running + rounded.astype(jnp.float32), None)
    summed, _ = lax.scan(add_group, jnp.zeros((seq_len, width), jnp.float32), (grads_grouped, weights_grouped))
    return summed.astype(jnp.bfloat16)
```

```python
import functools

import jax
import jax.numpy as jnp
from jax import lax
from jax.experimental import pallas as pl
from jax.experimental.pallas import tpu as pltpu
from jax.sharding import PartitionSpec as P

MESH = pl.DeviceIdType.MESH
F32 = jnp.float32
BF16 = jnp.bfloat16
SUB = 8
LANES = 128
COLUMNS = 2


def one_minus_exp(x):
    series = jnp.ones_like(x)
    for k in range(9, 1, -1):
        series = 1.0 - x * series * (1.0 / k)
    return jnp.where(x < 0.25, x * series, 1.0 - jnp.exp(-x))


def kernel(
    n_ctx,
    n_tp,
    x_hbm,
    w_hbm,
    taps_hbm,
    rate_hbm,
    res_hbm,
    cot_hbm,
    out_hbm,
    w,
    xg,
    taps,
    rate,
    res,
    cot,
    proj,
    gate,
    keyp,
    valp,
    mixp,
    glp,
    fwd_pow,
    rev_pow,
    kern,
    spread,
    gain,
    w_fwd,
    w_bwd,
    part,
    state,
    state_in,
    rim,
    gfp,
    sliding,
    long_out,
    grad_mix,
    gp,
    rs_out,
    rs_in,
    x_out,
    x_in,
    result,
    local_sem,
    w_sem,
    g_send,
    g_recv,
    s_send,
    s_recv,
    rim_send,
    rim_recv,
    r_send,
    r_recv,
):
    rows, chans = x_hbm.shape
    poles = rate_hbm.shape[0]
    ring = n_tp // COLUMNS
    far, near = (ring - 1 + 1) // 2, (ring - 1) // 2
    streams = ((0, 1, far), (0, -1, near), (1, 1, near), (1, -1, far))
    ctx = lax.axis_index("ctx")
    tp = lax.axis_index("tp")
    col, z = tp // ring, tp % ring

    def at_z(column, zz):
        return column * ring + (zz + 2 * ring) % ring

    partner = at_z(1 - col, z)
    neighbour = {1: at_z(col, z + 1), -1: at_z(col, z - 1)}
    next_ctx = lax.rem(ctx + 1, n_ctx)
    prev_ctx = lax.rem(ctx + n_ctx - 1, n_ctx)

    barrier = pltpu.get_barrier_semaphore()
    for other in (neighbour[1], neighbour[-1], partner):
        pl.semaphore_signal(barrier, inc=1, device_id=(ctx, other), device_id_type=MESH)

    def greet(o, _):
        pl.semaphore_signal(barrier, inc=1, device_id=(lax.rem(ctx + o, n_ctx), tp), device_id_type=MESH)
        return 0

    lax.fori_loop(1, n_ctx, greet, 0)

    w_copies = [pltpu.make_async_copy(w_hbm.at[j], w.at[j], w_sem.at[j]) for j in range(3)]
    small = [
        pltpu.make_async_copy(src, dst, local_sem.at[i])
        for i, (src, dst) in enumerate(
            ((x_hbm, xg.at[tp]), (taps_hbm, taps), (rate_hbm, rate), (res_hbm, res), (cot_hbm, cot))
        )
    ]
    for c in small + w_copies:
        c.start()
    pl.semaphore_wait(barrier, 3 + n_ctx - 1)

    def remote(src, dst, send, recv, device):
        return pltpu.make_async_remote_copy(
            src_ref=src, dst_ref=dst, send_sem=send, recv_sem=recv, device_id=device, device_id_type=MESH
        )

    def g_copy(k, s, slot, src=None):
        here = xg.at[slot]
        return remote(here if src is None else src, here, g_send.at[k, s], g_recv.at[k, s], (ctx, neighbour[streams[k][1]]))

    def x_pair(slot, src):
        return remote(src, xg.at[slot], g_send.at[4, 0], g_recv.at[4, 0], (ctx, partner))

    x_pair(tp, x_hbm).start()
    g_copy(0, 1, tp, x_hbm).start()
    g_copy(1, 1, tp, x_hbm).start()

    for c in small[1:]:
        c.wait()

    rates = rate[...]
    gain[...] = jnp.sqrt(one_minus_exp(2.0 * rates))
    kern[...] = jnp.zeros_like(kern)
    steps = lax.broadcasted_iota(jnp.int32, (rows, chans), 0).astype(F32)
    state_in[ctx] = jnp.zeros(state_in.shape[1:], BF16)

    def tables(n, _):
        r = rate[pl.ds(n, 1), :]
        up = jnp.exp(-r * steps)
        fwd_pow[n] = up
        rev_pow[n] = jnp.exp(-r * (rows - 1.0 - steps))
        kern[...] += up * (res[pl.ds(n, 1), :] * gain[pl.ds(n, 1), :])
        return 0

    def state_weights(i, _):
        gap = (jnp.abs(ctx - i) - 1) * rows
        weight = jnp.exp(-rate[...] * gap.astype(F32))
        w_fwd[i] = jnp.where(i < ctx, weight, 0.0)
        w_bwd[i] = jnp.where(i > ctx, weight, 0.0)
        return 0

    def project(slot):
        block = xg[slot]
        start = pl.multiple_of(slot * chans, chans)

        def branch(j, _):
            proj[j, SUB:, :] += jnp.dot(block, w[j, pl.ds(start, chans), :], preferred_element_type=F32)
            return 0

        lax.fori_loop(0, 3, branch, 0)

    proj[...] = jnp.zeros_like(proj)
    small[0].wait()
    for c in w_copies:
        c.wait()
    project(tp)
    x_pair(partner, xg.at[partner]).wait_recv()
    g_copy(2, 1, partner).start()
    g_copy(3, 1, partner).start()
    project(partner)
    per_step = -(-poles // far)
    ctx_per_step = -(-n_ctx // far)

    def gather_step(s, _):
        for k, (c, d, hops) in enumerate(streams):
            slot = at_z(col if c == 0 else 1 - col, z - s * d)

            @pl.when(s <= hops)
            def _(k=k, slot=slot, hops=hops):
                g_copy(k, s, slot).wait_recv()

                @pl.when(s < hops)
                def _():
                    g_copy(k, s + 1, slot).start()

                project(slot)

        lax.fori_loop((s - 1) * per_step, jnp.minimum(s * per_step, poles), tables, 0)
        lax.fori_loop((s - 1) * ctx_per_step, jnp.minimum(s * ctx_per_step, n_ctx), state_weights, 0)
        return 0

    lax.fori_loop(1, far + 1, gather_step, 0)

    def spread_rows(i, _):
        block = kern[pl.ds(pl.multiple_of(SUB * i, SUB), SUB), :]
        for r in range(SUB):
            spread[SUB * i + r] = jnp.broadcast_to(block[r : r + 1, :], (SUB, chans))
        return 0

    lax.fori_loop(0, rows // SUB, spread_rows, 0)

    for j in range(3):
        proj[j, SUB:, :] = proj[j, SUB:, :].astype(BF16).astype(F32)
    rim1 = remote(proj.at[:, pl.ds(rows, SUB), :], rim.at[0], rim_send.at[0], rim_recv.at[0], (next_ctx, tp))
    rim1.start()

    def filter_rows(lo, n):
        out = []
        for j in range(3):
            acc = taps[0, j : j + 1, :] * proj[j, SUB + lo : SUB + lo + n, :]
            acc += taps[1, j : j + 1, :] * proj[j, SUB + lo - 1 : SUB + lo + n - 1, :]
            acc += taps[2, j : j + 1, :] * proj[j, SUB + lo - 2 : SUB + lo + n - 2, :]
            out.append(acc)
        gate[lo : lo + n, :] = out[0]
        keyp[lo : lo + n, :] = out[1]
        valp[lo : lo + n, :] = out[2]
        mixp[SUB + lo : SUB + lo + n, :] = out[1] * out[2]
        glp[lo : lo + n, :] = cot[...].astype(F32)[lo : lo + n] * out[0]

    mixp[0:SUB, :] = jnp.zeros((SUB, chans), F32)
    glp[rows : rows + SUB, :] = jnp.zeros((SUB, chans), F32)
    filter_rows(SUB, rows - SUB)

    def partial_states(n, _):
        fwd = rev_pow[n, SUB:, :] * mixp[2 * SUB :, :]
        bwd = fwd_pow[n, SUB:, :] * glp[SUB:rows, :]
        part[0, n] = jnp.sum(fwd.reshape(rows // SUB - 1, SUB, chans), axis=0)
        part[1, n] = jnp.sum(bwd.reshape(rows // SUB - 1, SUB, chans), axis=0)
        return 0

    lax.fori_loop(0, poles, partial_states, 0)
    rim1.wait()
    proj[:, 0:SUB, :] = jnp.where(ctx > 0, rim[0], 0.0)
    filter_rows(0, SUB)

    def last_states(n, _):
        part[0, n] += rev_pow[n, 0:SUB, :] * mixp[SUB : 2 * SUB, :]
        part[1, n] += fwd_pow[n, 0:SUB, :] * glp[0:SUB, :]
        return 0

    lax.fori_loop(0, poles, last_states, 0)
    state[0] = (gain[...] * jnp.sum(part[0], axis=1)).astype(BF16)
    state[1] = jnp.sum(part[1], axis=1).astype(BF16)

    def s_copy(o):
        other = lax.rem(ctx + o, n_ctx)
        which = (other < ctx).astype(jnp.int32)
        return remote(state.at[which], state_in.at[ctx], s_send.at[o], s_recv.at[o], (other, tp))

    def send_state(o, _):
        s_copy(o).start()
        return 0

    lax.fori_loop(1, n_ctx, send_state, 0)

    tiles = rows // SUB

    def local_conv(which, flip, store):
        for lane in range(0, chans, LANES):
            cols = slice(lane, lane + LANES)

            def tap(r, acc, cols=cols):
                acc = list(acc)
                block = [sliding[which, r, SUB * i : SUB * i + SUB, cols] for i in range(tiles)]
                for m in range(tiles):
                    k = spread[SUB * m + r, :, cols]
                    for i in range(tiles - m):
                        if flip:
                            acc[i + m] = acc[i + m] + k * block[i]
                        else:
                            acc[i] = acc[i] + k * block[i + m]
                return tuple(acc)

            acc = lax.fori_loop(0, SUB, tap, (jnp.zeros((SUB, LANES), F32),) * tiles)
            for i in range(tiles):
                store[SUB * i : SUB * i + SUB, cols] = acc[i]

    for r in range(SUB):
        sliding[0, r] = mixp[SUB - r : SUB - r + rows, :]
        sliding[1, r] = glp[r : r + rows, :]
    local_conv(0, True, long_out)
    local_conv(1, False, grad_mix)

    def wait_state(o, _):
        s_copy(o).wait()
        return 0

    lax.fori_loop(1, n_ctx, wait_state, 0)

    def add_state(i, carried):
        got = state_in[i].astype(F32)
        return carried[0] + w_fwd[i] * got, carried[1] + w_bwd[i] * got

    none = jnp.zeros((poles, chans), F32)
    before, after = lax.fori_loop(0, n_ctx, add_state, (none, none))
    decayed = res[...] * jnp.exp(-rates)
    part[0, :, 0, :] = decayed * before
    part[1, :, 0, :] = decayed * gain[...] * after

    def finish_rows(lo, n):
        def add_fwd(p, acc):
            return acc + fwd_pow[p, lo : lo + n, :] * part[0, p, 0:1, :]

        def add_bwd(p, acc):
            return acc + rev_pow[p, lo : lo + n, :] * part[1, p, 0:1, :]

        whole = lax.fori_loop(0, poles, add_fwd, long_out[lo : lo + n, :])
        gfp[0, lo : lo + n, :] = cot[...].astype(F32)[lo : lo + n] * whole
        whole = lax.fori_loop(0, poles, add_bwd, grad_mix[lo : lo + n, :])
        gfp[1, lo : lo + n, :] = whole * valp[lo : lo + n, :]
        gfp[2, lo : lo + n, :] = whole * keyp[lo : lo + n, :]

    finish_rows(0, SUB)
    rim2 = remote(gfp.at[:, pl.ds(0, SUB), :], rim.at[1], rim_send.at[1], rim_recv.at[1], (prev_ctx, tp))
    rim2.start()
    finish_rows(SUB, rows - SUB)
    rim2.wait()
    gfp[:, rows : rows + SUB, :] = jnp.where(ctx < n_ctx - 1, rim[1], 0.0)
    for j in range(3):
        acc = taps[0, j : j + 1, :] * gfp[j, 0:rows, :]
        acc += taps[1, j : j + 1, :] * gfp[j, 1 : rows + 1, :]
        acc += taps[2, j : j + 1, :] * gfp[j, 2 : rows + 2, :]
        gp[j] = acc.astype(BF16)

    def partial_of(slot):
        start = pl.multiple_of(slot * chans, chans)

        def branch(j, acc):
            return acc + lax.dot_general(
                gp[j], w[j, pl.ds(start, chans), :], (((1,), (1,)), ((), ())), preferred_element_type=F32
            )

        return lax.fori_loop(0, 3, branch, jnp.zeros((rows, chans), F32))

    def r_copy(k, s):
        return remote(rs_out.at[k, s], rs_in.at[k, s], r_send.at[k, s], r_recv.at[k, s], (ctx, neighbour[streams[k][1]]))

    order = (3, 2, 0, 1)

    def reduce_step(s, _):
        for k in order:
            c, d, hops = streams[k]
            slot = at_z(col if c == 0 else 1 - col, z + (hops - s) * d)

            @pl.when(s < hops)
            def _(k=k, slot=slot):
                rs_out[k, s] = partial_of(slot).astype(BF16)

                @pl.when(s > 0)
                def _():
                    r_copy(k, s - 1).wait_recv()
                    rs_out[k, s] = (rs_out[k, s].astype(F32) + rs_in[k, s - 1].astype(F32)).astype(BF16)

                r_copy(k, s).start()

        return 0

    lax.fori_loop(0, far, reduce_step, 0)
    long_out[...] = partial_of(partner)
    for k in (2, 3):
        r_copy(k, streams[k][2] - 1).wait_recv()
        long_out[...] += rs_in[k, streams[k][2] - 1].astype(F32)
    x_out[...] = long_out[...].astype(BF16)
    swap = remote(x_out, x_in, r_send.at[4, 0], r_recv.at[4, 0], (ctx, partner))
    swap.start()
    long_out[...] = partial_of(tp)
    for k in (0, 1):
        r_copy(k, streams[k][2] - 1).wait_recv()
        long_out[...] += rs_in[k, streams[k][2] - 1].astype(F32)
    swap.wait_recv()
    result[...] = (long_out[...] + x_in[...].astype(F32)).astype(BF16)
    done = pltpu.make_async_copy(result, out_hbm, local_sem.at[0])
    done.start()

    swap.wait_send()
    x_pair(tp, x_hbm).wait_send()
    for k, (c, d, hops) in enumerate(streams):

        def left(s, _, k=k):
            g_copy(k, s, tp).wait_send()
            r_copy(k, s - 1).wait_send()
            return 0

        lax.fori_loop(1, hops + 1, left, 0)
    done.wait()


def body(n_ctx, n_tp, inputs, w_in, conv_taps, pole_rates, residues, cotangent):
    rows, chans = inputs.shape
    width = w_in.shape[0]
    poles = pole_rates.shape[1]
    far = n_tp // COLUMNS // 2
    vmem = pltpu.VMEM
    dma = pltpu.SemaphoreType.DMA
    scratch = [
        vmem((3, width, chans), BF16),
        vmem((n_tp, rows, chans), BF16),
        vmem((3, 3, chans), F32),
        vmem((poles, chans), F32),
        vmem((poles, chans), F32),
        vmem((rows, chans), BF16),
        vmem((3, rows + SUB, chans), F32),
        vmem((rows, chans), F32),
        vmem((rows, chans), F32),
        vmem((rows, chans), F32),
        vmem((rows + SUB, chans), F32),
        vmem((rows + SUB, chans), F32),
        vmem((poles, rows, chans), F32),
        vmem((poles, rows, chans), F32),
        vmem((rows, chans), F32),
        vmem((rows, SUB, chans), F32),
        vmem((poles, chans), F32),
        vmem((n_ctx, poles, chans), F32),
        vmem((n_ctx, poles, chans), F32),
        vmem((2, poles, SUB, chans), F32),
        vmem((2, poles, chans), BF16),
        vmem((n_ctx, poles, chans), BF16),
        vmem((2, 3, SUB, chans), F32),
        vmem((3, rows + SUB, chans), F32),
        vmem((2, SUB, rows, chans), F32),
        vmem((rows, chans), F32),
        vmem((rows, chans), F32),
        vmem((3, rows, chans), BF16),
        vmem((4, far, rows, chans), BF16),
        vmem((4, far, rows, chans), BF16),
        vmem((rows, chans), BF16),
        vmem((rows, chans), BF16),
        vmem((rows, chans), BF16),
        dma((5,)),
        dma((3,)),
        dma((5, far + 1)),
        dma((5, far + 1)),
        dma((n_ctx,)),
        dma((n_ctx,)),
        dma((2,)),
        dma((2,)),
        dma((5, far)),
        dma((5, far)),
    ]
    return pl.pallas_call(
        functools.partial(kernel, n_ctx, n_tp),
        out_shape=jax.ShapeDtypeStruct((rows, chans), BF16),
        in_specs=[pl.BlockSpec(memory_space=pl.ANY)] * 6,
        out_specs=pl.BlockSpec(memory_space=pl.ANY),
        scratch_shapes=scratch,
        compiler_params=pltpu.CompilerParams(
            collective_id=0, has_side_effects=True, vmem_limit_bytes=60 * 1024 * 1024
        ),
        cost_estimate=pl.CostEstimate(
            flops=4 * rows * width * 3 * chans, bytes_accessed=2 * 3 * width * chans, transcendentals=0
        ),
        name="hyena_input_grad",
    )(inputs, w_in.transpose(1, 0, 2), conv_taps, pole_rates.T, residues.T, cotangent)


def solution(mesh):
    in_specs = (
        P("ctx", "tp"),
        P(None, None, "tp"),
        P(None, None, "tp"),
        P("tp", None),
        P("tp", None),
        P("ctx", "tp"),
    )
    out_specs = P("ctx", "tp")
    step = functools.partial(body, mesh.shape["ctx"], mesh.shape["tp"])
    return jax.shard_map(step, mesh=mesh, in_specs=in_specs, out_specs=out_specs, check_vma=False)
```

```python
import functools

import jax
import jax.numpy as jnp
from jax import lax
from jax.experimental import pallas as pl
from jax.experimental.pallas import tpu as pltpu
from jax.sharding import PartitionSpec as P

MESH = pl.DeviceIdType.MESH
F32 = jnp.float32
BF16 = jnp.bfloat16
SUB = 8
LANES = 128
PIECES = 2
COLUMNS = 2


def one_minus_exp(x):
    series = jnp.ones_like(x)
    for k in range(9, 1, -1):
        series = 1.0 - x * series * (1.0 / k)
    return jnp.where(x < 0.25, x * series, 1.0 - jnp.exp(-x))


def kernel(
    n_ctx,
    n_tp,
    x_hbm,
    w_hbm,
    taps_hbm,
    rate_hbm,
    res_hbm,
    cot_hbm,
    out_hbm,
    w,
    xg,
    taps,
    rate,
    res,
    cot,
    proj,
    gate,
    keyp,
    valp,
    mixp,
    glp,
    fwd_pow,
    rev_pow,
    kern,
    kern_late,
    spread,
    gain,
    w_fwd,
    w_bwd,
    part,
    ends,
    state,
    state_in,
    gfp,
    sliding,
    long_out,
    grad_mix,
    gp,
    ready,
    rs_out,
    rs_in,
    x_out,
    x_in,
    result,
    local_sem,
    w_sem,
    g_send,
    g_recv,
    s_send,
    s_recv,
    r_send,
    r_recv,
):
    rows, chans = x_hbm.shape
    poles = rate_hbm.shape[0]
    ring = n_tp // COLUMNS
    far, near = (ring - 1 + 1) // 2, (ring - 1) // 2
    streams = ((0, 1, far), (0, -1, near), (1, 1, near), (1, -1, far))
    ctx = lax.axis_index("ctx")
    tp = lax.axis_index("tp")
    col, z = tp // ring, tp % ring

    def at_z(column, zz):
        return column * ring + (zz + 2 * ring) % ring

    partner = at_z(1 - col, z)
    neighbour = {1: at_z(col, z + 1), -1: at_z(col, z - 1)}
    diagonal = {1: at_z(1 - col, z + 1), -1: at_z(1 - col, z - 1)}

    barrier = pltpu.get_barrier_semaphore()
    for other in (neighbour[1], neighbour[-1], diagonal[1], diagonal[-1], partner):
        pl.semaphore_signal(barrier, inc=1, device_id=(ctx, other), device_id_type=MESH)

    def greet(o, _):
        pl.semaphore_signal(barrier, inc=1, device_id=(lax.rem(ctx + o, n_ctx), tp), device_id_type=MESH)
        return 0

    lax.fori_loop(1, n_ctx, greet, 0)

    w_copies = [pltpu.make_async_copy(w_hbm.at[j], w.at[j], w_sem.at[j]) for j in range(3)]
    small = [
        pltpu.make_async_copy(src, dst, local_sem.at[i])
        for i, (src, dst) in enumerate(
            ((x_hbm, xg.at[tp]), (taps_hbm, taps), (rate_hbm, rate), (res_hbm, res), (cot_hbm, cot))
        )
    ]
    for c in small + w_copies:
        c.start()
    pl.semaphore_wait(barrier, 5 + n_ctx - 1)

    def remote(src, dst, send, recv, device):
        return pltpu.make_async_remote_copy(
            src_ref=src, dst_ref=dst, send_sem=send, recv_sem=recv, device_id=device, device_id_type=MESH
        )

    size = rows // PIECES

    def piece(p):
        return pl.ds(p * size, size)

    def g_copy(k, s, p, slot, src=None):
        c, d, _ = streams[k]
        here = xg.at[slot, piece(p)]
        there = neighbour[d] if src is None or c == 0 else diagonal[d]
        src = here if src is None else src.at[piece(p)]
        return remote(src, here, g_send.at[k, s, p], g_recv.at[k, s, p], (ctx, there))

    def x_pair(slot):
        return remote(x_hbm, xg.at[slot], g_send.at[4, 0, 0], g_recv.at[4, 0, 0], (ctx, partner))

    for p in range(PIECES):
        for k in range(4):
            g_copy(k, 1, p, tp, x_hbm).start()
    x_pair(tp).start()

    for c in small[1:]:
        c.wait()

    rates = rate[...]
    gain[...] = jnp.sqrt(one_minus_exp(2.0 * rates))
    kern[...] = jnp.zeros_like(kern)
    steps = lax.broadcasted_iota(jnp.int32, (rows, chans), 0).astype(F32)
    state_in[ctx, 0:poles] = jnp.zeros((poles, chans), BF16)

    def tables(n, _):
        r = rate[pl.ds(n, 1), :]
        up = jnp.exp(-r * steps)
        fwd_pow[n] = up
        rev_pow[n] = jnp.exp(-r * (rows - 1.0 - steps))
        kern[...] += up * (res[pl.ds(n, 1), :] * gain[pl.ds(n, 1), :])
        return 0

    def state_weights(i, _):
        gap = (jnp.abs(ctx - i) - 1) * rows
        weight = jnp.exp(-rate[...] * gap.astype(F32))
        w_fwd[i] = jnp.where(i < ctx, weight, 0.0)
        w_bwd[i] = jnp.where(i > ctx, weight, 0.0)
        return 0

    def project(slot):
        block = xg[slot]
        start = pl.multiple_of(slot * chans, chans)

        def branch(j, _):
            proj[j, SUB:, :] += jnp.dot(block, w[j, pl.ds(start, chans), :], preferred_element_type=F32)
            return 0

        lax.fori_loop(0, 3, branch, 0)

    proj[...] = jnp.zeros_like(proj)
    small[0].wait()
    for c in w_copies:
        c.wait()
    project(tp)
    per_step = -(-poles // far)
    ctx_per_step = -(-n_ctx // far)

    def gather_step(s, _):
        slots = [at_z(col if c == 0 else 1 - col, z - s * d) for c, d, _ in streams]
        for p in range(PIECES):
            for k, (_, _, hops) in enumerate(streams):

                @pl.when(s <= hops)
                def _(k=k, p=p, hops=hops):
                    g_copy(k, s, p, slots[k]).wait_recv()

                    @pl.when(s < hops)
                    def _():
                        g_copy(k, s + 1, p, slots[k]).start()

        for k, (_, _, hops) in enumerate(streams):

            @pl.when(s <= hops)
            def _(k=k):
                project(slots[k])

        @pl.when(s == min(2, far))
        def _():
            x_pair(partner).wait_recv()
            project(partner)

        lax.fori_loop((s - 1) * per_step, jnp.minimum(s * per_step, poles), tables, 0)
        lax.fori_loop((s - 1) * ctx_per_step, jnp.minimum(s * ctx_per_step, n_ctx), state_weights, 0)
        return 0

    lax.fori_loop(1, far + 1, gather_step, 0)

    def spread_rows(i, _):
        block = kern[pl.ds(pl.multiple_of(SUB * i, SUB), SUB), :]
        for r in range(SUB):
            spread[SUB * i + r] = jnp.broadcast_to(block[r : r + 1, :], (SUB, chans))
        return 0

    lax.fori_loop(0, rows // SUB, spread_rows, 0)
    kern_late[0:1, :] = jnp.zeros((1, chans), F32)
    kern_late[1:rows, :] = kern[0 : rows - 1, :]

    for j in range(3):
        proj[j, SUB:, :] = proj[j, SUB:, :].astype(BF16).astype(F32)
    edge = [proj[j, SUB : SUB + 1, :] for j in range(3)] + [cot[0:16, :].astype(F32)[0:1]]
    edge += [proj[j, SUB + 1 : SUB + 2, :] for j in range(3)] + [cot[0:16, :].astype(F32)[1:2]]
    blank = jnp.zeros((1, chans), F32)
    edge += [proj[j, SUB + rows - 2 : SUB + rows - 1, :] for j in range(3)] + [blank]
    edge += [proj[j, SUB + rows - 1 : SUB + rows, :] for j in range(3)] + [blank]
    edge = jnp.concatenate(edge, axis=0).astype(BF16)
    for target in (state.at[0], state.at[1], state_in.at[ctx]):
        target[poles:, :] = edge

    filtered = []
    for j in range(3):
        acc = taps[0, j : j + 1, :] * proj[j, SUB : SUB + rows, :]
        acc += taps[1, j : j + 1, :] * proj[j, SUB - 1 : SUB + rows - 1, :]
        acc += taps[2, j : j + 1, :] * proj[j, SUB - 2 : SUB + rows - 2, :]
        filtered.append(acc)
    keyp[...] = filtered[1]
    valp[...] = filtered[2]
    mixp[0:SUB, :] = jnp.zeros((SUB, chans), F32)
    mixp[SUB:, :] = jnp.where(steps >= 2.0, filtered[1] * filtered[2], 0.0)
    glp[0:rows, :] = jnp.where(steps >= 2.0, cot[...].astype(F32) * filtered[0], 0.0)
    glp[rows : rows + SUB, :] = jnp.zeros((SUB, chans), F32)

    def partial_states(n, _):
        fwd = rev_pow[n] * mixp[SUB:, :]
        bwd = fwd_pow[n] * glp[0:rows, :]
        part[0, n] = jnp.sum(fwd.reshape(rows // SUB, SUB, chans), axis=0)
        part[1, n] = jnp.sum(bwd.reshape(rows // SUB, SUB, chans), axis=0)
        return 0

    lax.fori_loop(0, poles, partial_states, 0)
    ends[0] = gain[...] * jnp.sum(part[0], axis=1)
    ends[1] = jnp.sum(part[1], axis=1)
    state[0, 0:poles, :] = ends[0].astype(BF16)
    state[1, 0:poles, :] = ends[1].astype(BF16)

    def s_copy(o):
        other = lax.rem(ctx + o, n_ctx)
        which = (other < ctx).astype(jnp.int32)
        return remote(state.at[which], state_in.at[ctx], s_send.at[o], s_recv.at[o], (other, tp))

    def send_state(o, _):
        s_copy(o).start()
        return 0

    lax.fori_loop(1, n_ctx, send_state, 0)

    tiles = rows // SUB

    def local_conv(which, flip, store):
        for lane in range(0, chans, LANES):
            cols = slice(lane, lane + LANES)

            def tap(r, acc, cols=cols):
                acc = list(acc)
                block = [sliding[which, r, SUB * i : SUB * i + SUB, cols] for i in range(tiles)]
                for m in range(tiles):
                    k = spread[SUB * m + r, :, cols]
                    for i in range(tiles - m):
                        if flip:
                            acc[i + m] = acc[i + m] + k * block[i]
                        else:
                            acc[i] = acc[i] + k * block[i + m]
                return tuple(acc)

            acc = lax.fori_loop(0, SUB, tap, (jnp.zeros((SUB, LANES), F32),) * tiles)
            for i in range(tiles):
                store[SUB * i : SUB * i + SUB, cols] = acc[i]

    for r in range(SUB):
        sliding[0, r] = mixp[SUB - r : SUB - r + rows, :]
        sliding[1, r] = glp[r : r + rows, :]
    local_conv(0, True, long_out)
    local_conv(1, False, grad_mix)

    def wait_state(o, _):
        s_copy(o).wait()
        return 0

    lax.fori_loop(1, n_ctx, wait_state, 0)

    branch_row = lax.broadcasted_iota(jnp.int32, (SUB, chans), 0)
    upper = branch_row < 4
    tap_rows = [jnp.concatenate([taps[i], blank, taps[i], blank], axis=0) for i in range(3)]

    def first_rows(i):
        here = state_in[i, poles:, :].astype(F32)[0:SUB]
        before = state_in[jnp.maximum(i - 1, 0), poles:, :].astype(F32)[SUB:]
        before = jnp.where(i > 0, before, 0.0)
        shifted = jnp.where(upper, pltpu.roll(before, 4, 0), pltpu.roll(here, 4, 0))
        full = tap_rows[0] * here + tap_rows[1] * shifted + tap_rows[2] * before
        return [(here[r + 3 : r + 4], full[r : r + 1], full[r + 1 : r + 2], full[r + 2 : r + 3]) for r in (0, 4)]

    decay = jnp.exp(-rates)
    gained = [gain[...] * jnp.exp(-rates * (rows - 1.0)), gain[...] * jnp.exp(-rates * (rows - 2.0))]
    none = jnp.zeros((poles, chans), F32)

    def add_before(i, total):
        (_, _, k0, v0), (_, _, k1, v1) = first_rows(i)
        end = state_in[i, 0:poles, :].astype(F32) + gained[0] * (k0 * v0) + gained[1] * (k1 * v1)
        return total + w_fwd[i] * end

    def add_after(i, total):
        (c0, g0, _, _), (c1, g1, _, _) = first_rows(i)
        return total + w_bwd[i] * (state_in[i, 0:poles, :].astype(F32) + c0 * g0 + decay * (c1 * g1))

    before = lax.fori_loop(0, ctx, add_before, none)
    after = lax.fori_loop(ctx + 1, n_ctx, add_after, none)
    out_gain = res[...] * gain[...]
    part[0, :, 0, :] = res[...] * decay * before
    part[1, :, 0, :] = out_gain * decay * after

    (c0, g0, k0, v0), (c1, g1, k1, v1) = first_rows(ctx)
    keyp[0:1, :], valp[0:1, :], keyp[1:2, :], valp[1:2, :] = k0, v0, k1, v1
    mix0, mix1, gl0, gl1 = k0 * v0, k1 * v1, c0 * g0, c1 * g1
    taps0, taps1 = kern[0:1, :], kern[1:2, :]
    grad_mix[0:1, :] += taps0 * gl0 + taps1 * gl1
    grad_mix[1:2, :] += taps0 * gl1
    leaving = jnp.exp(-rates * float(rows)) * before + ends[0] + gained[0] * mix0 + gained[1] * mix1
    (c0, g0, k0, v0), (c1, g1, k1, v1) = first_rows(jnp.minimum(ctx + 1, n_ctx - 1))
    leaving = res[...] * decay * leaving
    out0 = jnp.sum(leaving, axis=0, keepdims=True) + taps0 * (k0 * v0)
    out1 = jnp.sum(leaving * decay, axis=0, keepdims=True) + taps1 * (k0 * v0) + taps0 * (k1 * v1)
    adj0 = jnp.sum(out_gain * after, axis=0, keepdims=True)
    adj1 = jnp.sum(out_gain * jnp.exp(rates) * (after - c0 * g0), axis=0, keepdims=True)
    for j, pair in enumerate(((c0 * out0, c1 * out1), (adj0 * v0, adj1 * v1), (adj0 * k0, adj1 * k1))):
        for r in range(2):
            gfp[j, rows + r : rows + r + 1, :] = jnp.where(ctx < n_ctx - 1, pair[r], 0.0)

    def add_fwd(p, acc):
        return acc + fwd_pow[p] * part[0, p, 0:1, :]

    def add_bwd(p, acc):
        return acc + rev_pow[p] * part[1, p, 0:1, :]

    whole = lax.fori_loop(0, poles, add_fwd, long_out[...] + kern[...] * mix0 + kern_late[...] * mix1)
    gfp[0, 0:rows, :] = cot[...].astype(F32) * whole
    whole = lax.fori_loop(0, poles, add_bwd, grad_mix[...])
    gfp[1, 0:rows, :] = whole * valp[...]
    gfp[2, 0:rows, :] = whole * keyp[...]
    for j in range(3):
        acc = taps[0, j : j + 1, :] * gfp[j, 0:rows, :]
        acc += taps[1, j : j + 1, :] * gfp[j, 1 : rows + 1, :]
        acc += taps[2, j : j + 1, :] * gfp[j, 2 : rows + 2, :]
        gp[j] = acc.astype(BF16)

    def partial_of(slot):
        start = pl.multiple_of(slot * chans, chans)

        def branch(j, acc):
            return acc + lax.dot_general(
                gp[j], w[j, pl.ds(start, chans), :], (((1,), (1,)), ((), ())), preferred_element_type=F32
            )

        return lax.fori_loop(0, 3, branch, jnp.zeros((rows, chans), F32))

    def r_copy(k, s, p):
        c, d, hops = streams[k]
        there = neighbour[d] if c == 0 else jnp.where(s == hops - 1, diagonal[d], neighbour[d])
        at = (k, s, piece(p))
        return remote(rs_out.at[at], rs_in.at[at], r_send.at[k, s, p], r_recv.at[k, s, p], (ctx, there))

    swap = remote(x_out, x_in, r_send.at[4, 0, 0], r_recv.at[4, 0, 0], (ctx, partner))

    def slot_of(k, s):
        c, d, hops = streams[k]
        return at_z(col if c == 0 else 1 - col, z + (hops - s) * d)

    for k in range(4):
        rs_out[k, 0] = partial_of(slot_of(k, 0)).astype(BF16)
        for p in range(PIECES):
            r_copy(k, 0, p).start()
    x_out[...] = partial_of(partner).astype(BF16)
    swap.start()

    def reduce_step(s, _):
        for k, (_, _, hops) in enumerate(streams):

            @pl.when(s < hops)
            def _(k=k):
                ready[k] = partial_of(slot_of(k, s))

        for p in range(PIECES):
            for k, (_, _, hops) in enumerate(streams):

                @pl.when(s < hops)
                def _(k=k, p=p):
                    at = piece(p)
                    r_copy(k, s - 1, p).wait_recv()
                    rs_out[k, s, at] = (ready[k, at] + rs_in[k, s - 1, at].astype(F32)).astype(BF16)
                    r_copy(k, s, p).start()

        return 0

    lax.fori_loop(1, far, reduce_step, 0)
    long_out[...] = partial_of(tp)
    swap.wait_recv()
    long_out[...] += x_in[...].astype(F32)
    for p in range(PIECES):
        at = piece(p)
        for k, (_, _, hops) in enumerate(streams):
            r_copy(k, hops - 1, p).wait_recv()
        total = long_out[at]
        for k, (_, _, hops) in enumerate(streams):
            total += rs_in[k, hops - 1, at].astype(F32)
        result[at] = total.astype(BF16)
    done = pltpu.make_async_copy(result, out_hbm, local_sem.at[0])
    done.start()

    swap.wait_send()
    x_pair(tp).wait_send()
    for k, (c, d, hops) in enumerate(streams):

        def left(s, _, k=k):
            for p in range(PIECES):
                g_copy(k, s, p, tp).wait_send()
                r_copy(k, s - 1, p).wait_send()
            return 0

        lax.fori_loop(1, hops + 1, left, 0)
    done.wait()


def body(n_ctx, n_tp, inputs, w_in, conv_taps, pole_rates, residues, cotangent):
    rows, chans = inputs.shape
    width = w_in.shape[0]
    poles = pole_rates.shape[1]
    far = n_tp // COLUMNS // 2
    vmem = pltpu.VMEM
    dma = pltpu.SemaphoreType.DMA
    scratch = [
        vmem((3, width, chans), BF16),
        vmem((n_tp, rows, chans), BF16),
        vmem((3, 3, chans), F32),
        vmem((poles, chans), F32),
        vmem((poles, chans), F32),
        vmem((rows, chans), BF16),
        vmem((3, rows + SUB, chans), F32),
        vmem((rows, chans), F32),
        vmem((rows, chans), F32),
        vmem((rows, chans), F32),
        vmem((rows + SUB, chans), F32),
        vmem((rows + SUB, chans), F32),
        vmem((poles, rows, chans), F32),
        vmem((poles, rows, chans), F32),
        vmem((rows, chans), F32),
        vmem((rows, chans), F32),
        vmem((rows, SUB, chans), F32),
        vmem((poles, chans), F32),
        vmem((n_ctx, poles, chans), F32),
        vmem((n_ctx, poles, chans), F32),
        vmem((2, poles, SUB, chans), F32),
        vmem((2, poles, chans), F32),
        vmem((2, poles + 2 * SUB, chans), BF16),
        vmem((n_ctx, poles + 2 * SUB, chans), BF16),
        vmem((3, rows + SUB, chans), F32),
        vmem((2, SUB, rows, chans), F32),
        vmem((rows, chans), F32),
        vmem((rows, chans), F32),
        vmem((3, rows, chans), BF16),
        vmem((4, rows, chans), F32),
        vmem((4, far, rows, chans), BF16),
        vmem((4, far, rows, chans), BF16),
        vmem((rows, chans), BF16),
        vmem((rows, chans), BF16),
        vmem((rows, chans), BF16),
        dma((5,)),
        dma((3,)),
        dma((5, far + 1, PIECES)),
        dma((5, far + 1, PIECES)),
        dma((n_ctx,)),
        dma((n_ctx,)),
        dma((5, far, PIECES)),
        dma((5, far, PIECES)),
    ]
    return pl.pallas_call(
        functools.partial(kernel, n_ctx, n_tp),
        out_shape=jax.ShapeDtypeStruct((rows, chans), BF16),
        in_specs=[pl.BlockSpec(memory_space=pl.ANY)] * 6,
        out_specs=pl.BlockSpec(memory_space=pl.ANY),
        scratch_shapes=scratch,
        compiler_params=pltpu.CompilerParams(
            collective_id=0, has_side_effects=True, vmem_limit_bytes=60 * 1024 * 1024
        ),
        cost_estimate=pl.CostEstimate(
            flops=4 * rows * width * 3 * chans, bytes_accessed=2 * 3 * width * chans, transcendentals=0
        ),
        name="hyena_input_grad",
    )(inputs, w_in.transpose(1, 0, 2), conv_taps, pole_rates.T, residues.T, cotangent)


def solution(mesh):
    in_specs = (
        P("ctx", "tp"),
        P(None, None, "tp"),
        P(None, None, "tp"),
        P("tp", None),
        P("tp", None),
        P("ctx", "tp"),
    )
    out_specs = P("ctx", "tp")
    step = functools.partial(body, mesh.shape["ctx"], mesh.shape["tp"])
    return jax.shard_map(step, mesh=mesh, in_specs=in_specs, out_specs=out_specs, check_vma=False)
```

```python
import functools

import jax
import jax.numpy as jnp
from jax import lax
from jax.experimental import pallas as pl
from jax.experimental.pallas import tpu as pltpu
from jax.sharding import PartitionSpec as P

MESH = pl.DeviceIdType.MESH
F32 = jnp.float32
BF16 = jnp.bfloat16
SUB = 8
LANES = 128
PIECES = 2
COLUMNS = 2


def one_minus_exp(x):
    series = jnp.ones_like(x)
    for k in range(9, 1, -1):
        series = 1.0 - x * series * (1.0 / k)
    return jnp.where(x < 0.25, x * series, 1.0 - jnp.exp(-x))


def kernel(
    n_ctx,
    n_tp,
    x_hbm,
    w_hbm,
    taps_hbm,
    rate_hbm,
    res_hbm,
    cot_hbm,
    out_hbm,
    w,
    xg,
    taps,
    rate,
    res,
    cot,
    proj,
    gate,
    keyp,
    valp,
    mixp,
    glp,
    fwd_pow,
    rev_pow,
    kern,
    kern_late,
    spread,
    gain,
    w_fwd,
    w_bwd,
    part,
    ends,
    state,
    state_in,
    gfp,
    sliding,
    long_out,
    grad_mix,
    gp,
    ready,
    rs_out,
    rs_in,
    x_out,
    x_in,
    result,
    local_sem,
    w_sem,
    g_send,
    g_recv,
    s_send,
    s_recv,
    met,
    r_send,
    r_recv,
):
    rows, chans = x_hbm.shape
    poles = rate_hbm.shape[0]
    ring = n_tp // COLUMNS
    hops = ring // 2 - 1
    streams = ((0, 1), (1, -1), (0, -1), (1, 1))
    ctx = lax.axis_index("ctx")
    tp = lax.axis_index("tp")
    col, z = tp // ring, tp % ring

    def at_z(column, zz):
        return column * ring + (zz + 2 * ring) % ring

    def column_of(c):
        return col if c == 0 else 1 - col

    partner = at_z(1 - col, z)

    rounds = n_ctx.bit_length() - 1

    def across(r):
        bit = (ctx // 2**r) % 2
        return ctx + 2**r * (1 - 2 * bit)

    barrier = pltpu.get_barrier_semaphore()
    others = [at_z(col, z + d) for d in (1, -1, 2, -2)]
    others += [at_z(1 - col, z + d) for d in ((1, -1) if hops > 1 else (1, -1, 2, -2))] + [partner]
    for other in others:
        pl.semaphore_signal(barrier, inc=1, device_id=(ctx, other), device_id_type=MESH)
    for r in range(rounds):
        pl.semaphore_signal(barrier, inc=1, device_id=(across(r), tp), device_id_type=MESH)

    def greet(r):
        if r < rounds:
            pl.semaphore_signal(met.at[r], inc=1, device_id=(across(r), tp), device_id_type=MESH)

    def greeted(r):
        if r < rounds:
            pl.semaphore_wait(met.at[r], 1)

    w_copies = [pltpu.make_async_copy(w_hbm.at[j], w.at[j], w_sem.at[j]) for j in range(3)]
    small = [
        pltpu.make_async_copy(src, dst, local_sem.at[i])
        for i, (src, dst) in enumerate(
            ((x_hbm, xg.at[tp]), (taps_hbm, taps), (rate_hbm, rate), (res_hbm, res), (cot_hbm, cot))
        )
    ]
    for c in small + w_copies:
        c.start()
    pl.semaphore_wait(barrier, len(others) + rounds)

    def remote(src, dst, send, recv, device):
        return pltpu.make_async_remote_copy(
            src_ref=src, dst_ref=dst, send_sem=send, recv_sem=recv, device_id=device, device_id_type=MESH
        )

    size = rows // PIECES

    def piece(p):
        return pl.ds(p * size, size)

    def halves(k):
        return (0, 1) if streams[k][1] > 0 else (1, 0)

    def g_copy(k, s, p):
        c, d = streams[k]
        skip = 2 if s > hops else 1
        held = z - (s - skip) * d
        own = s == skip
        slot = tp if own else at_z(column_of(c), held)
        there = at_z(1 - col if own and c == 1 else col, z + skip * d)
        src = x_hbm.at[piece(p)] if own else xg.at[slot, piece(p)]
        return remote(src, xg.at[slot, piece(p)], g_send.at[k, s, p], g_recv.at[k, s, p], (ctx, there))

    def arrived(k, s, p):
        here = xg.at[at_z(column_of(streams[k][0]), z - s * streams[k][1]), piece(p)]
        remote(here, here, g_send.at[k, s, p], g_recv.at[k, s, p], (ctx, partner)).wait_recv()

    x_pair = remote(x_hbm, xg.at[tp], g_send.at[4, 0, 0], g_recv.at[4, 0, 0], (ctx, partner))

    def forward(s, i):
        for k in range(4):
            p = halves(k)[i]
            if s > 0:
                arrived(k, s, p)
            if s == hops - 1 and i == 0:
                g_copy(k, hops + 1, p).start()
            if s < hops:
                g_copy(k, s + 1, p).start()

    for i in range(PIECES):
        forward(0, i)
    x_pair.start()
    greet(0)

    for c in small[1:]:
        c.wait()

    rates = rate[...]
    gain[...] = jnp.sqrt(one_minus_exp(2.0 * rates))
    kern[...] = jnp.zeros_like(kern)
    steps = lax.broadcasted_iota(jnp.int32, (rows, chans), 0).astype(F32)
    state_in[ctx, 0:poles] = jnp.zeros((poles, chans), BF16)

    def tables(n, _):
        r = rate[pl.ds(n, 1), :]
        up = jnp.exp(-r * steps)
        fwd_pow[n] = up
        rev_pow[n] = jnp.exp(-r * (rows - 1.0 - steps))
        kern[...] += up * (res[pl.ds(n, 1), :] * gain[pl.ds(n, 1), :])
        return 0

    def state_weights(i, _):
        gap = (jnp.abs(ctx - i) - 1) * rows
        weight = jnp.exp(-rate[...] * gap.astype(F32))
        w_fwd[i] = jnp.where(i < ctx, weight, 0.0)
        w_bwd[i] = jnp.where(i > ctx, weight, 0.0)
        return 0

    def project(slots):
        for j in range(3):
            total = proj[j, SUB:, :]
            for slot in slots:
                start = pl.multiple_of(slot * chans, chans)
                total += jnp.dot(xg[slot], w[j, pl.ds(start, chans), :], preferred_element_type=F32)
            proj[j, SUB:, :] = total

    proj[...] = jnp.zeros_like(proj)
    small[0].wait()
    for c in w_copies:
        c.wait()
    project([tp])
    per_step = -(-poles // hops)
    ctx_per_step = -(-n_ctx // hops)
    for s in range(1, hops + 1):
        for i in range(PIECES):
            forward(s, i)
        project([at_z(column_of(c), z - s * d) for c, d in streams])
        greeted(s - 1)
        greet(s)
        lax.fori_loop((s - 1) * per_step, min(s * per_step, poles), tables, 0)
        lax.fori_loop((s - 1) * ctx_per_step, min(s * ctx_per_step, n_ctx), state_weights, 0)
        if s == 1:
            x_pair.wait_recv()
            project([partner])
    for k in range(4):
        arrived(k, hops + 1, halves(k)[0])
    project([at_z(col, z + hops + 1), at_z(1 - col, z + hops + 1)])

    def spread_rows(i, _):
        block = kern[pl.ds(pl.multiple_of(SUB * i, SUB), SUB), :]
        for r in range(SUB):
            spread[SUB * i + r] = jnp.broadcast_to(block[r : r + 1, :], (SUB, chans))
        return 0

    lax.fori_loop(0, rows // SUB, spread_rows, 0)
    kern_late[0:1, :] = jnp.zeros((1, chans), F32)
    kern_late[1:rows, :] = kern[0 : rows - 1, :]

    for j in range(3):
        proj[j, SUB:, :] = proj[j, SUB:, :].astype(BF16).astype(F32)
    edge = [proj[j, SUB : SUB + 1, :] for j in range(3)] + [cot[0:16, :].astype(F32)[0:1]]
    edge += [proj[j, SUB + 1 : SUB + 2, :] for j in range(3)] + [cot[0:16, :].astype(F32)[1:2]]
    blank = jnp.zeros((1, chans), F32)
    edge += [proj[j, SUB + rows - 2 : SUB + rows - 1, :] for j in range(3)] + [blank]
    edge += [proj[j, SUB + rows - 1 : SUB + rows, :] for j in range(3)] + [blank]
    edge = jnp.concatenate(edge, axis=0).astype(BF16)
    for target in (state.at[0], state.at[1], state_in.at[ctx]):
        target[poles:, :] = edge

    filtered = []
    for j in range(3):
        acc = taps[0, j : j + 1, :] * proj[j, SUB : SUB + rows, :]
        acc += taps[1, j : j + 1, :] * proj[j, SUB - 1 : SUB + rows - 1, :]
        acc += taps[2, j : j + 1, :] * proj[j, SUB - 2 : SUB + rows - 2, :]
        filtered.append(acc)
    keyp[...] = filtered[1]
    valp[...] = filtered[2]
    mixp[0:SUB, :] = jnp.zeros((SUB, chans), F32)
    mixp[SUB:, :] = jnp.where(steps >= 2.0, filtered[1] * filtered[2], 0.0)
    glp[0:rows, :] = jnp.where(steps >= 2.0, cot[...].astype(F32) * filtered[0], 0.0)
    glp[rows : rows + SUB, :] = jnp.zeros((SUB, chans), F32)

    def partial_states(n, _):
        fwd = rev_pow[n] * mixp[SUB:, :]
        bwd = fwd_pow[n] * glp[0:rows, :]
        part[0, n] = jnp.sum(fwd.reshape(rows // SUB, SUB, chans), axis=0)
        part[1, n] = jnp.sum(bwd.reshape(rows // SUB, SUB, chans), axis=0)
        return 0

    lax.fori_loop(0, poles, partial_states, 0)
    ends[0] = gain[...] * jnp.sum(part[0], axis=1)
    ends[1] = jnp.sum(part[1], axis=1)
    state[0, 0:poles, :] = ends[0].astype(BF16)
    state[1, 0:poles, :] = ends[1].astype(BF16)

    greeted(hops)
    for r in range(hops + 1, rounds):
        greet(r)
        greeted(r)

    def s_copy(o):
        other = lax.rem(ctx + o, n_ctx)
        which = (other < ctx).astype(jnp.int32)
        return remote(state.at[which], state_in.at[ctx], s_send.at[o], s_recv.at[o], (other, tp))

    def send_state(o, _):
        s_copy(o).start()
        return 0

    lax.fori_loop(1, n_ctx, send_state, 0)

    tiles = rows // SUB

    def local_conv(which, flip, store):
        for lane in range(0, chans, LANES):
            cols = slice(lane, lane + LANES)

            def tap(r, acc, cols=cols):
                acc = list(acc)
                block = [sliding[which, r, SUB * i : SUB * i + SUB, cols] for i in range(tiles)]
                for m in range(tiles):
                    k = spread[SUB * m + r, :, cols]
                    for i in range(tiles - m):
                        if flip:
                            acc[i + m] = acc[i + m] + k * block[i]
                        else:
                            acc[i] = acc[i] + k * block[i + m]
                return tuple(acc)

            acc = lax.fori_loop(0, SUB, tap, (jnp.zeros((SUB, LANES), F32),) * tiles)
            for i in range(tiles):
                store[SUB * i : SUB * i + SUB, cols] = acc[i]

    for r in range(SUB):
        sliding[0, r] = mixp[SUB - r : SUB - r + rows, :]
        sliding[1, r] = glp[r : r + rows, :]
    local_conv(0, True, long_out)
    local_conv(1, False, grad_mix)

    def wait_state(o, _):
        s_copy(o).wait()
        return 0

    lax.fori_loop(1, n_ctx, wait_state, 0)

    branch_row = lax.broadcasted_iota(jnp.int32, (SUB, chans), 0)
    upper = branch_row < 4
    tap_rows = [jnp.concatenate([taps[i], blank, taps[i], blank], axis=0) for i in range(3)]

    def first_rows(i):
        here = state_in[i, poles:, :].astype(F32)[0:SUB]
        before = state_in[jnp.maximum(i - 1, 0), poles:, :].astype(F32)[SUB:]
        before = jnp.where(i > 0, before, 0.0)
        shifted = jnp.where(upper, pltpu.roll(before, 4, 0), pltpu.roll(here, 4, 0))
        full = tap_rows[0] * here + tap_rows[1] * shifted + tap_rows[2] * before
        return [(here[r + 3 : r + 4], full[r : r + 1], full[r + 1 : r + 2], full[r + 2 : r + 3]) for r in (0, 4)]

    decay = jnp.exp(-rates)
    gained = [gain[...] * jnp.exp(-rates * (rows - 1.0)), gain[...] * jnp.exp(-rates * (rows - 2.0))]
    none = jnp.zeros((poles, chans), F32)

    def add_before(i, total):
        (_, _, k0, v0), (_, _, k1, v1) = first_rows(i)
        end = state_in[i, 0:poles, :].astype(F32) + gained[0] * (k0 * v0) + gained[1] * (k1 * v1)
        return total + w_fwd[i] * end

    def add_after(i, total):
        (c0, g0, _, _), (c1, g1, _, _) = first_rows(i)
        return total + w_bwd[i] * (state_in[i, 0:poles, :].astype(F32) + c0 * g0 + decay * (c1 * g1))

    before = lax.fori_loop(0, ctx, add_before, none)
    after = lax.fori_loop(ctx + 1, n_ctx, add_after, none)
    out_gain = res[...] * gain[...]
    part[0, :, 0, :] = res[...] * decay * before
    part[1, :, 0, :] = out_gain * decay * after

    (c0, g0, k0, v0), (c1, g1, k1, v1) = first_rows(ctx)
    keyp[0:1, :], valp[0:1, :], keyp[1:2, :], valp[1:2, :] = k0, v0, k1, v1
    mix0, mix1, gl0, gl1 = k0 * v0, k1 * v1, c0 * g0, c1 * g1
    taps0, taps1 = kern[0:1, :], kern[1:2, :]
    grad_mix[0:1, :] += taps0 * gl0 + taps1 * gl1
    grad_mix[1:2, :] += taps0 * gl1
    leaving = jnp.exp(-rates * float(rows)) * before + ends[0] + gained[0] * mix0 + gained[1] * mix1
    (c0, g0, k0, v0), (c1, g1, k1, v1) = first_rows(jnp.minimum(ctx + 1, n_ctx - 1))
    leaving = res[...] * decay * leaving
    out0 = jnp.sum(leaving, axis=0, keepdims=True) + taps0 * (k0 * v0)
    out1 = jnp.sum(leaving * decay, axis=0, keepdims=True) + taps1 * (k0 * v0) + taps0 * (k1 * v1)
    adj0 = jnp.sum(out_gain * after, axis=0, keepdims=True)
    adj1 = jnp.sum(out_gain * jnp.exp(rates) * (after - c0 * g0), axis=0, keepdims=True)
    for j, pair in enumerate(((c0 * out0, c1 * out1), (adj0 * v0, adj1 * v1), (adj0 * k0, adj1 * k1))):
        for r in range(2):
            gfp[j, rows + r : rows + r + 1, :] = jnp.where(ctx < n_ctx - 1, pair[r], 0.0)

    def add_fwd(p, acc):
        return acc + fwd_pow[p] * part[0, p, 0:1, :]

    def add_bwd(p, acc):
        return acc + rev_pow[p] * part[1, p, 0:1, :]

    whole = lax.fori_loop(0, poles, add_fwd, long_out[...] + kern[...] * mix0 + kern_late[...] * mix1)
    gfp[0, 0:rows, :] = cot[...].astype(F32) * whole
    whole = lax.fori_loop(0, poles, add_bwd, grad_mix[...])
    gfp[1, 0:rows, :] = whole * valp[...]
    gfp[2, 0:rows, :] = whole * keyp[...]
    for j in range(3):
        acc = taps[0, j : j + 1, :] * gfp[j, 0:rows, :]
        acc += taps[1, j : j + 1, :] * gfp[j, 1 : rows + 1, :]
        acc += taps[2, j : j + 1, :] * gfp[j, 2 : rows + 2, :]
        gp[j] = acc.astype(BF16)

    def partial_of(slot):
        start = pl.multiple_of(slot * chans, chans)
        total = jnp.zeros((rows, chans), F32)
        for j in range(3):
            total += lax.dot_general(
                gp[j], w[j, pl.ds(start, chans), :], (((1,), (1,)), ((), ())), preferred_element_type=F32
            )
        return total

    def block_at(k, distance):
        c, d = streams[k]
        return at_z(column_of(c), z + distance * d)

    def r_copy(k, s, p):
        c, d = streams[k]
        there = at_z(1 - col if c == 1 and s == hops else col, z + d)
        at = (k, s, piece(p))
        return remote(rs_out.at[at], rs_in.at[at], r_send.at[k, s, p], r_recv.at[k, s, p], (ctx, there))

    def opposite(k):
        c, d = streams[k]
        p = halves(k)[0]
        there = at_z(1 - col if c == 1 and hops == 1 else col, z + 2 * d)
        at = (k, 0, piece(p))
        return remote(rs_out.at[at], rs_in.at[at], r_send.at[k, 0, p], r_recv.at[k, 0, p], (ctx, there))

    swap = remote(x_out, x_in, r_send.at[4, 0, 0], r_recv.at[4, 0, 0], (ctx, partner))

    for c in range(COLUMNS):
        both = partial_of(at_z(column_of(c), z + hops + 1)).astype(BF16)
        for k in range(4):
            if streams[k][0] == c:
                at = piece(halves(k)[0])
                rs_out[k, 0, at] = both[halves(k)[0] * size : halves(k)[0] * size + size]
                opposite(k).start()
    for pair in ((0, 1), (2, 3)):
        for k in pair:
            rs_out[k, 1] = partial_of(block_at(k, hops)).astype(BF16)
        for i in range(PIECES):
            for k in pair:
                r_copy(k, 1, halves(k)[i]).start()
    x_out[...] = partial_of(partner).astype(BF16)
    swap.start()

    for s in range(2, hops + 1):
        for k in range(4):
            ready[k] = partial_of(block_at(k, hops + 1 - s))
        for i in range(PIECES):
            for k in range(4):
                p = halves(k)[i]
                at = piece(p)
                total = ready[k, at]
                if s == 2 and i == 0:
                    opposite(k).wait_recv()
                    total += rs_in[k, 0, at].astype(F32)
                r_copy(k, s - 1, p).wait_recv()
                rs_out[k, s, at] = (total + rs_in[k, s - 1, at].astype(F32)).astype(BF16)
                r_copy(k, s, p).start()

    long_out[...] = partial_of(tp)
    swap.wait_recv()
    long_out[...] += x_in[...].astype(F32)
    if hops == 1:
        for k in range(4):
            at = piece(halves(k)[0])
            opposite(k).wait_recv()
            long_out[at] += rs_in[k, 0, at].astype(F32)
    for p in range(PIECES):
        at = piece(p)
        for k in range(4):
            r_copy(k, hops, p).wait_recv()
        total = long_out[at]
        for k in range(4):
            total += rs_in[k, hops, at].astype(F32)
        result[at] = total.astype(BF16)
    done = pltpu.make_async_copy(result, out_hbm, local_sem.at[0])
    done.start()

    swap.wait_send()
    x_pair.wait_send()
    for k in range(4):
        g_copy(k, hops + 1, halves(k)[0]).wait_send()
        opposite(k).wait_send()
        for p in range(PIECES):
            for s in range(1, hops + 1):
                g_copy(k, s, p).wait_send()
                r_copy(k, s, p).wait_send()
    done.wait()


def body(n_ctx, n_tp, inputs, w_in, conv_taps, pole_rates, residues, cotangent):
    rows, chans = inputs.shape
    width = w_in.shape[0]
    poles = pole_rates.shape[1]
    steps = n_tp // COLUMNS // 2 + 1
    vmem = pltpu.VMEM
    dma = pltpu.SemaphoreType.DMA
    scratch = [
        vmem((3, width, chans), BF16),
        vmem((n_tp, rows, chans), BF16),
        vmem((3, 3, chans), F32),
        vmem((poles, chans), F32),
        vmem((poles, chans), F32),
        vmem((rows, chans), BF16),
        vmem((3, rows + SUB, chans), F32),
        vmem((rows, chans), F32),
        vmem((rows, chans), F32),
        vmem((rows, chans), F32),
        vmem((rows + SUB, chans), F32),
        vmem((rows + SUB, chans), F32),
        vmem((poles, rows, chans), F32),
        vmem((poles, rows, chans), F32),
        vmem((rows, chans), F32),
        vmem((rows, chans), F32),
        vmem((rows, SUB, chans), F32),
        vmem((poles, chans), F32),
        vmem((n_ctx, poles, chans), F32),
        vmem((n_ctx, poles, chans), F32),
        vmem((2, poles, SUB, chans), F32),
        vmem((2, poles, chans), F32),
        vmem((2, poles + 2 * SUB, chans), BF16),
        vmem((n_ctx, poles + 2 * SUB, chans), BF16),
        vmem((3, rows + SUB, chans), F32),
        vmem((2, SUB, rows, chans), F32),
        vmem((rows, chans), F32),
        vmem((rows, chans), F32),
        vmem((3, rows, chans), BF16),
        vmem((4, rows, chans), F32),
        vmem((4, steps - 1, rows, chans), BF16),
        vmem((4, steps - 1, rows, chans), BF16),
        vmem((rows, chans), BF16),
        vmem((rows, chans), BF16),
        vmem((rows, chans), BF16),
        dma((5,)),
        dma((3,)),
        dma((5, steps, PIECES)),
        dma((5, steps, PIECES)),
        dma((n_ctx,)),
        dma((n_ctx,)),
        pltpu.SemaphoreType.REGULAR((n_ctx.bit_length(),)),
        dma((5, steps - 1, PIECES)),
        dma((5, steps - 1, PIECES)),
    ]
    return pl.pallas_call(
        functools.partial(kernel, n_ctx, n_tp),
        out_shape=jax.ShapeDtypeStruct((rows, chans), BF16),
        in_specs=[pl.BlockSpec(memory_space=pl.ANY)] * 6,
        out_specs=pl.BlockSpec(memory_space=pl.ANY),
        scratch_shapes=scratch,
        compiler_params=pltpu.CompilerParams(
            collective_id=0, has_side_effects=True, vmem_limit_bytes=60 * 1024 * 1024
        ),
        cost_estimate=pl.CostEstimate(
            flops=4 * rows * width * 3 * chans, bytes_accessed=2 * 3 * width * chans, transcendentals=0
        ),
        name="hyena_input_grad",
    )(inputs, w_in.transpose(1, 0, 2), conv_taps, pole_rates.T, residues.T, cotangent)


def solution(mesh):
    in_specs = (
        P("ctx", "tp"),
        P(None, None, "tp"),
        P(None, None, "tp"),
        P("tp", None),
        P("tp", None),
        P("ctx", "tp"),
    )
    out_specs = P("ctx", "tp")
    step = functools.partial(body, mesh.shape["ctx"], mesh.shape["tp"])
    return jax.shard_map(step, mesh=mesh, in_specs=in_specs, out_specs=out_specs, check_vma=False)
```

```python
import functools

import jax
import jax.numpy as jnp
from jax import lax
from jax.experimental import pallas as pl
from jax.experimental.pallas import tpu as pltpu
from jax.sharding import PartitionSpec as P

MESH = pl.DeviceIdType.MESH
F32 = jnp.float32
BF16 = jnp.bfloat16
SUB = 8
LANES = 128
PIECES = 2
COLUMNS = 2


def one_minus_exp(x):
    series = jnp.ones_like(x)
    for k in range(9, 1, -1):
        series = 1.0 - x * series * (1.0 / k)
    return jnp.where(x < 0.25, x * series, 1.0 - jnp.exp(-x))


def kernel(
    n_ctx,
    n_tp,
    x_hbm,
    w_hbm,
    taps_hbm,
    rate_hbm,
    res_hbm,
    cot_hbm,
    out_hbm,
    w,
    xg,
    taps,
    rate,
    res,
    cot,
    proj,
    gate,
    keyp,
    valp,
    mixp,
    glp,
    fwd_pow,
    rev_pow,
    kern,
    kern_late,
    spread,
    gain,
    w_fwd,
    w_bwd,
    part,
    ends,
    state,
    state_in,
    gfp,
    sliding,
    long_out,
    grad_mix,
    gp,
    ready,
    rs_out,
    rs_in,
    x_out,
    x_in,
    result,
    local_sem,
    w_sem,
    g_send,
    g_recv,
    s_send,
    s_recv,
    met,
    r_send,
    r_recv,
):
    rows, chans = x_hbm.shape
    poles = rate_hbm.shape[0]
    ring = n_tp // COLUMNS
    hops = ring // 2 - 1
    streams = ((0, 1), (0, -1), (1, 1), (1, -1))
    mine, theirs = (0, 1), (2, 3)
    ctx = lax.axis_index("ctx")
    tp = lax.axis_index("tp")
    col, z = tp // ring, tp % ring

    def at_z(column, zz):
        return column * ring + (zz + 2 * ring) % ring

    def column_of(c):
        return col if c == 0 else 1 - col

    partner = at_z(1 - col, z)

    rounds = n_ctx.bit_length() - 1

    def across(r):
        bit = (ctx // 2**r) % 2
        return ctx + 2**r * (1 - 2 * bit)

    barrier = pltpu.get_barrier_semaphore()
    others = [at_z(col, z + d) for d in (1, -1, 2, -2)]
    others += [at_z(1 - col, z + d) for d in (1, -1)] + [partner]
    for other in others:
        pl.semaphore_signal(barrier, inc=1, device_id=(ctx, other), device_id_type=MESH)
    for r in range(rounds):
        pl.semaphore_signal(barrier, inc=1, device_id=(across(r), tp), device_id_type=MESH)

    def greet(r):
        if r < rounds:
            pl.semaphore_signal(met.at[r], inc=1, device_id=(across(r), tp), device_id_type=MESH)

    def greeted(r):
        if r < rounds:
            pl.semaphore_wait(met.at[r], 1)

    w_copies = [pltpu.make_async_copy(w_hbm.at[j], w.at[j], w_sem.at[j]) for j in range(3)]
    small = [
        pltpu.make_async_copy(src, dst, local_sem.at[i])
        for i, (src, dst) in enumerate(
            ((x_hbm, xg.at[tp]), (taps_hbm, taps), (rate_hbm, rate), (res_hbm, res), (cot_hbm, cot))
        )
    ]
    for c in small + w_copies:
        c.start()
    pl.semaphore_wait(barrier, len(others) + rounds)

    def remote(src, dst, send, recv, device):
        return pltpu.make_async_remote_copy(
            src_ref=src, dst_ref=dst, send_sem=send, recv_sem=recv, device_id=device, device_id_type=MESH
        )

    size = rows // PIECES

    def piece(p):
        return pl.ds(p * size, size)

    def halves(k):
        return (0, 1) if streams[k][1] > 0 else (1, 0)

    def g_copy(k, s, p):
        c, d = streams[k]
        skip = 2 if s > hops else 1
        held, there = at_z(column_of(c), z - (s - skip) * d), at_z(col, z + skip * d)
        if c == 1 and s == 1:
            held, there = at_z(col, z - d), partner
        if c == 1 and s == 2:
            held, there = at_z(col, z - d), at_z(1 - col, z + d)
        block = xg.at[held, piece(p)]
        src = x_hbm.at[piece(p)] if c == 0 and s == 1 else block
        return remote(src, block, g_send.at[k, s, p], g_recv.at[k, s, p], (ctx, there))

    def arrived(k, s, p):
        here = xg.at[at_z(column_of(streams[k][0]), z - s * streams[k][1]), piece(p)]
        remote(here, here, g_send.at[k, s, p], g_recv.at[k, s, p], (ctx, partner)).wait_recv()

    x_pair = remote(x_hbm, xg.at[tp], g_send.at[4, 0, 0], g_recv.at[4, 0, 0], (ctx, partner))

    def forward(k, s, i):
        p = halves(k)[i]
        arrived(k, s, p)
        if s == hops - 1 and i == 0:
            g_copy(k, hops + 1, p).start()
        if s < hops:
            g_copy(k, s + 1, p).start()

    def block_at(k, distance):
        c, d = streams[k]
        return at_z(column_of(c), z + distance * d)

    for i in range(PIECES):
        for k in mine:
            g_copy(k, 1, halves(k)[i]).start()
    x_pair.start()
    greet(0)

    for c in small[1:]:
        c.wait()

    rates = rate[...]
    gain[...] = jnp.sqrt(one_minus_exp(2.0 * rates))
    kern[...] = jnp.zeros_like(kern)
    steps = lax.broadcasted_iota(jnp.int32, (rows, chans), 0).astype(F32)
    state_in[ctx, 0:poles] = jnp.zeros((poles, chans), BF16)

    def tables(n, _):
        r = rate[pl.ds(n, 1), :]
        up = jnp.exp(-r * steps)
        fwd_pow[n] = up
        rev_pow[n] = jnp.exp(-r * (rows - 1.0 - steps))
        kern[...] += up * (res[pl.ds(n, 1), :] * gain[pl.ds(n, 1), :])
        return 0

    def state_weights(i, _):
        gap = (jnp.abs(ctx - i) - 1) * rows
        weight = jnp.exp(-rate[...] * gap.astype(F32))
        w_fwd[i] = jnp.where(i < ctx, weight, 0.0)
        w_bwd[i] = jnp.where(i > ctx, weight, 0.0)
        return 0

    def project(slots):
        for j in range(3):
            total = proj[j, SUB:, :]
            for slot in slots:
                start = pl.multiple_of(slot * chans, chans)
                total += jnp.dot(xg[slot], w[j, pl.ds(start, chans), :], preferred_element_type=F32)
            proj[j, SUB:, :] = total

    proj[...] = jnp.zeros_like(proj)
    small[0].wait()
    for c in w_copies:
        c.wait()
    project([tp])
    per_step = -(-poles // hops)
    ctx_per_step = -(-n_ctx // hops)

    def beside(s):
        greeted(s - 1)
        greet(s)
        lax.fori_loop((s - 1) * per_step, min(s * per_step, poles), tables, 0)
        lax.fori_loop((s - 1) * ctx_per_step, min(s * ctx_per_step, n_ctx), state_weights, 0)

    for i in range(PIECES):
        for k in mine:
            forward(k, 1, i)
            g_copy(k + 2, 2, halves(k)[i]).start()
    for i in range(PIECES):
        for k in theirs:
            g_copy(k, 1, halves(k)[i]).start()
    project([block_at(k, -1) for k in mine])
    beside(1)
    for s in range(2, hops):
        for group in (mine, theirs):
            for i in range(PIECES):
                for k in group:
                    forward(k, s, i)
        project([block_at(k, -s) for k in range(4)])
        beside(s)
    x_pair.wait_recv()
    for k in mine:
        for i in range(PIECES):
            forward(k, hops, i)
    project([block_at(k, -hops) for k in mine] + [partner])
    beside(hops)
    for k in theirs:
        for i in range(PIECES):
            arrived(k, 1, halves(k)[i])
    project([block_at(k, -1) for k in theirs])
    for k in theirs:
        for i in range(PIECES):
            forward(k, hops, i)
    for k in range(4):
        arrived(k, hops + 1, halves(k)[0])
    project([block_at(k, -hops) for k in theirs] + [block_at(0, hops + 1), block_at(2, hops + 1)])

    def spread_rows(i, _):
        block = kern[pl.ds(pl.multiple_of(SUB * i, SUB), SUB), :]
        for r in range(SUB):
            spread[SUB * i + r] = jnp.broadcast_to(block[r : r + 1, :], (SUB, chans))
        return 0

    lax.fori_loop(0, rows // SUB, spread_rows, 0)
    kern_late[0:1, :] = jnp.zeros((1, chans), F32)
    kern_late[1:rows, :] = kern[0 : rows - 1, :]

    for j in range(3):
        proj[j, SUB:, :] = proj[j, SUB:, :].astype(BF16).astype(F32)
    edge = [proj[j, SUB : SUB + 1, :] for j in range(3)] + [cot[0:16, :].astype(F32)[0:1]]
    edge += [proj[j, SUB + 1 : SUB + 2, :] for j in range(3)] + [cot[0:16, :].astype(F32)[1:2]]
    blank = jnp.zeros((1, chans), F32)
    edge += [proj[j, SUB + rows - 2 : SUB + rows - 1, :] for j in range(3)] + [blank]
    edge += [proj[j, SUB + rows - 1 : SUB + rows, :] for j in range(3)] + [blank]
    edge = jnp.concatenate(edge, axis=0).astype(BF16)
    for target in (state.at[0], state.at[1], state_in.at[ctx]):
        target[poles:, :] = edge

    filtered = []
    for j in range(3):
        acc = taps[0, j : j + 1, :] * proj[j, SUB : SUB + rows, :]
        acc += taps[1, j : j + 1, :] * proj[j, SUB - 1 : SUB + rows - 1, :]
        acc += taps[2, j : j + 1, :] * proj[j, SUB - 2 : SUB + rows - 2, :]
        filtered.append(acc)
    keyp[...] = filtered[1]
    valp[...] = filtered[2]
    mixp[0:SUB, :] = jnp.zeros((SUB, chans), F32)
    mixp[SUB:, :] = jnp.where(steps >= 2.0, filtered[1] * filtered[2], 0.0)
    glp[0:rows, :] = jnp.where(steps >= 2.0, cot[...].astype(F32) * filtered[0], 0.0)
    glp[rows : rows + SUB, :] = jnp.zeros((SUB, chans), F32)

    def partial_states(n, _):
        fwd = rev_pow[n] * mixp[SUB:, :]
        bwd = fwd_pow[n] * glp[0:rows, :]
        part[0, n] = jnp.sum(fwd.reshape(rows // SUB, SUB, chans), axis=0)
        part[1, n] = jnp.sum(bwd.reshape(rows // SUB, SUB, chans), axis=0)
        return 0

    lax.fori_loop(0, poles, partial_states, 0)
    ends[0] = gain[...] * jnp.sum(part[0], axis=1)
    ends[1] = jnp.sum(part[1], axis=1)
    state[0, 0:poles, :] = ends[0].astype(BF16)
    state[1, 0:poles, :] = ends[1].astype(BF16)

    greeted(hops)
    for r in range(hops + 1, rounds):
        greet(r)
        greeted(r)

    def s_copy(o):
        other = ctx
        for r in range(rounds):
            if o >> r & 1:
                other = other + across(r) - ctx
        which = (other < ctx).astype(jnp.int32)
        return remote(state.at[which], state_in.at[ctx], s_send.at[o], s_recv.at[o], (other, tp))

    for o in range(n_ctx - 1, 0, -1):
        s_copy(o).start()

    tiles = rows // SUB

    def local_conv(which, flip, store):
        for lane in range(0, chans, LANES):
            cols = slice(lane, lane + LANES)

            def tap(r, acc, cols=cols):
                acc = list(acc)
                block = [sliding[which, r, SUB * i : SUB * i + SUB, cols] for i in range(tiles)]
                for m in range(tiles):
                    k = spread[SUB * m + r, :, cols]
                    for i in range(tiles - m):
                        if flip:
                            acc[i + m] = acc[i + m] + k * block[i]
                        else:
                            acc[i] = acc[i] + k * block[i + m]
                return tuple(acc)

            acc = lax.fori_loop(0, SUB, tap, (jnp.zeros((SUB, LANES), F32),) * tiles)
            for i in range(tiles):
                store[SUB * i : SUB * i + SUB, cols] = acc[i]

    for r in range(SUB):
        sliding[0, r] = mixp[SUB - r : SUB - r + rows, :]
        sliding[1, r] = glp[r : r + rows, :]
    local_conv(0, True, long_out)
    local_conv(1, False, grad_mix)

    for o in range(1, n_ctx):
        s_copy(o).wait()

    branch_row = lax.broadcasted_iota(jnp.int32, (SUB, chans), 0)
    upper = branch_row < 4
    tap_rows = [jnp.concatenate([taps[i], blank, taps[i], blank], axis=0) for i in range(3)]

    def first_rows(i):
        here = state_in[i, poles:, :].astype(F32)[0:SUB]
        before = state_in[jnp.maximum(i - 1, 0), poles:, :].astype(F32)[SUB:]
        before = jnp.where(i > 0, before, 0.0)
        shifted = jnp.where(upper, pltpu.roll(before, 4, 0), pltpu.roll(here, 4, 0))
        full = tap_rows[0] * here + tap_rows[1] * shifted + tap_rows[2] * before
        return [(here[r + 3 : r + 4], full[r : r + 1], full[r + 1 : r + 2], full[r + 2 : r + 3]) for r in (0, 4)]

    decay = jnp.exp(-rates)
    gained = [gain[...] * jnp.exp(-rates * (rows - 1.0)), gain[...] * jnp.exp(-rates * (rows - 2.0))]
    none = jnp.zeros((poles, chans), F32)

    def add_before(i, total):
        (_, _, k0, v0), (_, _, k1, v1) = first_rows(i)
        end = state_in[i, 0:poles, :].astype(F32) + gained[0] * (k0 * v0) + gained[1] * (k1 * v1)
        return total + w_fwd[i] * end

    def add_after(i, total):
        (c0, g0, _, _), (c1, g1, _, _) = first_rows(i)
        return total + w_bwd[i] * (state_in[i, 0:poles, :].astype(F32) + c0 * g0 + decay * (c1 * g1))

    before = lax.fori_loop(0, ctx, add_before, none)
    after = lax.fori_loop(ctx + 1, n_ctx, add_after, none)
    out_gain = res[...] * gain[...]
    part[0, :, 0, :] = res[...] * decay * before
    part[1, :, 0, :] = out_gain * decay * after

    (c0, g0, k0, v0), (c1, g1, k1, v1) = first_rows(ctx)
    keyp[0:1, :], valp[0:1, :], keyp[1:2, :], valp[1:2, :] = k0, v0, k1, v1
    mix0, mix1, gl0, gl1 = k0 * v0, k1 * v1, c0 * g0, c1 * g1
    taps0, taps1 = kern[0:1, :], kern[1:2, :]
    grad_mix[0:1, :] += taps0 * gl0 + taps1 * gl1
    grad_mix[1:2, :] += taps0 * gl1
    leaving = jnp.exp(-rates * float(rows)) * before + ends[0] + gained[0] * mix0 + gained[1] * mix1
    (c0, g0, k0, v0), (c1, g1, k1, v1) = first_rows(jnp.minimum(ctx + 1, n_ctx - 1))
    leaving = res[...] * decay * leaving
    out0 = jnp.sum(leaving, axis=0, keepdims=True) + taps0 * (k0 * v0)
    out1 = jnp.sum(leaving * decay, axis=0, keepdims=True) + taps1 * (k0 * v0) + taps0 * (k1 * v1)
    adj0 = jnp.sum(out_gain * after, axis=0, keepdims=True)
    adj1 = jnp.sum(out_gain * jnp.exp(rates) * (after - c0 * g0), axis=0, keepdims=True)
    for j, pair in enumerate(((c0 * out0, c1 * out1), (adj0 * v0, adj1 * v1), (adj0 * k0, adj1 * k1))):
        for r in range(2):
            gfp[j, rows + r : rows + r + 1, :] = jnp.where(ctx < n_ctx - 1, pair[r], 0.0)

    def add_fwd(p, acc):
        return acc + fwd_pow[p] * part[0, p, 0:1, :]

    def add_bwd(p, acc):
        return acc + rev_pow[p] * part[1, p, 0:1, :]

    whole = lax.fori_loop(0, poles, add_fwd, long_out[...] + kern[...] * mix0 + kern_late[...] * mix1)
    gfp[0, 0:rows, :] = cot[...].astype(F32) * whole
    whole = lax.fori_loop(0, poles, add_bwd, grad_mix[...])
    gfp[1, 0:rows, :] = whole * valp[...]
    gfp[2, 0:rows, :] = whole * keyp[...]
    for j in range(3):
        acc = taps[0, j : j + 1, :] * gfp[j, 0:rows, :]
        acc += taps[1, j : j + 1, :] * gfp[j, 1 : rows + 1, :]
        acc += taps[2, j : j + 1, :] * gfp[j, 2 : rows + 2, :]
        gp[j] = acc.astype(BF16)

    def partial_of(slot):
        start = pl.multiple_of(slot * chans, chans)
        total = jnp.zeros((rows, chans), F32)
        for j in range(3):
            total += lax.dot_general(
                gp[j], w[j, pl.ds(start, chans), :], (((1,), (1,)), ((), ())), preferred_element_type=F32
            )
        return total

    def r_copy(k, s, p):
        c, d = streams[k]
        there = at_z(col, z + d)
        if c == 1 and s == hops - 1:
            there = at_z(1 - col, z + d)
        if c == 1 and s == hops:
            there = partner
        at = (k, s, piece(p))
        return remote(rs_out.at[at], rs_in.at[at], r_send.at[k, s, p], r_recv.at[k, s, p], (ctx, there))

    def opposite(k):
        p = halves(k)[0]
        at = (k, 0, piece(p))
        there = at_z(col, z + 2 * streams[k][1])
        return remote(rs_out.at[at], rs_in.at[at], r_send.at[k, 0, p], r_recv.at[k, 0, p], (ctx, there))

    swap = remote(x_out, x_in, r_send.at[4, 0, 0], r_recv.at[4, 0, 0], (ctx, partner))

    for group in (mine, theirs):
        both = partial_of(block_at(group[0], hops + 1)).astype(BF16)
        for k in group:
            p = halves(k)[0]
            rs_out[k, 0, piece(p)] = both[p * size : p * size + size]
            opposite(k).start()
    for group, s, distance in ((theirs, 1, hops), (mine, 1, hops), (theirs, hops, 1)):
        for k in group:
            rs_out[k, s] = partial_of(block_at(k, distance)).astype(BF16)
        for i in range(PIECES):
            for k in group:
                r_copy(k, s, halves(k)[i]).start()
    x_out[...] = partial_of(partner).astype(BF16)
    swap.start()

    for s in range(2, hops):
        for k in range(4):
            ready[k] = partial_of(block_at(k, hops + 1 - s))
        for group in (theirs, mine):
            for i in range(PIECES):
                for k in group:
                    p = halves(k)[i]
                    at = piece(p)
                    total = ready[k, at]
                    if s == 2 and i == 0:
                        opposite(k).wait_recv()
                        total += rs_in[k, 0, at].astype(F32)
                    r_copy(k, s - 1, p).wait_recv()
                    rs_out[k, s, at] = (total + rs_in[k, s - 1, at].astype(F32)).astype(BF16)
                    r_copy(k, s, p).start()

    for k in mine:
        ready[k] = partial_of(block_at(k, 1))
    for i in range(PIECES):
        for k in mine:
            p = halves(k)[i]
            at = piece(p)
            total = ready[k, at]
            for other, step in ((k + 2, hops), (k, hops - 1), (k + 2, hops - 1)):
                r_copy(other, step, p).wait_recv()
                total += rs_in[other, step, at].astype(F32)
            rs_out[k, hops, at] = total.astype(BF16)
            r_copy(k, hops, p).start()

    long_out[...] = partial_of(tp)
    swap.wait_recv()
    long_out[...] += x_in[...].astype(F32)
    for p in range(PIECES):
        at = piece(p)
        total = long_out[at]
        for k in mine:
            r_copy(k, hops, p).wait_recv()
            total += rs_in[k, hops, at].astype(F32)
        result[at] = total.astype(BF16)
    done = pltpu.make_async_copy(result, out_hbm, local_sem.at[0])
    done.start()

    swap.wait_send()
    x_pair.wait_send()
    for k in range(4):
        g_copy(k, hops + 1, halves(k)[0]).wait_send()
        opposite(k).wait_send()
        for p in range(PIECES):
            for s in range(1, hops + 1):
                g_copy(k, s, p).wait_send()
                r_copy(k, s, p).wait_send()
    done.wait()


def body(n_ctx, n_tp, inputs, w_in, conv_taps, pole_rates, residues, cotangent):
    rows, chans = inputs.shape
    width = w_in.shape[0]
    poles = pole_rates.shape[1]
    steps = n_tp // COLUMNS // 2 + 1
    vmem = pltpu.VMEM
    dma = pltpu.SemaphoreType.DMA
    scratch = [
        vmem((3, width, chans), BF16),
        vmem((n_tp, rows, chans), BF16),
        vmem((3, 3, chans), F32),
        vmem((poles, chans), F32),
        vmem((poles, chans), F32),
        vmem((rows, chans), BF16),
        vmem((3, rows + SUB, chans), F32),
        vmem((rows, chans), F32),
        vmem((rows, chans), F32),
        vmem((rows, chans), F32),
        vmem((rows + SUB, chans), F32),
        vmem((rows + SUB, chans), F32),
        vmem((poles, rows, chans), F32),
        vmem((poles, rows, chans), F32),
        vmem((rows, chans), F32),
        vmem((rows, chans), F32),
        vmem((rows, SUB, chans), F32),
        vmem((poles, chans), F32),
        vmem((n_ctx, poles, chans), F32),
        vmem((n_ctx, poles, chans), F32),
        vmem((2, poles, SUB, chans), F32),
        vmem((2, poles, chans), F32),
        vmem((2, poles + 2 * SUB, chans), BF16),
        vmem((n_ctx, poles + 2 * SUB, chans), BF16),
        vmem((3, rows + SUB, chans), F32),
        vmem((2, SUB, rows, chans), F32),
        vmem((rows, chans), F32),
        vmem((rows, chans), F32),
        vmem((3, rows, chans), BF16),
        vmem((4, rows, chans), F32),
        vmem((4, steps - 1, rows, chans), BF16),
        vmem((4, steps - 1, rows, chans), BF16),
        vmem((rows, chans), BF16),
        vmem((rows, chans), BF16),
        vmem((rows, chans), BF16),
        dma((5,)),
        dma((3,)),
        dma((5, steps, PIECES)),
        dma((5, steps, PIECES)),
        dma((n_ctx,)),
        dma((n_ctx,)),
        pltpu.SemaphoreType.REGULAR((n_ctx.bit_length(),)),
        dma((5, steps - 1, PIECES)),
        dma((5, steps - 1, PIECES)),
    ]
    return pl.pallas_call(
        functools.partial(kernel, n_ctx, n_tp),
        out_shape=jax.ShapeDtypeStruct((rows, chans), BF16),
        in_specs=[pl.BlockSpec(memory_space=pl.ANY)] * 6,
        out_specs=pl.BlockSpec(memory_space=pl.ANY),
        scratch_shapes=scratch,
        compiler_params=pltpu.CompilerParams(
            collective_id=0, has_side_effects=True, vmem_limit_bytes=60 * 1024 * 1024
        ),
        cost_estimate=pl.CostEstimate(
            flops=4 * rows * width * 3 * chans, bytes_accessed=2 * 3 * width * chans, transcendentals=0
        ),
        name="hyena_input_grad",
    )(inputs, w_in.transpose(1, 0, 2), conv_taps, pole_rates.T, residues.T, cotangent)


def solution(mesh):
    in_specs = (
        P("ctx", "tp"),
        P(None, None, "tp"),
        P(None, None, "tp"),
        P("tp", None),
        P("tp", None),
        P("ctx", "tp"),
    )
    out_specs = P("ctx", "tp")
    step = functools.partial(body, mesh.shape["ctx"], mesh.shape["tp"])
    return jax.shard_map(step, mesh=mesh, in_specs=in_specs, out_specs=out_specs, check_vma=False)
```

```python
import functools

import jax
import jax.numpy as jnp
from jax import lax
from jax.experimental import pallas as pl
from jax.experimental.pallas import tpu as pltpu
from jax.sharding import PartitionSpec as P

MESH = pl.DeviceIdType.MESH
F32 = jnp.float32
BF16 = jnp.bfloat16
SUB = 8
LANES = 128
PIECES = 2
COLUMNS = 2


def one_minus_exp(x):
    series = jnp.ones_like(x)
    for k in range(9, 1, -1):
        series = 1.0 - x * series * (1.0 / k)
    return jnp.where(x < 0.25, x * series, 1.0 - jnp.exp(-x))


def kernel(
    n_ctx,
    n_tp,
    x_hbm,
    w_hbm,
    taps_hbm,
    rate_hbm,
    res_hbm,
    cot_hbm,
    out,
    w,
    xg,
    taps,
    rate,
    res,
    cot,
    proj,
    gate,
    keyp,
    valp,
    mixp,
    glp,
    fwd_pow,
    rev_pow,
    kern,
    kern_late,
    spread,
    gain,
    w_fwd,
    w_bwd,
    part,
    ends,
    state,
    state_in,
    gfp,
    sliding,
    long_out,
    grad_mix,
    gp,
    ready,
    rs_out,
    rs_in,
    x_out,
    x_in,
    far_out,
    far_in,
    local_sem,
    w_sem,
    g_send,
    g_recv,
    s_send,
    s_recv,
    met,
    r_send,
    r_recv,
):
    rows, chans = x_hbm.shape
    poles = rate_hbm.shape[0]
    ring = n_tp // COLUMNS
    hops = ring // 2 - 1
    streams = ((0, 1), (0, -1), (1, 1), (1, -1))
    mine, theirs = (0, 1), (2, 3)
    ctx = lax.axis_index("ctx")
    tp = lax.axis_index("tp")
    col, z = tp // ring, tp % ring

    def at_z(column, zz):
        return column * ring + (zz + 2 * ring) % ring

    def column_of(c):
        return col if c == 0 else 1 - col

    partner = at_z(1 - col, z)

    rounds = n_ctx.bit_length() - 1

    def across(r):
        bit = (ctx // 2**r) % 2
        return ctx + 2**r * (1 - 2 * bit)

    barrier = pltpu.get_barrier_semaphore()
    others = [at_z(col, z + d) for d in (1, -1, 2, -2, hops + 1)]
    others += [at_z(1 - col, z + d) for d in (1, -1)] + [partner]
    for other in others:
        pl.semaphore_signal(barrier, inc=1, device_id=(ctx, other), device_id_type=MESH)
    for r in range(rounds):
        pl.semaphore_signal(barrier, inc=1, device_id=(across(r), tp), device_id_type=MESH)

    def greet(r):
        if r < rounds:
            pl.semaphore_signal(met.at[r], inc=1, device_id=(across(r), tp), device_id_type=MESH)

    def greeted(r):
        if r < rounds:
            pl.semaphore_wait(met.at[r], 1)

    w_copies = [pltpu.make_async_copy(w_hbm.at[j], w.at[j], w_sem.at[j]) for j in range(3)]
    small = [
        pltpu.make_async_copy(src, dst, local_sem.at[i])
        for i, (src, dst) in enumerate(
            ((x_hbm, xg.at[tp]), (taps_hbm, taps), (rate_hbm, rate), (res_hbm, res), (cot_hbm, cot))
        )
    ]
    for c in small + w_copies:
        c.start()
    pl.semaphore_wait(barrier, len(others) + rounds)

    def remote(src, dst, send, recv, device):
        return pltpu.make_async_remote_copy(
            src_ref=src, dst_ref=dst, send_sem=send, recv_sem=recv, device_id=device, device_id_type=MESH
        )

    size = rows // PIECES

    def piece(p):
        return pl.ds(p * size, size)

    def halves(k):
        return (0, 1) if streams[k][1] > 0 else (1, 0)

    def g_copy(k, s, p):
        c, d = streams[k]
        skip = 2 if s > hops else 1
        held, there = at_z(column_of(c), z - (s - skip) * d), at_z(col, z + skip * d)
        if c == 1 and s == 1:
            held, there = at_z(col, z - d), partner
        if c == 1 and s == 2:
            held, there = at_z(col, z - d), at_z(1 - col, z + d)
        block = xg.at[held, piece(p)]
        src = x_hbm.at[piece(p)] if c == 0 and s == 1 else block
        return remote(src, block, g_send.at[k, s, p], g_recv.at[k, s, p], (ctx, there))

    def arrived(k, s, p):
        here = xg.at[at_z(column_of(streams[k][0]), z - s * streams[k][1]), piece(p)]
        remote(here, here, g_send.at[k, s, p], g_recv.at[k, s, p], (ctx, partner)).wait_recv()

    x_pair = remote(x_hbm, xg.at[tp], g_send.at[4, 0, 0], g_recv.at[4, 0, 0], (ctx, partner))

    def forward(k, s, i):
        p = halves(k)[i]
        arrived(k, s, p)
        if s == hops - 1 and i == 0:
            g_copy(k, hops + 1, p).start()
        if s < hops:
            g_copy(k, s + 1, p).start()

    def block_at(k, distance):
        c, d = streams[k]
        return at_z(column_of(c), z + distance * d)

    for i in range(PIECES):
        for k in mine:
            g_copy(k, 1, halves(k)[i]).start()
    x_pair.start()
    greet(0)

    for c in small[1:]:
        c.wait()

    rates = rate[...]
    gain[...] = jnp.sqrt(one_minus_exp(2.0 * rates))
    kern[...] = jnp.zeros_like(kern)
    steps = lax.broadcasted_iota(jnp.int32, (rows, chans), 0).astype(F32)
    state_in[ctx, 0:poles] = jnp.zeros((poles, chans), BF16)

    def tables(n, _):
        r = rate[pl.ds(n, 1), :]
        up = jnp.exp(-r * steps)
        fwd_pow[n] = up
        rev_pow[n] = jnp.exp(-r * (rows - 1.0 - steps))
        kern[...] += up * (res[pl.ds(n, 1), :] * gain[pl.ds(n, 1), :])
        return 0

    def state_weights(i, _):
        gap = (jnp.abs(ctx - i) - 1) * rows
        weight = jnp.exp(-rate[...] * gap.astype(F32))
        w_fwd[i] = jnp.where(i < ctx, weight, 0.0)
        w_bwd[i] = jnp.where(i > ctx, weight, 0.0)
        return 0

    def project(slots):
        for j in range(3):
            total = proj[j, SUB:, :]
            for slot in slots:
                start = pl.multiple_of(slot * chans, chans)
                total += jnp.dot(xg[slot], w[j, pl.ds(start, chans), :], preferred_element_type=F32)
            proj[j, SUB:, :] = total

    proj[...] = jnp.zeros_like(proj)
    small[0].wait()
    for c in w_copies:
        c.wait()
    project([tp])
    per_step = -(-poles // hops)
    ctx_per_step = -(-n_ctx // hops)

    def beside(s):
        greeted(s - 1)
        greet(s)
        lax.fori_loop((s - 1) * per_step, min(s * per_step, poles), tables, 0)
        lax.fori_loop((s - 1) * ctx_per_step, min(s * ctx_per_step, n_ctx), state_weights, 0)

    for i in range(PIECES):
        for k in mine:
            forward(k, 1, i)
            g_copy(k + 2, 2, halves(k)[i]).start()
    for i in range(PIECES):
        for k in theirs:
            g_copy(k, 1, halves(k)[i]).start()
    project([block_at(k, -1) for k in mine])
    beside(1)
    for s in range(2, hops):
        for group in (mine, theirs):
            for i in range(PIECES):
                for k in group:
                    forward(k, s, i)
        project([block_at(k, -s) for k in range(4)])
        beside(s)
    x_pair.wait_recv()
    for k in mine:
        for i in range(PIECES):
            forward(k, hops, i)
    project([block_at(k, -hops) for k in mine] + [partner])
    beside(hops)
    for k in theirs:
        for i in range(PIECES):
            arrived(k, 1, halves(k)[i])
    project([block_at(k, -1) for k in theirs])
    for k in theirs:
        for i in range(PIECES):
            forward(k, hops, i)
    for k in range(4):
        arrived(k, hops + 1, halves(k)[0])
    project([block_at(k, -hops) for k in theirs] + [block_at(0, hops + 1), block_at(2, hops + 1)])

    def spread_rows(i, _):
        block = kern[pl.ds(pl.multiple_of(SUB * i, SUB), SUB), :]
        for r in range(SUB):
            spread[SUB * i + r] = jnp.broadcast_to(block[r : r + 1, :], (SUB, chans))
        return 0

    lax.fori_loop(0, rows // SUB, spread_rows, 0)
    kern_late[0:1, :] = jnp.zeros((1, chans), F32)
    kern_late[1:rows, :] = kern[0 : rows - 1, :]

    for j in range(3):
        proj[j, SUB:, :] = proj[j, SUB:, :].astype(BF16).astype(F32)
    edge = [proj[j, SUB : SUB + 1, :] for j in range(3)] + [cot[0:16, :].astype(F32)[0:1]]
    edge += [proj[j, SUB + 1 : SUB + 2, :] for j in range(3)] + [cot[0:16, :].astype(F32)[1:2]]
    blank = jnp.zeros((1, chans), F32)
    edge += [proj[j, SUB + rows - 2 : SUB + rows - 1, :] for j in range(3)] + [blank]
    edge += [proj[j, SUB + rows - 1 : SUB + rows, :] for j in range(3)] + [blank]
    edge = jnp.concatenate(edge, axis=0).astype(BF16)
    for target in (state.at[0], state.at[1], state_in.at[ctx]):
        target[poles:, :] = edge

    filtered = []
    for j in range(3):
        acc = taps[0, j : j + 1, :] * proj[j, SUB : SUB + rows, :]
        acc += taps[1, j : j + 1, :] * proj[j, SUB - 1 : SUB + rows - 1, :]
        acc += taps[2, j : j + 1, :] * proj[j, SUB - 2 : SUB + rows - 2, :]
        filtered.append(acc)
    keyp[...] = filtered[1]
    valp[...] = filtered[2]
    mixp[0:SUB, :] = jnp.zeros((SUB, chans), F32)
    mixp[SUB:, :] = jnp.where(steps >= 2.0, filtered[1] * filtered[2], 0.0)
    glp[0:rows, :] = jnp.where(steps >= 2.0, cot[...].astype(F32) * filtered[0], 0.0)
    glp[rows : rows + SUB, :] = jnp.zeros((SUB, chans), F32)

    def partial_states(n, _):
        fwd = rev_pow[n] * mixp[SUB:, :]
        bwd = fwd_pow[n] * glp[0:rows, :]
        part[0, n] = jnp.sum(fwd.reshape(rows // SUB, SUB, chans), axis=0)
        part[1, n] = jnp.sum(bwd.reshape(rows // SUB, SUB, chans), axis=0)
        return 0

    lax.fori_loop(0, poles, partial_states, 0)
    ends[0] = gain[...] * jnp.sum(part[0], axis=1)
    ends[1] = jnp.sum(part[1], axis=1)
    state[0, 0:poles, :] = ends[0].astype(BF16)
    state[1, 0:poles, :] = ends[1].astype(BF16)

    greeted(hops)
    for r in range(hops + 1, rounds):
        greet(r)
        greeted(r)

    def s_copy(o):
        other = ctx
        for r in range(rounds):
            if o >> r & 1:
                other = other + across(r) - ctx
        which = (other < ctx).astype(jnp.int32)
        return remote(state.at[which], state_in.at[ctx], s_send.at[o], s_recv.at[o], (other, tp))

    for o in range(n_ctx - 1, 0, -1):
        s_copy(o).start()

    tiles = rows // SUB

    def local_conv(which, flip, store):
        for lane in range(0, chans, LANES):
            cols = slice(lane, lane + LANES)

            def tap(r, acc, cols=cols):
                acc = list(acc)
                block = [sliding[which, r, SUB * i : SUB * i + SUB, cols] for i in range(tiles)]
                for m in range(tiles):
                    k = spread[SUB * m + r, :, cols]
                    for i in range(tiles - m):
                        if flip:
                            acc[i + m] = acc[i + m] + k * block[i]
                        else:
                            acc[i] = acc[i] + k * block[i + m]
                return tuple(acc)

            acc = lax.fori_loop(0, SUB, tap, (jnp.zeros((SUB, LANES), F32),) * tiles)
            for i in range(tiles):
                store[SUB * i : SUB * i + SUB, cols] = acc[i]

    for r in range(SUB):
        sliding[0, r] = mixp[SUB - r : SUB - r + rows, :]
        sliding[1, r] = glp[r : r + rows, :]
    local_conv(0, True, long_out)
    local_conv(1, False, grad_mix)

    for o in range(1, n_ctx):
        s_copy(o).wait()

    branch_row = lax.broadcasted_iota(jnp.int32, (SUB, chans), 0)
    upper = branch_row < 4
    tap_rows = [jnp.concatenate([taps[i], blank, taps[i], blank], axis=0) for i in range(3)]

    def first_rows(i):
        here = state_in[i, poles:, :].astype(F32)[0:SUB]
        before = state_in[jnp.maximum(i - 1, 0), poles:, :].astype(F32)[SUB:]
        before = jnp.where(i > 0, before, 0.0)
        shifted = jnp.where(upper, pltpu.roll(before, 4, 0), pltpu.roll(here, 4, 0))
        full = tap_rows[0] * here + tap_rows[1] * shifted + tap_rows[2] * before
        return [(here[r + 3 : r + 4], full[r : r + 1], full[r + 1 : r + 2], full[r + 2 : r + 3]) for r in (0, 4)]

    decay = jnp.exp(-rates)
    gained = [gain[...] * jnp.exp(-rates * (rows - 1.0)), gain[...] * jnp.exp(-rates * (rows - 2.0))]
    none = jnp.zeros((poles, chans), F32)

    def add_before(i, total):
        (_, _, k0, v0), (_, _, k1, v1) = first_rows(i)
        end = state_in[i, 0:poles, :].astype(F32) + gained[0] * (k0 * v0) + gained[1] * (k1 * v1)
        return total + w_fwd[i] * end

    def add_after(i, total):
        (c0, g0, _, _), (c1, g1, _, _) = first_rows(i)
        return total + w_bwd[i] * (state_in[i, 0:poles, :].astype(F32) + c0 * g0 + decay * (c1 * g1))

    before = lax.fori_loop(0, ctx, add_before, none)
    after = lax.fori_loop(ctx + 1, n_ctx, add_after, none)
    out_gain = res[...] * gain[...]
    part[0, :, 0, :] = res[...] * decay * before
    part[1, :, 0, :] = out_gain * decay * after

    (c0, g0, k0, v0), (c1, g1, k1, v1) = first_rows(ctx)
    keyp[0:1, :], valp[0:1, :], keyp[1:2, :], valp[1:2, :] = k0, v0, k1, v1
    mix0, mix1, gl0, gl1 = k0 * v0, k1 * v1, c0 * g0, c1 * g1
    taps0, taps1 = kern[0:1, :], kern[1:2, :]
    grad_mix[0:1, :] += taps0 * gl0 + taps1 * gl1
    grad_mix[1:2, :] += taps0 * gl1
    leaving = jnp.exp(-rates * float(rows)) * before + ends[0] + gained[0] * mix0 + gained[1] * mix1
    (c0, g0, k0, v0), (c1, g1, k1, v1) = first_rows(jnp.minimum(ctx + 1, n_ctx - 1))
    leaving = res[...] * decay * leaving
    out0 = jnp.sum(leaving, axis=0, keepdims=True) + taps0 * (k0 * v0)
    out1 = jnp.sum(leaving * decay, axis=0, keepdims=True) + taps1 * (k0 * v0) + taps0 * (k1 * v1)
    adj0 = jnp.sum(out_gain * after, axis=0, keepdims=True)
    adj1 = jnp.sum(out_gain * jnp.exp(rates) * (after - c0 * g0), axis=0, keepdims=True)
    for j, pair in enumerate(((c0 * out0, c1 * out1), (adj0 * v0, adj1 * v1), (adj0 * k0, adj1 * k1))):
        for r in range(2):
            gfp[j, rows + r : rows + r + 1, :] = jnp.where(ctx < n_ctx - 1, pair[r], 0.0)

    def add_fwd(p, acc):
        return acc + fwd_pow[p] * part[0, p, 0:1, :]

    def add_bwd(p, acc):
        return acc + rev_pow[p] * part[1, p, 0:1, :]

    whole = lax.fori_loop(0, poles, add_fwd, long_out[...] + kern[...] * mix0 + kern_late[...] * mix1)
    gfp[0, 0:rows, :] = cot[...].astype(F32) * whole
    whole = lax.fori_loop(0, poles, add_bwd, grad_mix[...])
    gfp[1, 0:rows, :] = whole * valp[...]
    gfp[2, 0:rows, :] = whole * keyp[...]
    for j in range(3):
        acc = taps[0, j : j + 1, :] * gfp[j, 0:rows, :]
        acc += taps[1, j : j + 1, :] * gfp[j, 1 : rows + 1, :]
        acc += taps[2, j : j + 1, :] * gfp[j, 2 : rows + 2, :]
        gp[j] = acc.astype(BF16)

    def partial_of(slot):
        start = pl.multiple_of(slot * chans, chans)
        total = jnp.zeros((rows, chans), F32)
        for j in range(3):
            total += lax.dot_general(
                gp[j], w[j, pl.ds(start, chans), :], (((1,), (1,)), ((), ())), preferred_element_type=F32
            )
        return total

    def r_copy(k, s, p):
        c, d = streams[k]
        there = at_z(col, z + d)
        if c == 1 and s == hops - 1:
            there = at_z(1 - col, z + d)
        if c == 1 and s == hops:
            there = partner
        at = (k, s, piece(p))
        return remote(rs_out.at[at], rs_in.at[at], r_send.at[k, s, p], r_recv.at[k, s, p], (ctx, there))

    far_pair = remote(far_out.at[0], far_in.at[0], r_send.at[4, 1, 0], r_recv.at[4, 1, 0], (ctx, partner))
    far_sum = remote(far_out.at[1], far_in.at[1], r_send.at[4, 2, 0], r_recv.at[4, 2, 0], (ctx, at_z(col, z + hops + 1)))

    swap = remote(x_out, x_in, r_send.at[4, 0, 0], r_recv.at[4, 0, 0], (ctx, partner))

    for group, s, distance in ((theirs, 1, hops), (mine, 1, hops), (theirs, hops, 1)):
        if s == hops:
            far_out[0] = partial_of(block_at(theirs[0], hops + 1)).astype(BF16)
            far_pair.start()
        for k in group:
            rs_out[k, s] = partial_of(block_at(k, distance)).astype(BF16)
        for i in range(PIECES):
            for k in group:
                r_copy(k, s, halves(k)[i]).start()
    x_out[...] = partial_of(partner).astype(BF16)
    swap.start()

    for s in range(2, hops):
        for k in range(4):
            ready[k] = partial_of(block_at(k, hops + 1 - s))
        for group in (theirs, mine):
            for i in range(PIECES):
                for k in group:
                    p = halves(k)[i]
                    at = piece(p)
                    total = ready[k, at]
                    r_copy(k, s - 1, p).wait_recv()
                    rs_out[k, s, at] = (total + rs_in[k, s - 1, at].astype(F32)).astype(BF16)
                    r_copy(k, s, p).start()

    ready[2] = partial_of(block_at(0, hops + 1))
    for k in mine:
        ready[k] = partial_of(block_at(k, 1))
    far_pair.wait_recv()
    far_out[1] = (ready[2] + far_in[0].astype(F32)).astype(BF16)
    far_sum.start()
    for i in range(PIECES):
        for k in mine:
            p = halves(k)[i]
            at = piece(p)
            total = ready[k, at]
            for other, step in ((k + 2, hops), (k, hops - 1), (k + 2, hops - 1)):
                r_copy(other, step, p).wait_recv()
                total += rs_in[other, step, at].astype(F32)
            rs_out[k, hops, at] = total.astype(BF16)
            r_copy(k, hops, p).start()

    long_out[...] = partial_of(tp)
    swap.wait_recv()
    long_out[...] += x_in[...].astype(F32)
    far_sum.wait_recv()
    long_out[...] += far_in[1].astype(F32)
    for p in range(PIECES):
        at = piece(p)
        total = long_out[at]
        for k in mine:
            r_copy(k, hops, p).wait_recv()
            total += rs_in[k, hops, at].astype(F32)
        out[at] = total.astype(BF16)

    swap.wait_send()
    x_pair.wait_send()
    far_pair.wait_send()
    far_sum.wait_send()
    for k in range(4):
        g_copy(k, hops + 1, halves(k)[0]).wait_send()
        for p in range(PIECES):
            for s in range(1, hops + 1):
                g_copy(k, s, p).wait_send()
                r_copy(k, s, p).wait_send()


def body(n_ctx, n_tp, inputs, w_in, conv_taps, pole_rates, residues, cotangent):
    rows, chans = inputs.shape
    width = w_in.shape[0]
    poles = pole_rates.shape[1]
    steps = n_tp // COLUMNS // 2 + 1
    vmem = pltpu.VMEM
    dma = pltpu.SemaphoreType.DMA
    scratch = [
        vmem((3, width, chans), BF16),
        vmem((n_tp, rows, chans), BF16),
        vmem((3, 3, chans), F32),
        vmem((poles, chans), F32),
        vmem((poles, chans), F32),
        vmem((rows, chans), BF16),
        vmem((3, rows + SUB, chans), F32),
        vmem((rows, chans), F32),
        vmem((rows, chans), F32),
        vmem((rows, chans), F32),
        vmem((rows + SUB, chans), F32),
        vmem((rows + SUB, chans), F32),
        vmem((poles, rows, chans), F32),
        vmem((poles, rows, chans), F32),
        vmem((rows, chans), F32),
        vmem((rows, chans), F32),
        vmem((rows, SUB, chans), F32),
        vmem((poles, chans), F32),
        vmem((n_ctx, poles, chans), F32),
        vmem((n_ctx, poles, chans), F32),
        vmem((2, poles, SUB, chans), F32),
        vmem((2, poles, chans), F32),
        vmem((2, poles + 2 * SUB, chans), BF16),
        vmem((n_ctx, poles + 2 * SUB, chans), BF16),
        vmem((3, rows + SUB, chans), F32),
        vmem((2, SUB, rows, chans), F32),
        vmem((rows, chans), F32),
        vmem((rows, chans), F32),
        vmem((3, rows, chans), BF16),
        vmem((4, rows, chans), F32),
        vmem((4, steps - 1, rows, chans), BF16),
        vmem((4, steps - 1, rows, chans), BF16),
        vmem((rows, chans), BF16),
        vmem((rows, chans), BF16),
        vmem((2, rows, chans), BF16),
        vmem((2, rows, chans), BF16),
        dma((5,)),
        dma((3,)),
        dma((5, steps, PIECES)),
        dma((5, steps, PIECES)),
        dma((n_ctx,)),
        dma((n_ctx,)),
        pltpu.SemaphoreType.REGULAR((n_ctx.bit_length(),)),
        dma((5, steps - 1, PIECES)),
        dma((5, steps - 1, PIECES)),
    ]
    return pl.pallas_call(
        functools.partial(kernel, n_ctx, n_tp),
        out_shape=pltpu.VMEM((rows, chans), BF16),
        in_specs=[pl.BlockSpec(memory_space=pl.ANY)] * 6,
        out_specs=pl.BlockSpec(memory_space=pltpu.VMEM),
        scratch_shapes=scratch,
        compiler_params=pltpu.CompilerParams(
            collective_id=0, has_side_effects=True, vmem_limit_bytes=60 * 1024 * 1024
        ),
        cost_estimate=pl.CostEstimate(
            flops=4 * rows * width * 3 * chans, bytes_accessed=2 * 3 * width * chans, transcendentals=0
        ),
        name="hyena_input_grad",
    )(inputs, w_in.transpose(1, 0, 2), conv_taps, pole_rates.T, residues.T, cotangent)


def solution(mesh):
    in_specs = (
        P("ctx", "tp"),
        P(None, None, "tp"),
        P(None, None, "tp"),
        P("tp", None),
        P("tp", None),
        P("ctx", "tp"),
    )
    out_specs = P("ctx", "tp")
    step = functools.partial(body, mesh.shape["ctx"], mesh.shape["tp"])
    return jax.shard_map(step, mesh=mesh, in_specs=in_specs, out_specs=out_specs, check_vma=False)
```

```python
import functools

import jax
import jax.numpy as jnp
from jax import lax
from jax.experimental import pallas as pl
from jax.experimental.pallas import tpu as pltpu
from jax.sharding import PartitionSpec as P

MESH = pl.DeviceIdType.MESH
F32 = jnp.float32
BF16 = jnp.bfloat16
SUB = 8
LANES = 128
PIECES = 2
COLUMNS = 2


def one_minus_exp(x):
    series = jnp.ones_like(x)
    for k in range(9, 1, -1):
        series = 1.0 - x * series * (1.0 / k)
    return jnp.where(x < 0.25, x * series, 1.0 - jnp.exp(-x))


def kernel(
    n_ctx,
    n_tp,
    x_hbm,
    w_hbm,
    taps_hbm,
    rate_hbm,
    res_hbm,
    cot_hbm,
    out,
    w,
    xg,
    taps,
    rate,
    res,
    cot,
    proj,
    gate,
    keyp,
    valp,
    mixp,
    glp,
    fwd_pow,
    rev_pow,
    kern,
    kern_late,
    spread,
    gain,
    w_fwd,
    w_bwd,
    part,
    ends,
    state,
    state_in,
    gfp,
    sliding,
    long_out,
    grad_mix,
    gp,
    ready,
    rs_out,
    rs_in,
    x_out,
    x_in,
    far_out,
    far_in,
    local_sem,
    w_sem,
    g_send,
    g_recv,
    s_send,
    s_recv,
    met,
    r_send,
    r_recv,
):
    rows, chans = x_hbm.shape
    poles = rate_hbm.shape[0]
    ring = n_tp // COLUMNS
    hops = ring // 2 - 1
    streams = ((0, 1), (0, -1), (1, 1), (1, -1))
    mine, theirs = (0, 1), (2, 3)
    ctx = lax.axis_index("ctx")
    tp = lax.axis_index("tp")
    col, z = tp // ring, tp % ring

    def at_z(column, zz):
        return column * ring + (zz + 2 * ring) % ring

    def column_of(c):
        return col if c == 0 else 1 - col

    partner = at_z(1 - col, z)

    rounds = n_ctx.bit_length() - 1

    def across(r):
        bit = (ctx // 2**r) % 2
        return ctx + 2**r * (1 - 2 * bit)

    barrier = pltpu.get_barrier_semaphore()
    others = [at_z(col, z + d) for d in (1, -1, 2, -2, hops + 1)]
    others += [at_z(1 - col, z + d) for d in (1, -1)] + [partner]
    for other in others:
        pl.semaphore_signal(barrier, inc=1, device_id=(ctx, other), device_id_type=MESH)
    for r in range(rounds):
        pl.semaphore_signal(barrier, inc=1, device_id=(across(r), tp), device_id_type=MESH)

    def greet(r):
        if r < rounds:
            pl.semaphore_signal(met.at[r], inc=1, device_id=(across(r), tp), device_id_type=MESH)

    def greeted(r):
        if r < rounds:
            pl.semaphore_wait(met.at[r], 1)

    w_copies = [pltpu.make_async_copy(w_hbm.at[j], w.at[j], w_sem.at[j]) for j in range(3)]
    small = [
        pltpu.make_async_copy(src, dst, local_sem.at[i])
        for i, (src, dst) in enumerate(
            ((x_hbm, xg.at[tp]), (taps_hbm, taps), (rate_hbm, rate), (res_hbm, res), (cot_hbm, cot))
        )
    ]
    pl.semaphore_wait(barrier, len(others) + rounds)

    def remote(src, dst, send, recv, device):
        return pltpu.make_async_remote_copy(
            src_ref=src, dst_ref=dst, send_sem=send, recv_sem=recv, device_id=device, device_id_type=MESH
        )

    size = rows // PIECES

    def piece(p):
        return pl.ds(p * size, size)

    def halves(k):
        return (0, 1) if streams[k][1] > 0 else (1, 0)

    def g_copy(k, s, p):
        c, d = streams[k]
        skip = 2 if s > hops else 1
        held, there = at_z(column_of(c), z - (s - skip) * d), at_z(col, z + skip * d)
        if c == 1 and s == 1:
            held, there = at_z(col, z - d), partner
        if c == 1 and s == 2:
            held, there = at_z(col, z - d), at_z(1 - col, z + d)
        block = xg.at[held, piece(p)]
        src = x_hbm.at[piece(p)] if c == 0 and s == 1 else block
        return remote(src, block, g_send.at[k, s, p], g_recv.at[k, s, p], (ctx, there))

    def arrived(k, s, p):
        here = xg.at[at_z(column_of(streams[k][0]), z - s * streams[k][1]), piece(p)]
        remote(here, here, g_send.at[k, s, p], g_recv.at[k, s, p], (ctx, partner)).wait_recv()

    x_pair = remote(x_hbm, xg.at[tp], g_send.at[4, 0, 0], g_recv.at[4, 0, 0], (ctx, partner))

    def forward(k, s, i):
        p = halves(k)[i]
        arrived(k, s, p)
        if s == hops - 1 and i == 0:
            g_copy(k, hops + 1, p).start()
        if s < hops:
            g_copy(k, s + 1, p).start()

    def block_at(k, distance):
        c, d = streams[k]
        return at_z(column_of(c), z + distance * d)

    for i in range(PIECES):
        for k in mine:
            g_copy(k, 1, halves(k)[i]).start()
    x_pair.start()
    for c in small + w_copies:
        c.start()
    greet(0)

    for c in small[1:]:
        c.wait()

    rates = rate[...]
    gain[...] = jnp.sqrt(one_minus_exp(2.0 * rates))
    kern[...] = jnp.zeros_like(kern)
    steps = lax.broadcasted_iota(jnp.int32, (rows, chans), 0).astype(F32)
    state_in[ctx, 0:poles] = jnp.zeros((poles, chans), BF16)

    def tables(n, _):
        r = rate[pl.ds(n, 1), :]
        up = jnp.exp(-r * steps)
        fwd_pow[n] = up
        rev_pow[n] = jnp.exp(-r * (rows - 1.0 - steps))
        kern[...] += up * (res[pl.ds(n, 1), :] * gain[pl.ds(n, 1), :])
        return 0

    def state_weights(i, _):
        gap = (jnp.abs(ctx - i) - 1) * rows
        weight = jnp.exp(-rate[...] * gap.astype(F32))
        w_fwd[i] = jnp.where(i < ctx, weight, 0.0)
        w_bwd[i] = jnp.where(i > ctx, weight, 0.0)
        return 0

    def project(slots):
        for j in range(3):
            total = proj[j, SUB:, :]
            for slot in slots:
                start = pl.multiple_of(slot * chans, chans)
                total += jnp.dot(xg[slot], w[j, pl.ds(start, chans), :], preferred_element_type=F32)
            proj[j, SUB:, :] = total

    proj[...] = jnp.zeros_like(proj)
    def all_tables(part):
        half_poles, half_ctx = poles // 2, n_ctx // 2
        lax.fori_loop(part * half_poles, (part + 1) * half_poles, tables, 0)
        lax.fori_loop(part * half_ctx, (part + 1) * half_ctx, state_weights, 0)

    all_tables(0)
    for i in range(PIECES):
        for k in mine:
            forward(k, 1, i)
            g_copy(k + 2, 2, halves(k)[i]).start()
    for i in range(PIECES):
        for k in theirs:
            g_copy(k, 1, halves(k)[i]).start()
    small[0].wait()
    for c in w_copies:
        c.wait()
    project([tp] + [block_at(k, -1) for k in mine])
    greeted(0)
    greet(1)
    for s in range(2, hops):
        for group in (mine, theirs):
            for i in range(PIECES):
                for k in group:
                    forward(k, s, i)
        project([block_at(k, -s) for k in range(4)])
        greeted(s - 1)
        greet(s)
    all_tables(1)
    def spread_rows(i, _):
        block = kern[pl.ds(pl.multiple_of(SUB * i, SUB), SUB), :]
        for r in range(SUB):
            spread[SUB * i + r] = jnp.broadcast_to(block[r : r + 1, :], (SUB, chans))
        return 0

    lax.fori_loop(0, rows // SUB, spread_rows, 0)
    kern_late[0:1, :] = jnp.zeros((1, chans), F32)
    kern_late[1:rows, :] = kern[0 : rows - 1, :]

    x_pair.wait_recv()
    for k in mine:
        for i in range(PIECES):
            forward(k, hops, i)
    project([block_at(k, -hops) for k in mine] + [partner])
    greeted(hops - 1)
    greet(hops)
    for k in theirs:
        for i in range(PIECES):
            arrived(k, 1, halves(k)[i])
    for k in mine:
        arrived(k, hops + 1, halves(k)[0])
    project([block_at(k, -1) for k in theirs] + [block_at(0, hops + 1)])
    for k in theirs:
        for i in range(PIECES):
            forward(k, hops, i)
        arrived(k, hops + 1, halves(k)[0])
    project([block_at(k, -hops) for k in theirs] + [block_at(2, hops + 1)])

    for j in range(3):
        proj[j, SUB:, :] = proj[j, SUB:, :].astype(BF16).astype(F32)
    edge = [proj[j, SUB : SUB + 1, :] for j in range(3)] + [cot[0:16, :].astype(F32)[0:1]]
    edge += [proj[j, SUB + 1 : SUB + 2, :] for j in range(3)] + [cot[0:16, :].astype(F32)[1:2]]
    blank = jnp.zeros((1, chans), F32)
    edge += [proj[j, SUB + rows - 2 : SUB + rows - 1, :] for j in range(3)] + [blank]
    edge += [proj[j, SUB + rows - 1 : SUB + rows, :] for j in range(3)] + [blank]
    edge = jnp.concatenate(edge, axis=0).astype(BF16)
    for target in (state.at[0], state.at[1], state_in.at[ctx]):
        target[poles:, :] = edge

    filtered = []
    for j in range(3):
        acc = taps[0, j : j + 1, :] * proj[j, SUB : SUB + rows, :]
        acc += taps[1, j : j + 1, :] * proj[j, SUB - 1 : SUB + rows - 1, :]
        acc += taps[2, j : j + 1, :] * proj[j, SUB - 2 : SUB + rows - 2, :]
        filtered.append(acc)
    keyp[...] = filtered[1]
    valp[...] = filtered[2]
    mixp[0:SUB, :] = jnp.zeros((SUB, chans), F32)
    mixp[SUB:, :] = jnp.where(steps >= 2.0, filtered[1] * filtered[2], 0.0)
    glp[0:rows, :] = jnp.where(steps >= 2.0, cot[...].astype(F32) * filtered[0], 0.0)
    glp[rows : rows + SUB, :] = jnp.zeros((SUB, chans), F32)

    def partial_states(n, _):
        fwd = rev_pow[n] * mixp[SUB:, :]
        bwd = fwd_pow[n] * glp[0:rows, :]
        part[0, n] = jnp.sum(fwd.reshape(rows // SUB, SUB, chans), axis=0)
        part[1, n] = jnp.sum(bwd.reshape(rows // SUB, SUB, chans), axis=0)
        return 0

    lax.fori_loop(0, poles, partial_states, 0)
    ends[0] = gain[...] * jnp.sum(part[0], axis=1)
    ends[1] = jnp.sum(part[1], axis=1)
    state[0, 0:poles, :] = ends[0].astype(BF16)
    state[1, 0:poles, :] = ends[1].astype(BF16)

    greeted(hops)
    for r in range(hops + 1, rounds):
        greet(r)
        greeted(r)

    def s_copy(o):
        other = ctx
        for r in range(rounds):
            if o >> r & 1:
                other = other + across(r) - ctx
        which = (other < ctx).astype(jnp.int32)
        return remote(state.at[which], state_in.at[ctx], s_send.at[o], s_recv.at[o], (other, tp))

    for o in range(n_ctx - 1, 0, -1):
        s_copy(o).start()

    tiles = rows // SUB

    def local_conv(which, flip, store):
        for lane in range(0, chans, LANES):
            cols = slice(lane, lane + LANES)

            def tap(r, acc, cols=cols):
                acc = list(acc)
                block = [sliding[which, r, SUB * i : SUB * i + SUB, cols] for i in range(tiles)]
                for m in range(tiles):
                    k = spread[SUB * m + r, :, cols]
                    for i in range(tiles - m):
                        if flip:
                            acc[i + m] = acc[i + m] + k * block[i]
                        else:
                            acc[i] = acc[i] + k * block[i + m]
                return tuple(acc)

            acc = lax.fori_loop(0, SUB, tap, (jnp.zeros((SUB, LANES), F32),) * tiles)
            for i in range(tiles):
                store[SUB * i : SUB * i + SUB, cols] = acc[i]

    for r in range(SUB):
        sliding[0, r] = mixp[SUB - r : SUB - r + rows, :]
        sliding[1, r] = glp[r : r + rows, :]
    local_conv(0, True, long_out)
    local_conv(1, False, grad_mix)

    for o in range(1, n_ctx):
        s_copy(o).wait()

    branch_row = lax.broadcasted_iota(jnp.int32, (SUB, chans), 0)
    upper = branch_row < 4
    tap_rows = [jnp.concatenate([taps[i], blank, taps[i], blank], axis=0) for i in range(3)]

    def first_rows(i):
        here = state_in[i, poles:, :].astype(F32)[0:SUB]
        before = state_in[jnp.maximum(i - 1, 0), poles:, :].astype(F32)[SUB:]
        before = jnp.where(i > 0, before, 0.0)
        shifted = jnp.where(upper, pltpu.roll(before, 4, 0), pltpu.roll(here, 4, 0))
        full = tap_rows[0] * here + tap_rows[1] * shifted + tap_rows[2] * before
        return [(here[r + 3 : r + 4], full[r : r + 1], full[r + 1 : r + 2], full[r + 2 : r + 3]) for r in (0, 4)]

    decay = jnp.exp(-rates)
    gained = [gain[...] * jnp.exp(-rates * (rows - 1.0)), gain[...] * jnp.exp(-rates * (rows - 2.0))]
    none = jnp.zeros((poles, chans), F32)

    def add_before(i, total):
        (_, _, k0, v0), (_, _, k1, v1) = first_rows(i)
        end = state_in[i, 0:poles, :].astype(F32) + gained[0] * (k0 * v0) + gained[1] * (k1 * v1)
        return total + w_fwd[i] * end

    def add_after(i, total):
        (c0, g0, _, _), (c1, g1, _, _) = first_rows(i)
        return total + w_bwd[i] * (state_in[i, 0:poles, :].astype(F32) + c0 * g0 + decay * (c1 * g1))

    before = lax.fori_loop(0, ctx, add_before, none)
    after = lax.fori_loop(ctx + 1, n_ctx, add_after, none)
    out_gain = res[...] * gain[...]
    part[0, :, 0, :] = res[...] * decay * before
    part[1, :, 0, :] = out_gain * decay * after

    (c0, g0, k0, v0), (c1, g1, k1, v1) = first_rows(ctx)
    keyp[0:1, :], valp[0:1, :], keyp[1:2, :], valp[1:2, :] = k0, v0, k1, v1
    mix0, mix1, gl0, gl1 = k0 * v0, k1 * v1, c0 * g0, c1 * g1
    taps0, taps1 = kern[0:1, :], kern[1:2, :]
    grad_mix[0:1, :] += taps0 * gl0 + taps1 * gl1
    grad_mix[1:2, :] += taps0 * gl1
    leaving = jnp.exp(-rates * float(rows)) * before + ends[0] + gained[0] * mix0 + gained[1] * mix1
    (c0, g0, k0, v0), (c1, g1, k1, v1) = first_rows(jnp.minimum(ctx + 1, n_ctx - 1))
    leaving = res[...] * decay * leaving
    out0 = jnp.sum(leaving, axis=0, keepdims=True) + taps0 * (k0 * v0)
    out1 = jnp.sum(leaving * decay, axis=0, keepdims=True) + taps1 * (k0 * v0) + taps0 * (k1 * v1)
    adj0 = jnp.sum(out_gain * after, axis=0, keepdims=True)
    adj1 = jnp.sum(out_gain * jnp.exp(rates) * (after - c0 * g0), axis=0, keepdims=True)
    for j, pair in enumerate(((c0 * out0, c1 * out1), (adj0 * v0, adj1 * v1), (adj0 * k0, adj1 * k1))):
        for r in range(2):
            gfp[j, rows + r : rows + r + 1, :] = jnp.where(ctx < n_ctx - 1, pair[r], 0.0)

    def add_fwd(p, acc):
        return acc + fwd_pow[p] * part[0, p, 0:1, :]

    def add_bwd(p, acc):
        return acc + rev_pow[p] * part[1, p, 0:1, :]

    whole = lax.fori_loop(0, poles, add_fwd, long_out[...] + kern[...] * mix0 + kern_late[...] * mix1)
    gfp[0, 0:rows, :] = cot[...].astype(F32) * whole
    whole = lax.fori_loop(0, poles, add_bwd, grad_mix[...])
    gfp[1, 0:rows, :] = whole * valp[...]
    gfp[2, 0:rows, :] = whole * keyp[...]
    for j in range(3):
        acc = taps[0, j : j + 1, :] * gfp[j, 0:rows, :]
        acc += taps[1, j : j + 1, :] * gfp[j, 1 : rows + 1, :]
        acc += taps[2, j : j + 1, :] * gfp[j, 2 : rows + 2, :]
        gp[j] = acc.astype(BF16)

    def partial_of(slot):
        start = pl.multiple_of(slot * chans, chans)
        total = jnp.zeros((rows, chans), F32)
        for j in range(3):
            total += lax.dot_general(
                gp[j], w[j, pl.ds(start, chans), :], (((1,), (1,)), ((), ())), preferred_element_type=F32
            )
        return total

    def r_copy(k, s, p):
        c, d = streams[k]
        there = at_z(col, z + d)
        if c == 1 and s == hops - 1:
            there = at_z(1 - col, z + d)
        if c == 1 and s == hops:
            there = partner
        at = (k, s, piece(p))
        return remote(rs_out.at[at], rs_in.at[at], r_send.at[k, s, p], r_recv.at[k, s, p], (ctx, there))

    far_pair = remote(far_out.at[0], far_in.at[0], r_send.at[4, 1, 0], r_recv.at[4, 1, 0], (ctx, partner))
    far_sum = remote(far_out.at[1], far_in.at[1], r_send.at[4, 2, 0], r_recv.at[4, 2, 0], (ctx, at_z(col, z + hops + 1)))

    swap = remote(x_out, x_in, r_send.at[4, 0, 0], r_recv.at[4, 0, 0], (ctx, partner))

    for group, s, distance in ((theirs, 1, hops), (mine, 1, hops), (theirs, hops, 1)):
        if s == hops:
            far_out[0] = partial_of(block_at(theirs[0], hops + 1)).astype(BF16)
            far_pair.start()
        for k in group:
            rs_out[k, s] = partial_of(block_at(k, distance)).astype(BF16)
        for i in range(PIECES):
            for k in group:
                r_copy(k, s, halves(k)[i]).start()
    x_out[...] = partial_of(partner).astype(BF16)
    swap.start()

    for s in range(2, hops):
        for k in range(4):
            ready[k] = partial_of(block_at(k, hops + 1 - s))
        for group in (theirs, mine):
            for i in range(PIECES):
                for k in group:
                    p = halves(k)[i]
                    at = piece(p)
                    total = ready[k, at]
                    r_copy(k, s - 1, p).wait_recv()
                    rs_out[k, s, at] = (total + rs_in[k, s - 1, at].astype(F32)).astype(BF16)
                    r_copy(k, s, p).start()

    ready[2] = partial_of(block_at(0, hops + 1))
    for k in mine:
        ready[k] = partial_of(block_at(k, 1))
    far_pair.wait_recv()
    far_out[1] = (ready[2] + far_in[0].astype(F32)).astype(BF16)
    far_sum.start()
    for i in range(PIECES):
        for k in mine:
            p = halves(k)[i]
            at = piece(p)
            total = ready[k, at]
            for other, step in ((k + 2, hops), (k, hops - 1), (k + 2, hops - 1)):
                r_copy(other, step, p).wait_recv()
                total += rs_in[other, step, at].astype(F32)
            rs_out[k, hops, at] = total.astype(BF16)
            r_copy(k, hops, p).start()

    long_out[...] = partial_of(tp)
    swap.wait_recv()
    long_out[...] += x_in[...].astype(F32)
    far_sum.wait_recv()
    long_out[...] += far_in[1].astype(F32)
    for p in range(PIECES):
        at = piece(p)
        total = long_out[at]
        for k in mine:
            r_copy(k, hops, p).wait_recv()
            total += rs_in[k, hops, at].astype(F32)
        out[at] = total.astype(BF16)

    swap.wait_send()
    x_pair.wait_send()
    far_pair.wait_send()
    far_sum.wait_send()
    for k in range(4):
        g_copy(k, hops + 1, halves(k)[0]).wait_send()
        for p in range(PIECES):
            for s in range(1, hops + 1):
                g_copy(k, s, p).wait_send()
                r_copy(k, s, p).wait_send()


def body(n_ctx, n_tp, inputs, w_in, conv_taps, pole_rates, residues, cotangent):
    rows, chans = inputs.shape
    width = w_in.shape[0]
    poles = pole_rates.shape[1]
    steps = n_tp // COLUMNS // 2 + 1
    vmem = pltpu.VMEM
    dma = pltpu.SemaphoreType.DMA
    scratch = [
        vmem((3, width, chans), BF16),
        vmem((n_tp, rows, chans), BF16),
        vmem((3, 3, chans), F32),
        vmem((poles, chans), F32),
        vmem((poles, chans), F32),
        vmem((rows, chans), BF16),
        vmem((3, rows + SUB, chans), F32),
        vmem((rows, chans), F32),
        vmem((rows, chans), F32),
        vmem((rows, chans), F32),
        vmem((rows + SUB, chans), F32),
        vmem((rows + SUB, chans), F32),
        vmem((poles, rows, chans), F32),
        vmem((poles, rows, chans), F32),
        vmem((rows, chans), F32),
        vmem((rows, chans), F32),
        vmem((rows, SUB, chans), F32),
        vmem((poles, chans), F32),
        vmem((n_ctx, poles, chans), F32),
        vmem((n_ctx, poles, chans), F32),
        vmem((2, poles, SUB, chans), F32),
        vmem((2, poles, chans), F32),
        vmem((2, poles + 2 * SUB, chans), BF16),
        vmem((n_ctx, poles + 2 * SUB, chans), BF16),
        vmem((3, rows + SUB, chans), F32),
        vmem((2, SUB, rows, chans), F32),
        vmem((rows, chans), F32),
        vmem((rows, chans), F32),
        vmem((3, rows, chans), BF16),
        vmem((4, rows, chans), F32),
        vmem((4, steps - 1, rows, chans), BF16),
        vmem((4, steps - 1, rows, chans), BF16),
        vmem((rows, chans), BF16),
        vmem((rows, chans), BF16),
        vmem((2, rows, chans), BF16),
        vmem((2, rows, chans), BF16),
        dma((5,)),
        dma((3,)),
        dma((5, steps, PIECES)),
        dma((5, steps, PIECES)),
        dma((n_ctx,)),
        dma((n_ctx,)),
        pltpu.SemaphoreType.REGULAR((n_ctx.bit_length(),)),
        dma((5, steps - 1, PIECES)),
        dma((5, steps - 1, PIECES)),
    ]
    return pl.pallas_call(
        functools.partial(kernel, n_ctx, n_tp),
        out_shape=pltpu.VMEM((rows, chans), BF16),
        in_specs=[pl.BlockSpec(memory_space=pl.ANY)] * 6,
        out_specs=pl.BlockSpec(memory_space=pltpu.VMEM),
        scratch_shapes=scratch,
        compiler_params=pltpu.CompilerParams(
            collective_id=0, has_side_effects=True, vmem_limit_bytes=60 * 1024 * 1024
        ),
        cost_estimate=pl.CostEstimate(
            flops=4 * rows * width * 3 * chans, bytes_accessed=2 * 3 * width * chans, transcendentals=0
        ),
        name="hyena_input_grad",
    )(inputs, w_in.transpose(1, 0, 2), conv_taps, pole_rates.T, residues.T, cotangent)


def solution(mesh):
    in_specs = (
        P("ctx", "tp"),
        P(None, None, "tp"),
        P(None, None, "tp"),
        P("tp", None),
        P("tp", None),
        P("ctx", "tp"),
    )
    out_specs = P("ctx", "tp")
    step = functools.partial(body, mesh.shape["ctx"], mesh.shape["tp"])
    return jax.shard_map(step, mesh=mesh, in_specs=in_specs, out_specs=out_specs, check_vma=False)
```

```python
import functools

import jax
import jax.numpy as jnp
from jax import lax
from jax.experimental import pallas as pl
from jax.experimental.pallas import tpu as pltpu
from jax.sharding import PartitionSpec as P

MESH = pl.DeviceIdType.MESH
F32 = jnp.float32
BF16 = jnp.bfloat16
SUB = 8
LANES = 128
PIECES = 2
COLUMNS = 2


def one_minus_exp(x):
    series = jnp.ones_like(x)
    for k in range(9, 1, -1):
        series = 1.0 - x * series * (1.0 / k)
    return jnp.where(x < 0.25, x * series, 1.0 - jnp.exp(-x))


def kernel(
    n_ctx,
    n_tp,
    x_hbm,
    w_hbm,
    taps_hbm,
    rate_hbm,
    res_hbm,
    cot_hbm,
    out,
    w,
    xg,
    taps,
    rate,
    res,
    cot,
    proj,
    gate,
    keyp,
    valp,
    mixp,
    glp,
    fwd_pow,
    rev_pow,
    kern,
    kern_late,
    spread,
    gain,
    w_fwd,
    w_bwd,
    part,
    ends,
    state,
    state_in,
    gfp,
    sliding,
    long_out,
    grad_mix,
    gp,
    ready,
    rs_out,
    rs_in,
    x_out,
    x_in,
    far_out,
    far_in,
    local_sem,
    w_sem,
    g_send,
    g_recv,
    s_send,
    s_recv,
    met,
    r_send,
    r_recv,
):
    rows, chans = x_hbm.shape
    poles = rate_hbm.shape[0]
    ring = n_tp // COLUMNS
    hops = ring // 2 - 1
    streams = ((0, 1), (0, -1), (1, 1), (1, -1))
    mine, theirs = (0, 1), (2, 3)
    ctx = lax.axis_index("ctx")
    tp = lax.axis_index("tp")
    col, z = tp // ring, tp % ring

    def at_z(column, zz):
        return column * ring + (zz + 2 * ring) % ring

    def column_of(c):
        return col if c == 0 else 1 - col

    partner = at_z(1 - col, z)

    rounds = n_ctx.bit_length() - 1

    def across(r):
        bit = (ctx // 2**r) % 2
        return ctx + 2**r * (1 - 2 * bit)

    barrier = pltpu.get_barrier_semaphore()
    others = [at_z(col, z + 1), at_z(col, z - 1), partner]
    for other in others:
        pl.semaphore_signal(barrier, inc=1, device_id=(ctx, other), device_id_type=MESH)
    for r in range(rounds):
        pl.semaphore_signal(barrier, inc=1, device_id=(across(r), tp), device_id_type=MESH)

    def greet(r):
        if r < rounds:
            pl.semaphore_signal(met.at[r], inc=1, device_id=(across(r), tp), device_id_type=MESH)

    def greeted(r):
        if r < rounds:
            pl.semaphore_wait(met.at[r], 1)

    w_copies = [pltpu.make_async_copy(w_hbm.at[j], w.at[j], w_sem.at[j]) for j in range(3)]
    small = [
        pltpu.make_async_copy(src, dst, local_sem.at[i])
        for i, (src, dst) in enumerate(
            ((x_hbm, xg.at[tp]), (taps_hbm, taps), (rate_hbm, rate), (res_hbm, res), (cot_hbm, cot))
        )
    ]
    pl.semaphore_wait(barrier, len(others) + rounds)

    def remote(src, dst, send, recv, device):
        return pltpu.make_async_remote_copy(
            src_ref=src, dst_ref=dst, send_sem=send, recv_sem=recv, device_id=device, device_id_type=MESH
        )

    size = rows // PIECES

    def piece(p):
        return pl.ds(p * size, size)

    def halves(k):
        return (0, 1) if streams[k][1] > 0 else (1, 0)

    def g_copy(k, s, p):
        c, d = streams[k]
        skip = 2 if s > hops else 1
        held, there = at_z(column_of(c), z - (s - skip) * d), at_z(col, z + skip * d)
        if c == 1 and s == 1:
            held, there = at_z(col, z - d), partner
        if c == 1 and s == 2:
            held, there = at_z(col, z - d), at_z(1 - col, z + d)
        block = xg.at[held, piece(p)]
        src = x_hbm.at[piece(p)] if c == 0 and s == 1 else block
        return remote(src, block, g_send.at[k, s, p], g_recv.at[k, s, p], (ctx, there))

    def arrived(k, s, p):
        here = xg.at[at_z(column_of(streams[k][0]), z - s * streams[k][1]), piece(p)]
        remote(here, here, g_send.at[k, s, p], g_recv.at[k, s, p], (ctx, partner)).wait_recv()

    x_pair = remote(x_hbm, xg.at[tp], g_send.at[4, 0, 0], g_recv.at[4, 0, 0], (ctx, partner))

    def forward(k, s, i):
        p = halves(k)[i]
        arrived(k, s, p)
        if s == hops - 1 and i == 0:
            g_copy(k, hops + 1, p).start()
        if s < hops:
            g_copy(k, s + 1, p).start()

    def block_at(k, distance):
        c, d = streams[k]
        return at_z(column_of(c), z + distance * d)

    for i in range(PIECES):
        for k in mine:
            g_copy(k, 1, halves(k)[i]).start()
    x_pair.start()
    for c in small + w_copies:
        c.start()
    greet(0)

    for c in small[1:]:
        c.wait()

    rates = rate[...]
    gain[...] = jnp.sqrt(one_minus_exp(2.0 * rates))
    kern[...] = jnp.zeros_like(kern)
    steps = lax.broadcasted_iota(jnp.int32, (rows, chans), 0).astype(F32)
    state_in[ctx, 0:poles] = jnp.zeros((poles, chans), BF16)

    def tables(n, _):
        r = rate[pl.ds(n, 1), :]
        up = jnp.exp(-r * steps)
        fwd_pow[n] = up
        rev_pow[n] = jnp.exp(-r * (rows - 1.0 - steps))
        kern[...] += up * (res[pl.ds(n, 1), :] * gain[pl.ds(n, 1), :])
        return 0

    def state_weights(i, _):
        gap = (jnp.abs(ctx - i) - 1) * rows
        weight = jnp.exp(-rate[...] * gap.astype(F32))
        w_fwd[i] = jnp.where(i < ctx, weight, 0.0)
        w_bwd[i] = jnp.where(i > ctx, weight, 0.0)
        return 0

    def project(slots):
        for j in range(3):
            total = proj[j, SUB:, :]
            for slot in slots:
                start = pl.multiple_of(slot * chans, chans)
                total += jnp.dot(xg[slot], w[j, pl.ds(start, chans), :], preferred_element_type=F32)
            proj[j, SUB:, :] = total

    proj[...] = jnp.zeros_like(proj)
    def all_tables(part):
        half_poles, half_ctx = poles // 2, n_ctx // 2
        lax.fori_loop(part * half_poles, (part + 1) * half_poles, tables, 0)
        lax.fori_loop(part * half_ctx, (part + 1) * half_ctx, state_weights, 0)

    all_tables(0)
    for i in range(PIECES):
        for k in mine:
            forward(k, 1, i)
        for k in mine:
            g_copy(k + 2, 2, halves(k)[i]).start()
    for i in range(PIECES):
        for k in theirs:
            g_copy(k, 1, halves(k)[i]).start()
    small[0].wait()
    for c in w_copies:
        c.wait()
    project([tp] + [block_at(k, -1) for k in mine])
    greeted(0)
    greet(1)
    for s in range(2, hops):
        for group in (mine, theirs):
            for i in range(PIECES):
                for k in group:
                    forward(k, s, i)
        project([block_at(k, -s) for k in range(4)])
        greeted(s - 1)
        greet(s)
    all_tables(1)
    def spread_rows(i, _):
        block = kern[pl.ds(pl.multiple_of(SUB * i, SUB), SUB), :]
        for r in range(SUB):
            spread[SUB * i + r] = jnp.broadcast_to(block[r : r + 1, :], (SUB, chans))
        return 0

    lax.fori_loop(0, rows // SUB, spread_rows, 0)
    kern_late[0:1, :] = jnp.zeros((1, chans), F32)
    kern_late[1:rows, :] = kern[0 : rows - 1, :]

    x_pair.wait_recv()
    for k in mine:
        for i in range(PIECES):
            forward(k, hops, i)
    project([block_at(k, -hops) for k in mine] + [partner])
    greeted(hops - 1)
    greet(hops)
    for k in theirs:
        for i in range(PIECES):
            arrived(k, 1, halves(k)[i])
    for k in mine:
        arrived(k, hops + 1, halves(k)[0])
    project([block_at(k, -1) for k in theirs] + [block_at(0, hops + 1)])
    for k in theirs:
        for i in range(PIECES):
            forward(k, hops, i)
        arrived(k, hops + 1, halves(k)[0])
    project([block_at(k, -hops) for k in theirs] + [block_at(2, hops + 1)])

    for j in range(3):
        proj[j, SUB:, :] = proj[j, SUB:, :].astype(BF16).astype(F32)
    edge = [proj[j, SUB : SUB + 1, :] for j in range(3)] + [cot[0:16, :].astype(F32)[0:1]]
    edge += [proj[j, SUB + 1 : SUB + 2, :] for j in range(3)] + [cot[0:16, :].astype(F32)[1:2]]
    blank = jnp.zeros((1, chans), F32)
    edge += [proj[j, SUB + rows - 2 : SUB + rows - 1, :] for j in range(3)] + [blank]
    edge += [proj[j, SUB + rows - 1 : SUB + rows, :] for j in range(3)] + [blank]
    edge = jnp.concatenate(edge, axis=0).astype(BF16)
    for target in (state.at[0], state.at[1], state_in.at[ctx]):
        target[poles:, :] = edge

    filtered = []
    for j in range(3):
        acc = taps[0, j : j + 1, :] * proj[j, SUB : SUB + rows, :]
        acc += taps[1, j : j + 1, :] * proj[j, SUB - 1 : SUB + rows - 1, :]
        acc += taps[2, j : j + 1, :] * proj[j, SUB - 2 : SUB + rows - 2, :]
        filtered.append(acc)
    keyp[...] = filtered[1]
    valp[...] = filtered[2]
    mixp[0:SUB, :] = jnp.zeros((SUB, chans), F32)
    mixp[SUB:, :] = jnp.where(steps >= 2.0, filtered[1] * filtered[2], 0.0)
    glp[0:rows, :] = jnp.where(steps >= 2.0, cot[...].astype(F32) * filtered[0], 0.0)
    glp[rows : rows + SUB, :] = jnp.zeros((SUB, chans), F32)

    for lane in range(0, chans, LANES):
        cols = slice(lane, lane + LANES)
        mix_now, gl_now = mixp[SUB:, cols], glp[0:rows, cols]

        def partial_states(n, _, cols=cols, mix_now=mix_now, gl_now=gl_now):
            fwd = rev_pow[n, :, cols] * mix_now
            bwd = fwd_pow[n, :, cols] * gl_now
            part[0, n, :, cols] = jnp.sum(fwd.reshape(rows // SUB, SUB, LANES), axis=0)
            part[1, n, :, cols] = jnp.sum(bwd.reshape(rows // SUB, SUB, LANES), axis=0)
            return 0

        lax.fori_loop(0, poles, partial_states, 0, unroll=2)
    ends[0] = gain[...] * jnp.sum(part[0], axis=1)
    ends[1] = jnp.sum(part[1], axis=1)
    state[0, 0:poles, :] = ends[0].astype(BF16)
    state[1, 0:poles, :] = ends[1].astype(BF16)

    greeted(hops)
    for r in range(hops + 1, rounds):
        greet(r)
        greeted(r)

    def s_copy(o):
        other = ctx
        for r in range(rounds):
            if o >> r & 1:
                other = other + across(r) - ctx
        which = (other < ctx).astype(jnp.int32)
        return remote(state.at[which], state_in.at[ctx], s_send.at[o], s_recv.at[o], (other, tp))

    for o in range(n_ctx - 1, 0, -1):
        s_copy(o).start()

    tiles = rows // SUB

    def local_conv(which, flip, store):
        for lane in range(0, chans, LANES):
            cols = slice(lane, lane + LANES)

            def tap(r, acc, cols=cols):
                acc = list(acc)
                block = [sliding[which, r, SUB * i : SUB * i + SUB, cols] for i in range(tiles)]
                for m in range(tiles):
                    k = spread[SUB * m + r, :, cols]
                    for i in range(tiles - m):
                        if flip:
                            acc[i + m] = acc[i + m] + k * block[i]
                        else:
                            acc[i] = acc[i] + k * block[i + m]
                return tuple(acc)

            acc = lax.fori_loop(0, SUB, tap, (jnp.zeros((SUB, LANES), F32),) * tiles)
            for i in range(tiles):
                store[SUB * i : SUB * i + SUB, cols] = acc[i]

    for r in range(SUB):
        sliding[0, r] = mixp[SUB - r : SUB - r + rows, :]
        sliding[1, r] = glp[r : r + rows, :]
    local_conv(0, True, long_out)
    local_conv(1, False, grad_mix)

    for o in range(1, n_ctx):
        s_copy(o).wait()

    branch_row = lax.broadcasted_iota(jnp.int32, (SUB, chans), 0)
    upper = branch_row < 4
    tap_rows = [jnp.concatenate([taps[i], blank, taps[i], blank], axis=0) for i in range(3)]

    def first_rows(i):
        here = state_in[i, poles:, :].astype(F32)[0:SUB]
        before = state_in[jnp.maximum(i - 1, 0), poles:, :].astype(F32)[SUB:]
        before = jnp.where(i > 0, before, 0.0)
        shifted = jnp.where(upper, pltpu.roll(before, 4, 0), pltpu.roll(here, 4, 0))
        full = tap_rows[0] * here + tap_rows[1] * shifted + tap_rows[2] * before
        return [(here[r + 3 : r + 4], full[r : r + 1], full[r + 1 : r + 2], full[r + 2 : r + 3]) for r in (0, 4)]

    decay = jnp.exp(-rates)
    gained = [gain[...] * jnp.exp(-rates * (rows - 1.0)), gain[...] * jnp.exp(-rates * (rows - 2.0))]
    none = jnp.zeros((poles, chans), F32)

    def add_before(i, total):
        (_, _, k0, v0), (_, _, k1, v1) = first_rows(i)
        end = state_in[i, 0:poles, :].astype(F32) + gained[0] * (k0 * v0) + gained[1] * (k1 * v1)
        return total + w_fwd[i] * end

    def add_after(i, total):
        (c0, g0, _, _), (c1, g1, _, _) = first_rows(i)
        return total + w_bwd[i] * (state_in[i, 0:poles, :].astype(F32) + c0 * g0 + decay * (c1 * g1))

    before = lax.fori_loop(0, ctx, add_before, none)
    after = lax.fori_loop(ctx + 1, n_ctx, add_after, none)
    out_gain = res[...] * gain[...]
    part[0, :, 0, :] = res[...] * decay * before
    part[1, :, 0, :] = out_gain * decay * after

    (c0, g0, k0, v0), (c1, g1, k1, v1) = first_rows(ctx)
    keyp[0:1, :], valp[0:1, :], keyp[1:2, :], valp[1:2, :] = k0, v0, k1, v1
    mix0, mix1, gl0, gl1 = k0 * v0, k1 * v1, c0 * g0, c1 * g1
    taps0, taps1 = kern[0:1, :], kern[1:2, :]
    grad_mix[0:1, :] += taps0 * gl0 + taps1 * gl1
    grad_mix[1:2, :] += taps0 * gl1
    leaving = jnp.exp(-rates * float(rows)) * before + ends[0] + gained[0] * mix0 + gained[1] * mix1
    (c0, g0, k0, v0), (c1, g1, k1, v1) = first_rows(jnp.minimum(ctx + 1, n_ctx - 1))
    leaving = res[...] * decay * leaving
    out0 = jnp.sum(leaving, axis=0, keepdims=True) + taps0 * (k0 * v0)
    out1 = jnp.sum(leaving * decay, axis=0, keepdims=True) + taps1 * (k0 * v0) + taps0 * (k1 * v1)
    adj0 = jnp.sum(out_gain * after, axis=0, keepdims=True)
    adj1 = jnp.sum(out_gain * jnp.exp(rates) * (after - c0 * g0), axis=0, keepdims=True)
    for j, pair in enumerate(((c0 * out0, c1 * out1), (adj0 * v0, adj1 * v1), (adj0 * k0, adj1 * k1))):
        for r in range(2):
            gfp[j, rows + r : rows + r + 1, :] = jnp.where(ctx < n_ctx - 1, pair[r], 0.0)

    def add_fwd(p, acc):
        return acc + fwd_pow[p] * part[0, p, 0:1, :]

    def add_bwd(p, acc):
        return acc + rev_pow[p] * part[1, p, 0:1, :]

    whole = lax.fori_loop(0, poles, add_fwd, long_out[...] + kern[...] * mix0 + kern_late[...] * mix1)
    gfp[0, 0:rows, :] = cot[...].astype(F32) * whole
    whole = lax.fori_loop(0, poles, add_bwd, grad_mix[...])
    gfp[1, 0:rows, :] = whole * valp[...]
    gfp[2, 0:rows, :] = whole * keyp[...]
    for j in range(3):
        acc = taps[0, j : j + 1, :] * gfp[j, 0:rows, :]
        acc += taps[1, j : j + 1, :] * gfp[j, 1 : rows + 1, :]
        acc += taps[2, j : j + 1, :] * gfp[j, 2 : rows + 2, :]
        gp[j] = acc.astype(BF16)

    def partial_of(slot):
        start = pl.multiple_of(slot * chans, chans)
        total = jnp.zeros((rows, chans), F32)
        for j in range(3):
            total += lax.dot_general(
                gp[j], w[j, pl.ds(start, chans), :], (((1,), (1,)), ((), ())), preferred_element_type=F32
            )
        return total

    def r_copy(k, s, p):
        c, d = streams[k]
        there = at_z(col, z + d)
        if c == 1 and s == hops - 1:
            there = at_z(1 - col, z + d)
        if c == 1 and s == hops:
            there = partner
        at = (k, s, piece(p))
        return remote(rs_out.at[at], rs_in.at[at], r_send.at[k, s, p], r_recv.at[k, s, p], (ctx, there))

    far_pair = remote(far_out.at[0], far_in.at[0], r_send.at[4, 1, 0], r_recv.at[4, 1, 0], (ctx, partner))
    far_sum = remote(far_out.at[1], far_in.at[1], r_send.at[4, 2, 0], r_recv.at[4, 2, 0], (ctx, at_z(col, z + hops + 1)))

    swap = remote(x_out, x_in, r_send.at[4, 0, 0], r_recv.at[4, 0, 0], (ctx, partner))

    for group, s, distance in ((theirs, 1, hops), (mine, 1, hops), (theirs, hops, 1)):
        if s == hops:
            far_out[0] = partial_of(block_at(theirs[0], hops + 1)).astype(BF16)
            far_pair.start()
        for k in group:
            rs_out[k, s] = partial_of(block_at(k, distance)).astype(BF16)
        for i in range(PIECES):
            for k in group:
                r_copy(k, s, halves(k)[i]).start()
    x_out[...] = partial_of(partner).astype(BF16)
    swap.start()

    for s in range(2, hops):
        for k in range(4):
            ready[k] = partial_of(block_at(k, hops + 1 - s))
        for group in (theirs, mine):
            for i in range(PIECES):
                for k in group:
                    p = halves(k)[i]
                    at = piece(p)
                    total = ready[k, at]
                    r_copy(k, s - 1, p).wait_recv()
                    rs_out[k, s, at] = (total + rs_in[k, s - 1, at].astype(F32)).astype(BF16)
                    r_copy(k, s, p).start()

    ready[2] = partial_of(block_at(0, hops + 1))
    for k in mine:
        ready[k] = partial_of(block_at(k, 1))
    far_pair.wait_recv()
    far_out[1] = (ready[2] + far_in[0].astype(F32)).astype(BF16)
    far_sum.start()
    for i in range(PIECES):
        for k in mine:
            p = halves(k)[i]
            at = piece(p)
            total = ready[k, at]
            for other, step in ((k + 2, hops), (k, hops - 1), (k + 2, hops - 1)):
                r_copy(other, step, p).wait_recv()
                total += rs_in[other, step, at].astype(F32)
            rs_out[k, hops, at] = total.astype(BF16)
            r_copy(k, hops, p).start()

    long_out[...] = partial_of(tp)
    swap.wait_recv()
    long_out[...] += x_in[...].astype(F32)
    far_sum.wait_recv()
    long_out[...] += far_in[1].astype(F32)
    for p in range(PIECES):
        at = piece(p)
        total = long_out[at]
        for k in mine:
            r_copy(k, hops, p).wait_recv()
            total += rs_in[k, hops, at].astype(F32)
        out[at] = total.astype(BF16)

    swap.wait_send()
    x_pair.wait_send()
    far_pair.wait_send()
    far_sum.wait_send()
    for k in range(4):
        g_copy(k, hops + 1, halves(k)[0]).wait_send()
        for p in range(PIECES):
            for s in range(1, hops + 1):
                g_copy(k, s, p).wait_send()
                r_copy(k, s, p).wait_send()


def body(n_ctx, n_tp, inputs, w_in, conv_taps, pole_rates, residues, cotangent):
    rows, chans = inputs.shape
    width = w_in.shape[0]
    poles = pole_rates.shape[1]
    steps = n_tp // COLUMNS // 2 + 1
    vmem = pltpu.VMEM
    dma = pltpu.SemaphoreType.DMA
    scratch = [
        vmem((3, width, chans), BF16),
        vmem((n_tp, rows, chans), BF16),
        vmem((3, 3, chans), F32),
        vmem((poles, chans), F32),
        vmem((poles, chans), F32),
        vmem((rows, chans), BF16),
        vmem((3, rows + SUB, chans), F32),
        vmem((rows, chans), F32),
        vmem((rows, chans), F32),
        vmem((rows, chans), F32),
        vmem((rows + SUB, chans), F32),
        vmem((rows + SUB, chans), F32),
        vmem((poles, rows, chans), F32),
        vmem((poles, rows, chans), F32),
        vmem((rows, chans), F32),
        vmem((rows, chans), F32),
        vmem((rows, SUB, chans), F32),
        vmem((poles, chans), F32),
        vmem((n_ctx, poles, chans), F32),
        vmem((n_ctx, poles, chans), F32),
        vmem((2, poles, SUB, chans), F32),
        vmem((2, poles, chans), F32),
        vmem((2, poles + 2 * SUB, chans), BF16),
        vmem((n_ctx, poles + 2 * SUB, chans), BF16),
        vmem((3, rows + SUB, chans), F32),
        vmem((2, SUB, rows, chans), F32),
        vmem((rows, chans), F32),
        vmem((rows, chans), F32),
        vmem((3, rows, chans), BF16),
        vmem((4, rows, chans), F32),
        vmem((4, steps - 1, rows, chans), BF16),
        vmem((4, steps - 1, rows, chans), BF16),
        vmem((rows, chans), BF16),
        vmem((rows, chans), BF16),
        vmem((2, rows, chans), BF16),
        vmem((2, rows, chans), BF16),
        dma((5,)),
        dma((3,)),
        dma((5, steps, PIECES)),
        dma((5, steps, PIECES)),
        dma((n_ctx,)),
        dma((n_ctx,)),
        pltpu.SemaphoreType.REGULAR((n_ctx.bit_length(),)),
        dma((5, steps - 1, PIECES)),
        dma((5, steps - 1, PIECES)),
    ]
    return pl.pallas_call(
        functools.partial(kernel, n_ctx, n_tp),
        out_shape=pltpu.VMEM((rows, chans), BF16),
        in_specs=[pl.BlockSpec(memory_space=pl.ANY)] * 6,
        out_specs=pl.BlockSpec(memory_space=pltpu.VMEM),
        scratch_shapes=scratch,
        compiler_params=pltpu.CompilerParams(
            collective_id=0, has_side_effects=True, vmem_limit_bytes=60 * 1024 * 1024
        ),
        cost_estimate=pl.CostEstimate(
            flops=4 * rows * width * 3 * chans, bytes_accessed=2 * 3 * width * chans, transcendentals=0
        ),
        name="hyena_input_grad",
    )(inputs, w_in.transpose(1, 0, 2), conv_taps, pole_rates.T, residues.T, cotangent)


def solution(mesh):
    in_specs = (
        P("ctx", "tp"),
        P(None, None, "tp"),
        P(None, None, "tp"),
        P("tp", None),
        P("tp", None),
        P("ctx", "tp"),
    )
    out_specs = P("ctx", "tp")
    step = functools.partial(body, mesh.shape["ctx"], mesh.shape["tp"])
    return jax.shard_map(step, mesh=mesh, in_specs=in_specs, out_specs=out_specs, check_vma=False)
```

```python
import functools

import jax
import jax.numpy as jnp
from jax import lax
from jax.experimental import pallas as pl
from jax.experimental.pallas import tpu as pltpu
from jax.sharding import PartitionSpec as P

MESH = pl.DeviceIdType.MESH
F32 = jnp.float32
BF16 = jnp.bfloat16
SUB = 8
LANES = 128
PIECES = 2
COLUMNS = 2


def one_minus_exp(x):
    series = jnp.ones_like(x)
    for k in range(9, 1, -1):
        series = 1.0 - x * series * (1.0 / k)
    return jnp.where(x < 0.25, x * series, 1.0 - jnp.exp(-x))


def kernel(
    n_ctx,
    n_tp,
    x_hbm,
    w_hbm,
    taps_hbm,
    rate_hbm,
    res_hbm,
    cot_hbm,
    out,
    w,
    xg,
    taps,
    rate,
    res,
    cot,
    proj,
    gate,
    keyp,
    valp,
    mixp,
    glp,
    fwd_pow,
    rev_pow,
    kern,
    kern_late,
    spread,
    gain,
    w_fwd,
    w_bwd,
    part,
    ends,
    state,
    state_in,
    gfp,
    sliding,
    long_out,
    grad_mix,
    gp,
    ready,
    rs_out,
    rs_in,
    x_out,
    x_in,
    far_out,
    far_in,
    local_sem,
    w_sem,
    g_send,
    g_recv,
    s_send,
    s_recv,
    met,
    r_send,
    r_recv,
):
    rows, chans = x_hbm.shape
    poles = rate_hbm.shape[0]
    ring = n_tp // COLUMNS
    hops = ring // 2 - 1
    streams = ((0, 1), (0, -1), (1, 1), (1, -1))
    mine, theirs = (0, 1), (2, 3)
    ctx = lax.axis_index("ctx")
    tp = lax.axis_index("tp")
    col, z = tp // ring, tp % ring

    def at_z(column, zz):
        return column * ring + (zz + 2 * ring) % ring

    def column_of(c):
        return col if c == 0 else 1 - col

    partner = at_z(1 - col, z)

    rounds = n_ctx.bit_length() - 1

    def across(r):
        bit = (ctx // 2**r) % 2
        return ctx + 2**r * (1 - 2 * bit)

    barrier = pltpu.get_barrier_semaphore()
    others = [at_z(col, z + 1), at_z(col, z - 1), partner]
    for other in others:
        pl.semaphore_signal(barrier, inc=1, device_id=(ctx, other), device_id_type=MESH)
    for r in range(rounds):
        pl.semaphore_signal(barrier, inc=1, device_id=(across(r), tp), device_id_type=MESH)

    def greet(r):
        if r < rounds:
            pl.semaphore_signal(met.at[r], inc=1, device_id=(across(r), tp), device_id_type=MESH)

    def greeted(r):
        if r < rounds:
            pl.semaphore_wait(met.at[r], 1)

    w_copies = [pltpu.make_async_copy(w_hbm.at[j], w.at[j], w_sem.at[j]) for j in range(3)]
    small = [
        pltpu.make_async_copy(src, dst, local_sem.at[i])
        for i, (src, dst) in enumerate(
            ((x_hbm, xg.at[tp]), (taps_hbm, taps), (rate_hbm, rate), (res_hbm, res), (cot_hbm, cot))
        )
    ]
    pl.semaphore_wait(barrier, len(others) + rounds)

    def remote(src, dst, send, recv, device):
        return pltpu.make_async_remote_copy(
            src_ref=src, dst_ref=dst, send_sem=send, recv_sem=recv, device_id=device, device_id_type=MESH
        )

    size = rows // PIECES

    def piece(p):
        return pl.ds(p * size, size)

    def halves(k):
        return (0, 1) if streams[k][1] > 0 else (1, 0)

    def g_copy(k, s, p):
        c, d = streams[k]
        skip = 2 if s > hops else 1
        held, there = at_z(column_of(c), z - (s - skip) * d), at_z(col, z + skip * d)
        if c == 1 and s == 1:
            held, there = at_z(col, z - d), partner
        if c == 1 and s == 2:
            held, there = at_z(col, z - d), at_z(1 - col, z + d)
        block = xg.at[held, piece(p)]
        src = x_hbm.at[piece(p)] if c == 0 and s == 1 else block
        return remote(src, block, g_send.at[k, s, p], g_recv.at[k, s, p], (ctx, there))

    def arrived(k, s, p):
        here = xg.at[at_z(column_of(streams[k][0]), z - s * streams[k][1]), piece(p)]
        remote(here, here, g_send.at[k, s, p], g_recv.at[k, s, p], (ctx, partner)).wait_recv()

    x_pair = remote(x_hbm, xg.at[tp], g_send.at[4, 0, 0], g_recv.at[4, 0, 0], (ctx, partner))

    def forward(k, s, i):
        p = halves(k)[i]
        arrived(k, s, p)
        if s == hops - 1 and i == 0:
            g_copy(k, hops + 1, p).start()
        if s < hops:
            g_copy(k, s + 1, p).start()

    def block_at(k, distance):
        c, d = streams[k]
        return at_z(column_of(c), z + distance * d)

    for i in range(PIECES):
        for k in mine:
            g_copy(k, 1, halves(k)[i]).start()
    x_pair.start()
    for c in small + w_copies:
        c.start()
    greet(0)

    for c in small[1:]:
        c.wait()

    rates = rate[...]
    gain[...] = jnp.sqrt(one_minus_exp(2.0 * rates))
    kern[...] = jnp.zeros_like(kern)
    steps = lax.broadcasted_iota(jnp.int32, (rows, chans), 0).astype(F32)
    state_in[ctx, 0:poles] = jnp.zeros((poles, chans), BF16)

    def tables(n, _):
        r = rate[pl.ds(n, 1), :]
        up = jnp.exp(-r * steps)
        fwd_pow[n] = up
        rev_pow[n] = jnp.exp(-r * (rows - 1.0 - steps))
        kern[...] += up * (res[pl.ds(n, 1), :] * gain[pl.ds(n, 1), :])
        return 0

    def state_weights(i, _):
        gap = (jnp.abs(ctx - i) - 1) * rows
        weight = jnp.exp(-rate[...] * gap.astype(F32))
        w_fwd[i] = jnp.where(i < ctx, weight, 0.0)
        w_bwd[i] = jnp.where(i > ctx, weight, 0.0)
        return 0

    def project(slots):
        for j in range(3):
            total = proj[j, SUB:, :]
            for slot in slots:
                start = pl.multiple_of(slot * chans, chans)
                total += jnp.dot(xg[slot], w[j, pl.ds(start, chans), :], preferred_element_type=F32)
            proj[j, SUB:, :] = total

    proj[...] = jnp.zeros_like(proj)
    def all_tables(part):
        first_poles, first_ctx = poles * 4 // 16, n_ctx * 4 // 16
        lax.fori_loop(*((0, first_poles), (first_poles, poles))[part], tables, 0)
        lax.fori_loop(*((0, first_ctx), (first_ctx, n_ctx))[part], state_weights, 0)

    all_tables(0)
    for i in range(PIECES):
        for k in mine:
            forward(k, 1, i)
        for k in mine:
            g_copy(k + 2, 2, halves(k)[i]).start()
    for i in range(PIECES):
        for k in theirs:
            g_copy(k, 1, halves(k)[i]).start()
    small[0].wait()
    for c in w_copies:
        c.wait()
    project([tp] + [block_at(k, -1) for k in mine])
    greeted(0)
    greet(1)
    for s in range(2, hops):
        for group in (mine, theirs):
            for i in range(PIECES):
                for k in group:
                    forward(k, s, i)
        project([block_at(k, -s) for k in range(4)])
        greeted(s - 1)
        greet(s)
    all_tables(1)
    def spread_rows(i, _):
        block = kern[pl.ds(pl.multiple_of(SUB * i, SUB), SUB), :]
        for r in range(SUB):
            spread[SUB * i + r] = jnp.broadcast_to(block[r : r + 1, :], (SUB, chans))
        return 0

    lax.fori_loop(0, rows // SUB, spread_rows, 0)
    kern_late[0:1, :] = jnp.zeros((1, chans), F32)
    kern_late[1:rows, :] = kern[0 : rows - 1, :]

    x_pair.wait_recv()
    for k in mine:
        for i in range(PIECES):
            forward(k, hops, i)
    project([block_at(k, -hops) for k in mine] + [partner])
    greeted(hops - 1)
    greet(hops)
    for k in theirs:
        for i in range(PIECES):
            arrived(k, 1, halves(k)[i])
    for k in mine:
        arrived(k, hops + 1, halves(k)[0])
    project([block_at(k, -1) for k in theirs] + [block_at(0, hops + 1)])
    for k in theirs:
        for i in range(PIECES):
            forward(k, hops, i)
        arrived(k, hops + 1, halves(k)[0])
    project([block_at(k, -hops) for k in theirs] + [block_at(2, hops + 1)])

    for j in range(3):
        proj[j, SUB:, :] = proj[j, SUB:, :].astype(BF16).astype(F32)
    edge = [proj[j, SUB : SUB + 1, :] for j in range(3)] + [cot[0:16, :].astype(F32)[0:1]]
    edge += [proj[j, SUB + 1 : SUB + 2, :] for j in range(3)] + [cot[0:16, :].astype(F32)[1:2]]
    blank = jnp.zeros((1, chans), F32)
    edge += [proj[j, SUB + rows - 2 : SUB + rows - 1, :] for j in range(3)] + [blank]
    edge += [proj[j, SUB + rows - 1 : SUB + rows, :] for j in range(3)] + [blank]
    edge = jnp.concatenate(edge, axis=0).astype(BF16)
    for target in (state.at[0], state.at[1], state_in.at[ctx]):
        target[poles:, :] = edge

    filtered = []
    for j in range(3):
        acc = taps[0, j : j + 1, :] * proj[j, SUB : SUB + rows, :]
        acc += taps[1, j : j + 1, :] * proj[j, SUB - 1 : SUB + rows - 1, :]
        acc += taps[2, j : j + 1, :] * proj[j, SUB - 2 : SUB + rows - 2, :]
        filtered.append(acc)
    keyp[...] = filtered[1]
    valp[...] = filtered[2]
    mixp[0:SUB, :] = jnp.zeros((SUB, chans), F32)
    mixp[SUB:, :] = jnp.where(steps >= 2.0, filtered[1] * filtered[2], 0.0)
    glp[0:rows, :] = jnp.where(steps >= 2.0, cot[...].astype(F32) * filtered[0], 0.0)
    glp[rows : rows + SUB, :] = jnp.zeros((SUB, chans), F32)

    for lane in range(0, chans, LANES):
        cols = slice(lane, lane + LANES)
        mix_now, gl_now = mixp[SUB:, cols], glp[0:rows, cols]

        def partial_states(n, _, cols=cols, mix_now=mix_now, gl_now=gl_now):
            fwd = rev_pow[n, :, cols] * mix_now
            bwd = fwd_pow[n, :, cols] * gl_now
            part[0, n, :, cols] = jnp.sum(fwd.reshape(rows // SUB, SUB, LANES), axis=0)
            part[1, n, :, cols] = jnp.sum(bwd.reshape(rows // SUB, SUB, LANES), axis=0)
            return 0

        lax.fori_loop(0, poles, partial_states, 0, unroll=2)
    ends[0] = gain[...] * jnp.sum(part[0], axis=1)
    ends[1] = jnp.sum(part[1], axis=1)
    state[0, 0:poles, :] = ends[0].astype(BF16)
    state[1, 0:poles, :] = ends[1].astype(BF16)

    greeted(hops)
    for r in range(hops + 1, rounds):
        greet(r)
        greeted(r)

    def s_copy(o):
        other = ctx
        for r in range(rounds):
            if o >> r & 1:
                other = other + across(r) - ctx
        which = (other < ctx).astype(jnp.int32)
        return remote(state.at[which], state_in.at[ctx], s_send.at[o], s_recv.at[o], (other, tp))

    for o in range(n_ctx - 1, 0, -1):
        s_copy(o).start()

    tiles = rows // SUB

    def local_conv(which, flip, store):
        for lane in range(0, chans, LANES):
            cols = slice(lane, lane + LANES)

            def tap(r, acc, cols=cols):
                acc = list(acc)
                block = [sliding[which, r, SUB * i : SUB * i + SUB, cols] for i in range(tiles)]
                for m in range(tiles):
                    k = spread[SUB * m + r, :, cols]
                    for i in range(tiles - m):
                        if flip:
                            acc[i + m] = acc[i + m] + k * block[i]
                        else:
                            acc[i] = acc[i] + k * block[i + m]
                return tuple(acc)

            acc = lax.fori_loop(0, SUB, tap, (jnp.zeros((SUB, LANES), F32),) * tiles)
            for i in range(tiles):
                store[SUB * i : SUB * i + SUB, cols] = acc[i]

    for r in range(SUB):
        sliding[0, r] = mixp[SUB - r : SUB - r + rows, :]
        sliding[1, r] = glp[r : r + rows, :]
    local_conv(0, True, long_out)
    local_conv(1, False, grad_mix)

    for o in range(1, n_ctx):
        s_copy(o).wait()

    branch_row = lax.broadcasted_iota(jnp.int32, (SUB, chans), 0)
    upper = branch_row < 4
    tap_rows = [jnp.concatenate([taps[i], blank, taps[i], blank], axis=0) for i in range(3)]

    def first_rows(i):
        here = state_in[i, poles:, :].astype(F32)[0:SUB]
        before = state_in[jnp.maximum(i - 1, 0), poles:, :].astype(F32)[SUB:]
        before = jnp.where(i > 0, before, 0.0)
        shifted = jnp.where(upper, pltpu.roll(before, 4, 0), pltpu.roll(here, 4, 0))
        full = tap_rows[0] * here + tap_rows[1] * shifted + tap_rows[2] * before
        return [(here[r + 3 : r + 4], full[r : r + 1], full[r + 1 : r + 2], full[r + 2 : r + 3]) for r in (0, 4)]

    decay = jnp.exp(-rates)
    gained = [gain[...] * jnp.exp(-rates * (rows - 1.0)), gain[...] * jnp.exp(-rates * (rows - 2.0))]
    none = jnp.zeros((poles, chans), F32)

    def add_before(i, total):
        (_, _, k0, v0), (_, _, k1, v1) = first_rows(i)
        end = state_in[i, 0:poles, :].astype(F32) + gained[0] * (k0 * v0) + gained[1] * (k1 * v1)
        return total + w_fwd[i] * end

    def add_after(i, total):
        (c0, g0, _, _), (c1, g1, _, _) = first_rows(i)
        return total + w_bwd[i] * (state_in[i, 0:poles, :].astype(F32) + c0 * g0 + decay * (c1 * g1))

    before = lax.fori_loop(0, ctx, add_before, none)
    after = lax.fori_loop(ctx + 1, n_ctx, add_after, none)
    out_gain = res[...] * gain[...]
    part[0, :, 0, :] = res[...] * decay * before
    part[1, :, 0, :] = out_gain * decay * after

    (c0, g0, k0, v0), (c1, g1, k1, v1) = first_rows(ctx)
    keyp[0:1, :], valp[0:1, :], keyp[1:2, :], valp[1:2, :] = k0, v0, k1, v1
    mix0, mix1, gl0, gl1 = k0 * v0, k1 * v1, c0 * g0, c1 * g1
    taps0, taps1 = kern[0:1, :], kern[1:2, :]
    grad_mix[0:1, :] += taps0 * gl0 + taps1 * gl1
    grad_mix[1:2, :] += taps0 * gl1
    leaving = jnp.exp(-rates * float(rows)) * before + ends[0] + gained[0] * mix0 + gained[1] * mix1
    (c0, g0, k0, v0), (c1, g1, k1, v1) = first_rows(jnp.minimum(ctx + 1, n_ctx - 1))
    leaving = res[...] * decay * leaving
    out0 = jnp.sum(leaving, axis=0, keepdims=True) + taps0 * (k0 * v0)
    out1 = jnp.sum(leaving * decay, axis=0, keepdims=True) + taps1 * (k0 * v0) + taps0 * (k1 * v1)
    adj0 = jnp.sum(out_gain * after, axis=0, keepdims=True)
    adj1 = jnp.sum(out_gain * jnp.exp(rates) * (after - c0 * g0), axis=0, keepdims=True)
    for j, pair in enumerate(((c0 * out0, c1 * out1), (adj0 * v0, adj1 * v1), (adj0 * k0, adj1 * k1))):
        for r in range(2):
            gfp[j, rows + r : rows + r + 1, :] = jnp.where(ctx < n_ctx - 1, pair[r], 0.0)

    def add_fwd(p, acc):
        return acc + fwd_pow[p] * part[0, p, 0:1, :]

    def add_bwd(p, acc):
        return acc + rev_pow[p] * part[1, p, 0:1, :]

    whole = lax.fori_loop(0, poles, add_fwd, long_out[...] + kern[...] * mix0 + kern_late[...] * mix1)
    gfp[0, 0:rows, :] = cot[...].astype(F32) * whole
    whole = lax.fori_loop(0, poles, add_bwd, grad_mix[...])
    gfp[1, 0:rows, :] = whole * valp[...]
    gfp[2, 0:rows, :] = whole * keyp[...]
    for j in range(3):
        acc = taps[0, j : j + 1, :] * gfp[j, 0:rows, :]
        acc += taps[1, j : j + 1, :] * gfp[j, 1 : rows + 1, :]
        acc += taps[2, j : j + 1, :] * gfp[j, 2 : rows + 2, :]
        gp[j] = acc.astype(BF16)

    def partial_of(slot):
        start = pl.multiple_of(slot * chans, chans)
        total = jnp.zeros((rows, chans), F32)
        for j in range(3):
            total += lax.dot_general(
                gp[j], w[j, pl.ds(start, chans), :], (((1,), (1,)), ((), ())), preferred_element_type=F32
            )
        return total

    def r_copy(k, s, p):
        c, d = streams[k]
        there = at_z(col, z + d)
        if c == 1 and s == hops - 1:
            there = at_z(1 - col, z + d)
        if c == 1 and s == hops:
            there = partner
        at = (k, s, piece(p))
        return remote(rs_out.at[at], rs_in.at[at], r_send.at[k, s, p], r_recv.at[k, s, p], (ctx, there))

    far_pair = remote(far_out.at[0], far_in.at[0], r_send.at[4, 1, 0], r_recv.at[4, 1, 0], (ctx, partner))
    far_sum = remote(far_out.at[1], far_in.at[1], r_send.at[4, 2, 0], r_recv.at[4, 2, 0], (ctx, at_z(col, z + hops + 1)))

    swap = remote(x_out, x_in, r_send.at[4, 0, 0], r_recv.at[4, 0, 0], (ctx, partner))

    for group, s, distance in ((theirs, 1, hops), (mine, 1, hops), (theirs, hops, 1)):
        if s == hops:
            far_out[0] = partial_of(block_at(theirs[0], hops + 1)).astype(BF16)
            far_pair.start()
        for k in group:
            rs_out[k, s] = partial_of(block_at(k, distance)).astype(BF16)
        for i in range(PIECES):
            for k in group:
                r_copy(k, s, halves(k)[i]).start()
    x_out[...] = partial_of(partner).astype(BF16)
    swap.start()

    for s in range(2, hops):
        for k in range(4):
            ready[k] = partial_of(block_at(k, hops + 1 - s))
        for group in (theirs, mine):
            for i in range(PIECES):
                for k in group:
                    p = halves(k)[i]
                    at = piece(p)
                    total = ready[k, at]
                    r_copy(k, s - 1, p).wait_recv()
                    rs_out[k, s, at] = (total + rs_in[k, s - 1, at].astype(F32)).astype(BF16)
                    r_copy(k, s, p).start()

    ready[2] = partial_of(block_at(0, hops + 1))
    for k in mine:
        ready[k] = partial_of(block_at(k, 1))
    far_pair.wait_recv()
    far_out[1] = (ready[2] + far_in[0].astype(F32)).astype(BF16)
    far_sum.start()
    for i in range(PIECES):
        for k in mine:
            p = halves(k)[i]
            at = piece(p)
            total = ready[k, at]
            for other, step in ((k + 2, hops), (k, hops - 1), (k + 2, hops - 1)):
                r_copy(other, step, p).wait_recv()
                total += rs_in[other, step, at].astype(F32)
            rs_out[k, hops, at] = total.astype(BF16)
            r_copy(k, hops, p).start()

    long_out[...] = partial_of(tp)
    swap.wait_recv()
    long_out[...] += x_in[...].astype(F32)
    far_sum.wait_recv()
    long_out[...] += far_in[1].astype(F32)
    for p in range(PIECES):
        at = piece(p)
        total = long_out[at]
        for k in mine:
            r_copy(k, hops, p).wait_recv()
            total += rs_in[k, hops, at].astype(F32)
        out[at] = total.astype(BF16)

    swap.wait_send()
    x_pair.wait_send()
    far_pair.wait_send()
    far_sum.wait_send()
    for k in range(4):
        g_copy(k, hops + 1, halves(k)[0]).wait_send()
        for p in range(PIECES):
            for s in range(1, hops + 1):
                g_copy(k, s, p).wait_send()
                r_copy(k, s, p).wait_send()


def body(n_ctx, n_tp, inputs, w_in, conv_taps, pole_rates, residues, cotangent):
    rows, chans = inputs.shape
    width = w_in.shape[0]
    poles = pole_rates.shape[1]
    steps = n_tp // COLUMNS // 2 + 1
    vmem = pltpu.VMEM
    dma = pltpu.SemaphoreType.DMA
    scratch = [
        vmem((3, width, chans), BF16),
        vmem((n_tp, rows, chans), BF16),
        vmem((3, 3, chans), F32),
        vmem((poles, chans), F32),
        vmem((poles, chans), F32),
        vmem((rows, chans), BF16),
        vmem((3, rows + SUB, chans), F32),
        vmem((rows, chans), F32),
        vmem((rows, chans), F32),
        vmem((rows, chans), F32),
        vmem((rows + SUB, chans), F32),
        vmem((rows + SUB, chans), F32),
        vmem((poles, rows, chans), F32),
        vmem((poles, rows, chans), F32),
        vmem((rows, chans), F32),
        vmem((rows, chans), F32),
        vmem((rows, SUB, chans), F32),
        vmem((poles, chans), F32),
        vmem((n_ctx, poles, chans), F32),
        vmem((n_ctx, poles, chans), F32),
        vmem((2, poles, SUB, chans), F32),
        vmem((2, poles, chans), F32),
        vmem((2, poles + 2 * SUB, chans), BF16),
        vmem((n_ctx, poles + 2 * SUB, chans), BF16),
        vmem((3, rows + SUB, chans), F32),
        vmem((2, SUB, rows, chans), F32),
        vmem((rows, chans), F32),
        vmem((rows, chans), F32),
        vmem((3, rows, chans), BF16),
        vmem((4, rows, chans), F32),
        vmem((4, steps - 1, rows, chans), BF16),
        vmem((4, steps - 1, rows, chans), BF16),
        vmem((rows, chans), BF16),
        vmem((rows, chans), BF16),
        vmem((2, rows, chans), BF16),
        vmem((2, rows, chans), BF16),
        dma((5,)),
        dma((3,)),
        dma((5, steps, PIECES)),
        dma((5, steps, PIECES)),
        dma((n_ctx,)),
        dma((n_ctx,)),
        pltpu.SemaphoreType.REGULAR((n_ctx.bit_length(),)),
        dma((5, steps - 1, PIECES)),
        dma((5, steps - 1, PIECES)),
    ]
    return pl.pallas_call(
        functools.partial(kernel, n_ctx, n_tp),
        out_shape=pltpu.VMEM((rows, chans), BF16),
        in_specs=[pl.BlockSpec(memory_space=pl.ANY)] * 6,
        out_specs=pl.BlockSpec(memory_space=pltpu.VMEM),
        scratch_shapes=scratch,
        compiler_params=pltpu.CompilerParams(
            collective_id=0, has_side_effects=True, vmem_limit_bytes=60 * 1024 * 1024
        ),
        cost_estimate=pl.CostEstimate(
            flops=4 * rows * width * 3 * chans, bytes_accessed=2 * 3 * width * chans, transcendentals=0
        ),
        name="hyena_input_grad",
    )(inputs, w_in.transpose(1, 0, 2), conv_taps, pole_rates.T, residues.T, cotangent)


def solution(mesh):
    in_specs = (
        P("ctx", "tp"),
        P(None, None, "tp"),
        P(None, None, "tp"),
        P("tp", None),
        P("tp", None),
        P("ctx", "tp"),
    )
    out_specs = P("ctx", "tp")
    step = functools.partial(body, mesh.shape["ctx"], mesh.shape["tp"])
    return jax.shard_map(step, mesh=mesh, in_specs=in_specs, out_specs=out_specs, check_vma=False)
```

```python
import functools

import jax
import jax.numpy as jnp
from jax import lax
from jax.experimental import pallas as pl
from jax.experimental.pallas import tpu as pltpu
from jax.sharding import PartitionSpec as P

MESH = pl.DeviceIdType.MESH
F32 = jnp.float32
BF16 = jnp.bfloat16
SUB = 8
LANES = 128
PIECES = 2
COLUMNS = 2


def one_minus_exp(x):
    series = jnp.ones_like(x)
    for k in range(9, 1, -1):
        series = 1.0 - x * series * (1.0 / k)
    return jnp.where(x < 0.25, x * series, 1.0 - jnp.exp(-x))


def kernel(
    n_ctx,
    n_tp,
    x_hbm,
    w_hbm,
    taps_hbm,
    rate_hbm,
    res_hbm,
    cot_hbm,
    out,
    w,
    xg,
    taps,
    rate,
    res,
    cot,
    proj,
    gate,
    keyp,
    valp,
    mixp,
    glp,
    fwd_pow,
    rev_pow,
    kern,
    kern_late,
    spread,
    gain,
    w_fwd,
    w_bwd,
    part,
    ends,
    state,
    state_in,
    gfp,
    sliding,
    long_out,
    grad_mix,
    gp,
    ready,
    rs_out,
    rs_in,
    x_out,
    x_in,
    far_out,
    far_in,
    local_sem,
    w_sem,
    g_send,
    g_recv,
    s_send,
    s_recv,
    met,
    r_send,
    r_recv,
):
    rows, chans = x_hbm.shape
    poles = rate_hbm.shape[0]
    ring = n_tp // COLUMNS
    hops = ring // 2 - 1
    streams = ((0, 1), (0, -1), (1, 1), (1, -1))
    mine, theirs = (0, 1), (2, 3)
    ctx = lax.axis_index("ctx")
    tp = lax.axis_index("tp")
    col, z = tp // ring, tp % ring

    def at_z(column, zz):
        return column * ring + (zz + 2 * ring) % ring

    def column_of(c):
        return col if c == 0 else 1 - col

    partner = at_z(1 - col, z)

    rounds = n_ctx.bit_length() - 1

    def across(r):
        bit = (ctx // 2**r) % 2
        return ctx + 2**r * (1 - 2 * bit)

    barrier = pltpu.get_barrier_semaphore()
    others = [at_z(col, z + 1), at_z(col, z - 1), partner]
    for other in others:
        pl.semaphore_signal(barrier, inc=1, device_id=(ctx, other), device_id_type=MESH)
    for r in range(rounds):
        pl.semaphore_signal(barrier, inc=1, device_id=(across(r), tp), device_id_type=MESH)

    def greet(r):
        if r < rounds:
            pl.semaphore_signal(met.at[r], inc=1, device_id=(across(r), tp), device_id_type=MESH)

    def greeted(r):
        if r < rounds:
            pl.semaphore_wait(met.at[r], 1)

    w_copies = [pltpu.make_async_copy(w_hbm.at[j], w.at[j], w_sem.at[j]) for j in range(3)]
    small = [
        pltpu.make_async_copy(src, dst, local_sem.at[i])
        for i, (src, dst) in enumerate(
            ((x_hbm, xg.at[tp]), (taps_hbm, taps), (rate_hbm, rate), (res_hbm, res), (cot_hbm, cot))
        )
    ]
    pl.semaphore_wait(barrier, len(others) + rounds)

    def remote(src, dst, send, recv, device):
        return pltpu.make_async_remote_copy(
            src_ref=src, dst_ref=dst, send_sem=send, recv_sem=recv, device_id=device, device_id_type=MESH
        )

    size = rows // PIECES

    def piece(p):
        return pl.ds(p * size, size)

    def halves(k):
        return (0, 1) if streams[k][1] > 0 else (1, 0)

    def g_copy(k, s, p):
        c, d = streams[k]
        skip = 2 if s > hops else 1
        held, there = at_z(column_of(c), z - (s - skip) * d), at_z(col, z + skip * d)
        if c == 1 and s == 1:
            held, there = at_z(col, z - d), partner
        if c == 1 and s == 2:
            held, there = at_z(col, z - d), at_z(1 - col, z + d)
        block = xg.at[held, piece(p)]
        src = x_hbm.at[piece(p)] if c == 0 and s == 1 else block
        return remote(src, block, g_send.at[k, s, p], g_recv.at[k, s, p], (ctx, there))

    def arrived(k, s, p):
        here = xg.at[at_z(column_of(streams[k][0]), z - s * streams[k][1]), piece(p)]
        remote(here, here, g_send.at[k, s, p], g_recv.at[k, s, p], (ctx, partner)).wait_recv()

    x_pair = remote(x_hbm, xg.at[tp], g_send.at[4, 0, 0], g_recv.at[4, 0, 0], (ctx, partner))

    def forward(k, s, i):
        p = halves(k)[i]
        arrived(k, s, p)
        if s == hops - 1 and i == 0:
            g_copy(k, hops + 1, p).start()
        if s < hops:
            g_copy(k, s + 1, p).start()

    def block_at(k, distance):
        c, d = streams[k]
        return at_z(column_of(c), z + distance * d)

    for i in range(PIECES):
        for k in mine:
            g_copy(k, 1, halves(k)[i]).start()
    x_pair.start()
    for c in small + w_copies:
        c.start()
    greet(0)

    for c in small[1:]:
        c.wait()

    rates = rate[...]
    gain[...] = jnp.sqrt(one_minus_exp(2.0 * rates))
    kern[...] = jnp.zeros_like(kern)
    steps = lax.broadcasted_iota(jnp.int32, (rows, chans), 0).astype(F32)
    state_in[ctx, 0:poles] = jnp.zeros((poles, chans), BF16)

    def tables(n, _):
        r = rate[pl.ds(n, 1), :]
        up = jnp.exp(-r * steps)
        fwd_pow[n] = up
        rev_pow[n] = jnp.exp(-r * (rows - 1.0 - steps))
        kern[...] += up * (res[pl.ds(n, 1), :] * gain[pl.ds(n, 1), :])
        return 0

    def state_weights(i, _):
        gap = (jnp.abs(ctx - i) - 1) * rows
        weight = jnp.exp(-rate[...] * gap.astype(F32))
        w_fwd[i] = jnp.where(i < ctx, weight, 0.0)
        w_bwd[i] = jnp.where(i > ctx, weight, 0.0)
        return 0

    def project(slots):
        for j in range(3):
            total = proj[j, SUB:, :]
            for slot in slots:
                start = pl.multiple_of(slot * chans, chans)
                total += jnp.dot(xg[slot], w[j, pl.ds(start, chans), :], preferred_element_type=F32)
            proj[j, SUB:, :] = total

    proj[...] = jnp.zeros_like(proj)
    def all_tables(part):
        first_poles, first_ctx = poles * 4 // 16, n_ctx * 4 // 16
        lax.fori_loop(*((0, first_poles), (first_poles, poles))[part], tables, 0)
        lax.fori_loop(*((0, first_ctx), (first_ctx, n_ctx))[part], state_weights, 0)

    all_tables(0)
    for i in range(PIECES):
        for k in mine:
            forward(k, 1, i)
        for k in mine:
            g_copy(k + 2, 2, halves(k)[i]).start()
    for i in range(PIECES):
        for k in theirs:
            g_copy(k, 1, halves(k)[i]).start()
    small[0].wait()
    for c in w_copies:
        c.wait()
    project([tp] + [block_at(k, -1) for k in mine])
    greeted(0)
    greet(1)
    for s in range(2, hops):
        for group in (mine, theirs):
            for i in range(PIECES):
                for k in group:
                    forward(k, s, i)
        project([block_at(k, -s) for k in range(4)])
        greeted(s - 1)
        greet(s)
    all_tables(1)
    def spread_rows(i, _):
        block = kern[pl.ds(pl.multiple_of(SUB * i, SUB), SUB), :]
        for r in range(SUB):
            spread[SUB * i + r] = jnp.broadcast_to(block[r : r + 1, :], (SUB, chans))
        return 0

    lax.fori_loop(0, rows // SUB, spread_rows, 0)
    kern_late[0:1, :] = jnp.zeros((1, chans), F32)
    kern_late[1:rows, :] = kern[0 : rows - 1, :]

    x_pair.wait_recv()
    for k in mine:
        for i in range(PIECES):
            forward(k, hops, i)
    project([block_at(k, -hops) for k in mine] + [partner])
    greeted(hops - 1)
    greet(hops)
    for k in theirs:
        for i in range(PIECES):
            arrived(k, 1, halves(k)[i])
    for k in mine:
        arrived(k, hops + 1, halves(k)[0])
    project([block_at(k, -1) for k in theirs] + [block_at(0, hops + 1)])
    for k in theirs:
        for i in range(PIECES):
            forward(k, hops, i)
        arrived(k, hops + 1, halves(k)[0])
    project([block_at(k, -hops) for k in theirs] + [block_at(2, hops + 1)])

    for j in range(3):
        proj[j, SUB:, :] = proj[j, SUB:, :].astype(BF16).astype(F32)
    edge = [proj[j, SUB : SUB + 1, :] for j in range(3)] + [cot[0:16, :].astype(F32)[0:1]]
    edge += [proj[j, SUB + 1 : SUB + 2, :] for j in range(3)] + [cot[0:16, :].astype(F32)[1:2]]
    blank = jnp.zeros((1, chans), F32)
    edge += [proj[j, SUB + rows - 2 : SUB + rows - 1, :] for j in range(3)] + [blank]
    edge += [proj[j, SUB + rows - 1 : SUB + rows, :] for j in range(3)] + [blank]
    edge = jnp.concatenate(edge, axis=0).astype(BF16)
    for target in (state.at[0], state.at[1], state_in.at[ctx]):
        target[poles:, :] = edge

    filtered = []
    for j in range(3):
        acc = taps[0, j : j + 1, :] * proj[j, SUB : SUB + rows, :]
        acc += taps[1, j : j + 1, :] * proj[j, SUB - 1 : SUB + rows - 1, :]
        acc += taps[2, j : j + 1, :] * proj[j, SUB - 2 : SUB + rows - 2, :]
        filtered.append(acc)
    keyp[...] = filtered[1]
    valp[...] = filtered[2]
    mixp[0:SUB, :] = jnp.zeros((SUB, chans), F32)
    mixp[SUB:, :] = jnp.where(steps >= 2.0, filtered[1] * filtered[2], 0.0)
    glp[0:rows, :] = jnp.where(steps >= 2.0, cot[...].astype(F32) * filtered[0], 0.0)
    glp[rows : rows + SUB, :] = jnp.zeros((SUB, chans), F32)

    for lane in range(0, chans, LANES):
        cols = slice(lane, lane + LANES)
        mix_now, gl_now = mixp[SUB:, cols], glp[0:rows, cols]

        def partial_states(n, _, cols=cols, mix_now=mix_now, gl_now=gl_now):
            fwd = rev_pow[n, :, cols] * mix_now
            bwd = fwd_pow[n, :, cols] * gl_now
            part[0, n, :, cols] = jnp.sum(fwd.reshape(rows // SUB, SUB, LANES), axis=0)
            part[1, n, :, cols] = jnp.sum(bwd.reshape(rows // SUB, SUB, LANES), axis=0)
            return 0

        lax.fori_loop(0, poles, partial_states, 0, unroll=2)
    ends[0] = gain[...] * jnp.sum(part[0], axis=1)
    ends[1] = jnp.sum(part[1], axis=1)
    state[0, 0:poles, :] = ends[0].astype(BF16)
    state[1, 0:poles, :] = ends[1].astype(BF16)

    greeted(hops)
    for r in range(hops + 1, rounds):
        greet(r)
        greeted(r)

    def s_copy(o):
        other = ctx
        for r in range(rounds):
            if o >> r & 1:
                other = other + across(r) - ctx
        which = (other < ctx).astype(jnp.int32)
        return remote(state.at[which], state_in.at[ctx], s_send.at[o], s_recv.at[o], (other, tp))

    for o in range(n_ctx - 1, 0, -1):
        s_copy(o).start()

    tiles = rows // SUB

    def local_conv(which, flip, store):
        for lane in range(0, chans, LANES):
            cols = slice(lane, lane + LANES)

            def tap(r, acc, cols=cols):
                acc = list(acc)
                block = [sliding[which, r, SUB * i : SUB * i + SUB, cols] for i in range(tiles)]
                for m in range(tiles):
                    k = spread[SUB * m + r, :, cols]
                    for i in range(tiles - m):
                        if flip:
                            acc[i + m] = acc[i + m] + k * block[i]
                        else:
                            acc[i] = acc[i] + k * block[i + m]
                return tuple(acc)

            acc = lax.fori_loop(0, SUB, tap, (jnp.zeros((SUB, LANES), F32),) * tiles)
            for i in range(tiles):
                store[SUB * i : SUB * i + SUB, cols] = acc[i]

    for r in range(SUB):
        sliding[0, r] = mixp[SUB - r : SUB - r + rows, :]
        sliding[1, r] = glp[r : r + rows, :]
    local_conv(0, True, long_out)
    local_conv(1, False, grad_mix)

    for o in range(1, n_ctx):
        s_copy(o).wait()

    branch_row = lax.broadcasted_iota(jnp.int32, (SUB, chans), 0)
    upper = branch_row < 4
    tap_rows = [jnp.concatenate([taps[i], blank, taps[i], blank], axis=0) for i in range(3)]

    def first_rows(i):
        here = state_in[i, poles:, :].astype(F32)[0:SUB]
        before = state_in[jnp.maximum(i - 1, 0), poles:, :].astype(F32)[SUB:]
        before = jnp.where(i > 0, before, 0.0)
        shifted = jnp.where(upper, pltpu.roll(before, 4, 0), pltpu.roll(here, 4, 0))
        full = tap_rows[0] * here + tap_rows[1] * shifted + tap_rows[2] * before
        return [(here[r + 3 : r + 4], full[r : r + 1], full[r + 1 : r + 2], full[r + 2 : r + 3]) for r in (0, 4)]

    decay = jnp.exp(-rates)
    gained = [gain[...] * jnp.exp(-rates * (rows - 1.0)), gain[...] * jnp.exp(-rates * (rows - 2.0))]
    none = jnp.zeros((poles, chans), F32)

    def add_before(i, total):
        (_, _, k0, v0), (_, _, k1, v1) = first_rows(i)
        end = state_in[i, 0:poles, :].astype(F32) + gained[0] * (k0 * v0) + gained[1] * (k1 * v1)
        return total + w_fwd[i] * end

    def add_after(i, total):
        (c0, g0, _, _), (c1, g1, _, _) = first_rows(i)
        return total + w_bwd[i] * (state_in[i, 0:poles, :].astype(F32) + c0 * g0 + decay * (c1 * g1))

    before = lax.fori_loop(0, ctx, add_before, none)
    after = lax.fori_loop(ctx + 1, n_ctx, add_after, none)
    out_gain = res[...] * gain[...]
    part[0, :, 0, :] = res[...] * decay * before
    part[1, :, 0, :] = out_gain * decay * after

    (c0, g0, k0, v0), (c1, g1, k1, v1) = first_rows(ctx)
    keyp[0:1, :], valp[0:1, :], keyp[1:2, :], valp[1:2, :] = k0, v0, k1, v1
    mix0, mix1, gl0, gl1 = k0 * v0, k1 * v1, c0 * g0, c1 * g1
    taps0, taps1 = kern[0:1, :], kern[1:2, :]
    grad_mix[0:1, :] += taps0 * gl0 + taps1 * gl1
    grad_mix[1:2, :] += taps0 * gl1
    leaving = jnp.exp(-rates * float(rows)) * before + ends[0] + gained[0] * mix0 + gained[1] * mix1
    (c0, g0, k0, v0), (c1, g1, k1, v1) = first_rows(jnp.minimum(ctx + 1, n_ctx - 1))
    leaving = res[...] * decay * leaving
    out0 = jnp.sum(leaving, axis=0, keepdims=True) + taps0 * (k0 * v0)
    out1 = jnp.sum(leaving * decay, axis=0, keepdims=True) + taps1 * (k0 * v0) + taps0 * (k1 * v1)
    adj0 = jnp.sum(out_gain * after, axis=0, keepdims=True)
    adj1 = jnp.sum(out_gain * jnp.exp(rates) * (after - c0 * g0), axis=0, keepdims=True)
    for j, pair in enumerate(((c0 * out0, c1 * out1), (adj0 * v0, adj1 * v1), (adj0 * k0, adj1 * k1))):
        for r in range(2):
            gfp[j, rows + r : rows + r + 1, :] = jnp.where(ctx < n_ctx - 1, pair[r], 0.0)

    def add_fwd(p, acc):
        return acc + fwd_pow[p] * part[0, p, 0:1, :]

    def add_bwd(p, acc):
        return acc + rev_pow[p] * part[1, p, 0:1, :]

    whole = lax.fori_loop(0, poles, add_fwd, long_out[...] + kern[...] * mix0 + kern_late[...] * mix1)
    gfp[0, 0:rows, :] = cot[...].astype(F32) * whole
    whole = lax.fori_loop(0, poles, add_bwd, grad_mix[...])
    gfp[1, 0:rows, :] = whole * valp[...]
    gfp[2, 0:rows, :] = whole * keyp[...]
    for j in range(3):
        acc = taps[0, j : j + 1, :] * gfp[j, 0:rows, :]
        acc += taps[1, j : j + 1, :] * gfp[j, 1 : rows + 1, :]
        acc += taps[2, j : j + 1, :] * gfp[j, 2 : rows + 2, :]
        gp[j] = acc.astype(BF16)

    def partial_of(slot):
        start = pl.multiple_of(slot * chans, chans)
        total = jnp.zeros((rows, chans), F32)
        for j in range(3):
            total += lax.dot_general(
                gp[j], w[j, pl.ds(start, chans), :], (((1,), (1,)), ((), ())), preferred_element_type=F32
            )
        return total

    def r_copy(k, s, p):
        c, d = streams[k]
        there = at_z(col, z + d)
        if c == 1 and s == hops - 1:
            there = at_z(1 - col, z + d)
        if c == 1 and s == hops:
            there = partner
        at = (k, s, piece(p))
        return remote(rs_out.at[at], rs_in.at[at], r_send.at[k, s, p], r_recv.at[k, s, p], (ctx, there))

    far_pair = remote(far_out.at[0], far_in.at[0], r_send.at[4, 1, 0], r_recv.at[4, 1, 0], (ctx, partner))
    far_sum = remote(far_out.at[1], far_in.at[1], r_send.at[4, 2, 0], r_recv.at[4, 2, 0], (ctx, at_z(col, z + hops + 1)))

    swap = remote(x_out, x_in, r_send.at[4, 0, 0], r_recv.at[4, 0, 0], (ctx, partner))

    for group, s, distance in ((theirs, 1, hops), (mine, 1, hops), (theirs, hops, 1)):
        if s == hops:
            far_out[0] = partial_of(block_at(theirs[0], hops + 1)).astype(BF16)
            far_pair.start()
        for k in group:
            rs_out[k, s] = partial_of(block_at(k, distance)).astype(BF16)
        for i in range(PIECES):
            for k in group:
                r_copy(k, s, halves(k)[i]).start()
    x_out[...] = partial_of(partner).astype(BF16)
    swap.start()

    for s in range(2, hops):
        for k in range(4):
            ready[k] = partial_of(block_at(k, hops + 1 - s))
        for group in (theirs, mine):
            for i in range(PIECES):
                for k in group:
                    p = halves(k)[i]
                    at = piece(p)
                    total = ready[k, at]
                    r_copy(k, s - 1, p).wait_recv()
                    rs_out[k, s, at] = (total + rs_in[k, s - 1, at].astype(F32)).astype(BF16)
                    r_copy(k, s, p).start()

    total = partial_of(block_at(0, hops + 1))
    far_pair.wait_recv()
    far_out[1] = (total + far_in[0].astype(F32)).astype(BF16)
    far_sum.start()
    for k in mine:
        ready[k] = partial_of(block_at(k, 1))
    for i in range(PIECES):
        for k in mine:
            p = halves(k)[i]
            at = piece(p)
            total = ready[k, at]
            for other, step in ((k + 2, hops), (k, hops - 1), (k + 2, hops - 1)):
                r_copy(other, step, p).wait_recv()
                total += rs_in[other, step, at].astype(F32)
            rs_out[k, hops, at] = total.astype(BF16)
            r_copy(k, hops, p).start()

    long_out[...] = partial_of(tp)
    swap.wait_recv()
    long_out[...] += x_in[...].astype(F32)
    far_sum.wait_recv()
    long_out[...] += far_in[1].astype(F32)
    for p in range(PIECES):
        at = piece(p)
        total = long_out[at]
        for k in mine:
            r_copy(k, hops, p).wait_recv()
            total += rs_in[k, hops, at].astype(F32)
        out[at] = total.astype(BF16)

    swap.wait_send()
    x_pair.wait_send()
    far_pair.wait_send()
    far_sum.wait_send()
    for k in range(4):
        g_copy(k, hops + 1, halves(k)[0]).wait_send()
        for p in range(PIECES):
            for s in range(1, hops + 1):
                g_copy(k, s, p).wait_send()
                r_copy(k, s, p).wait_send()


def body(n_ctx, n_tp, inputs, w_in, conv_taps, pole_rates, residues, cotangent):
    rows, chans = inputs.shape
    width = w_in.shape[0]
    poles = pole_rates.shape[1]
    steps = n_tp // COLUMNS // 2 + 1
    vmem = pltpu.VMEM
    dma = pltpu.SemaphoreType.DMA
    scratch = [
        vmem((3, width, chans), BF16),
        vmem((n_tp, rows, chans), BF16),
        vmem((3, 3, chans), F32),
        vmem((poles, chans), F32),
        vmem((poles, chans), F32),
        vmem((rows, chans), BF16),
        vmem((3, rows + SUB, chans), F32),
        vmem((rows, chans), F32),
        vmem((rows, chans), F32),
        vmem((rows, chans), F32),
        vmem((rows + SUB, chans), F32),
        vmem((rows + SUB, chans), F32),
        vmem((poles, rows, chans), F32),
        vmem((poles, rows, chans), F32),
        vmem((rows, chans), F32),
        vmem((rows, chans), F32),
        vmem((rows, SUB, chans), F32),
        vmem((poles, chans), F32),
        vmem((n_ctx, poles, chans), F32),
        vmem((n_ctx, poles, chans), F32),
        vmem((2, poles, SUB, chans), F32),
        vmem((2, poles, chans), F32),
        vmem((2, poles + 2 * SUB, chans), BF16),
        vmem((n_ctx, poles + 2 * SUB, chans), BF16),
        vmem((3, rows + SUB, chans), F32),
        vmem((2, SUB, rows, chans), F32),
        vmem((rows, chans), F32),
        vmem((rows, chans), F32),
        vmem((3, rows, chans), BF16),
        vmem((4, rows, chans), F32),
        vmem((4, steps - 1, rows, chans), BF16),
        vmem((4, steps - 1, rows, chans), BF16),
        vmem((rows, chans), BF16),
        vmem((rows, chans), BF16),
        vmem((2, rows, chans), BF16),
        vmem((2, rows, chans), BF16),
        dma((5,)),
        dma((3,)),
        dma((5, steps, PIECES)),
        dma((5, steps, PIECES)),
        dma((n_ctx,)),
        dma((n_ctx,)),
        pltpu.SemaphoreType.REGULAR((n_ctx.bit_length(),)),
        dma((5, steps - 1, PIECES)),
        dma((5, steps - 1, PIECES)),
    ]
    return pl.pallas_call(
        functools.partial(kernel, n_ctx, n_tp),
        out_shape=pltpu.VMEM((rows, chans), BF16),
        in_specs=[pl.BlockSpec(memory_space=pl.ANY)] * 6,
        out_specs=pl.BlockSpec(memory_space=pltpu.VMEM),
        scratch_shapes=scratch,
        compiler_params=pltpu.CompilerParams(
            collective_id=0, has_side_effects=True, vmem_limit_bytes=60 * 1024 * 1024
        ),
        cost_estimate=pl.CostEstimate(
            flops=4 * rows * width * 3 * chans, bytes_accessed=2 * 3 * width * chans, transcendentals=0
        ),
        name="hyena_input_grad",
    )(inputs, w_in.transpose(1, 0, 2), conv_taps, pole_rates.T, residues.T, cotangent)


def solution(mesh):
    in_specs = (
        P("ctx", "tp"),
        P(None, None, "tp"),
        P(None, None, "tp"),
        P("tp", None),
        P("tp", None),
        P("ctx", "tp"),
    )
    out_specs = P("ctx", "tp")
    step = functools.partial(body, mesh.shape["ctx"], mesh.shape["tp"])
    return jax.shard_map(step, mesh=mesh, in_specs=in_specs, out_specs=out_specs, check_vma=False)
```
